32 devices in a mesh: tm: 8 (over y, x, core), batch: 4 (over z).
Axes of the slice: x: 2, y: 2, z: 4, core: 2. Of those that a mesh axis runs over, the one named last changes fastest.
Arguments:
- signal: bfloat16 [4, 1024, 4096], P('batch', 'tm'), may hold values from -7.5 to 7.5
- gate_input: bfloat16 [4, 1024, 4096], P('batch', 'tm'), may hold values from -6 to 6
- bc_forward: bfloat16 [4, 1024, 128], P('batch', 'tm'), may hold values from -6 to 6
- bc_backward: bfloat16 [4, 1024, 128], P('batch', 'tm'), may hold values from -6 to 6
- step_raw: bfloat16 [4, 1024, 128], P('batch', 'tm'), may hold values from -12 to 2
- decay_rate: float32 [2, 64], replicated, may hold values from 0.3 to 1
- conv_weight: float32 [2, 4, 4224], replicated, may hold values from -3 to 3
- conv_bias: float32 [2, 4224], replicated, may hold values from -1.5 to 1.5
- skip_gain: float32 [2, 64], replicated, may hold values from 0.5 to 1.5
- norm_gain: float32 [4096], replicated, may hold values from 0.1 to 1.9
Outputs:
- mixed: bfloat16 [4, 1024, 4096], P(None, 'batch', 'tm')
The draws below stay inside these ranges and needn't reach their ends.
All inputs are finite; a program needn't handle non-finite values.
Results may differ from the reference program's by a relative error of at most 0.0075.
Values may be sent and summed in bfloat16 or wider, within the bound.
A program may use at most 256 MiB of HBM per device.

```python
import math
import jax
import jax.numpy as jnp
from jax import lax

INNER = 4096
HEADDIM = 64
STATE = 64
CONV = 4
GROUP = 128
T_DEV = 128
HEADS = 64
CAPTURE_DURATION = 1024
TRACE_COUNT = 4


def head_classes(key):
    picks = jax.random.uniform(jax.random.fold_in(key, 101), (2, HEADS))
    slow_cut = 0.4
    middle_cut = 0.75
    slow_mask = picks < slow_cut
    middle_mask = (picks >= slow_cut) & (picks < middle_cut)
    return (slow_mask, middle_mask)


def draw_decay_rate(key, part):
    slow_mask, middle_mask = head_classes(key)
    slow_rate = jax.random.uniform(jax.random.fold_in(key, 1), (2, HEADS), jnp.float32, 0.3, 0.6)
    middle_rate = jax.random.uniform(jax.random.fold_in(key, 6), (2, HEADS), jnp.float32, 0.5, 0.7)
    fast_rate = jax.random.uniform(jax.random.fold_in(key, 2), (2, HEADS), jnp.float32, 0.6, 1.0)
    return jnp.where(slow_mask, slow_rate, jnp.where(middle_mask, middle_rate, fast_rate)).astype(jnp.float32)


def draw_step_raw(key, part):
    slow_mask, middle_mask = head_classes(key)
    slow_slots = jnp.concatenate([slow_mask[0], slow_mask[1]])
    middle_slots = jnp.concatenate([middle_mask[0], middle_mask[1]])
    blocks = CAPTURE_DURATION // T_DEV
    noise_jitter = jax.random.uniform(jax.random.fold_in(key, 3), (TRACE_COUNT, CAPTURE_DURATION, 2 * HEADS), jnp.float32, -0.7, 0.7)
    displacement_sizes = jax.random.uniform(jax.random.fold_in(key, 4), (TRACE_COUNT, blocks, 1, 2 * HEADS), jnp.float32, -0.5, 0.5)
    displacement_sizes = jnp.broadcast_to(displacement_sizes, (TRACE_COUNT, blocks, T_DEV, 2 * HEADS)).reshape(TRACE_COUNT, CAPTURE_DURATION, 2 * HEADS)
    resting_floor = jnp.where(slow_slots, math.log(2.0 / CAPTURE_DURATION), jnp.where(middle_slots, math.log(1.1 / T_DEV), math.log(1.6 / T_DEV)))
    spike_moments = jax.random.randint(jax.random.fold_in(key, 5), (TRACE_COUNT, 3), 0, CAPTURE_DURATION)
    spike_trace_picks = jnp.any(jnp.arange(CAPTURE_DURATION)[None, :, None] == spike_moments[:, None, :], axis=-1)
    spike_height = jnp.where(spike_trace_picks[:, :, None] & slow_slots[None, None, :], math.log(0.25 * CAPTURE_DURATION), 0.0)
    combined_waveform = resting_floor[None, None, :] + noise_jitter + displacement_sizes + spike_height
    return combined_waveform.astype(jnp.float32).astype(jnp.bfloat16)


def draw_signal(key, part):
    blocks = CAPTURE_DURATION // T_DEV
    noise_values = jnp.clip(jax.random.normal(jax.random.fold_in(key, 11), (TRACE_COUNT, blocks, T_DEV, INNER), jnp.float32), -6.0, 6.0)
    shard_levels = jnp.exp(jax.random.uniform(jax.random.fold_in(key, 12), (TRACE_COUNT, blocks, 1, 1), jnp.float32, -3.0, 0.2))
    leveled = (noise_values * shard_levels).reshape(TRACE_COUNT, CAPTURE_DURATION, INNER)
    return leveled.astype(jnp.float32).astype(jnp.bfloat16)


def steps_of(key, extent, cuts, smallest, largest):
    gain, own = 1.0, jax.random.fold_in(key, 6)
    for position, blocks in cuts:
        draws = jnp.exp(jax.random.uniform(jax.random.fold_in(own, position), (blocks,), jnp.float32, smallest / len(cuts), largest / len(cuts)))
        gain = gain * jnp.repeat(draws, extent[position] // blocks).reshape([-1 if axis == position else 1 for axis in range(len(extent))])
    return gain


def centred(stream_key, dims, scale, bound, cuts=(), dtype=jnp.bfloat16):
    entries = scale * jax.random.normal(stream_key, dims, jnp.float32)
    if cuts:
        entries = entries * steps_of(stream_key, dims, cuts, -0.22, 0.18)
    return jnp.clip(entries, -bound, bound).astype(dtype)


def setup_inputs(seed: int = 0) -> dict:
    key_list = jax.random.split(jax.random.key(seed), 11)
    return {
        "signal": draw_signal(jax.random.fold_in(key_list[10], 71), 0),
        "gate_input": centred(key_list[1], (TRACE_COUNT, CAPTURE_DURATION, INNER), 1.0, 6.0, ((0, 4), (1, 8))),
        "bc_forward": centred(key_list[2], (TRACE_COUNT, CAPTURE_DURATION, 2 * STATE), 1.0, 6.0, ((0, 4), (1, 8))),
        "bc_backward": centred(key_list[3], (TRACE_COUNT, CAPTURE_DURATION, 2 * STATE), 1.0, 6.0, ((0, 4), (1, 8))),
        "step_raw": draw_step_raw(jax.random.fold_in(key_list[10], 71), 0),
        "decay_rate": draw_decay_rate(jax.random.fold_in(key_list[10], 71), 0),
        "conv_weight": centred(key_list[6], (2, CONV, INNER + 2 * STATE), CONV ** -0.5, 3.0, (), jnp.float32),
        "conv_bias": centred(key_list[7], (2, INNER + 2 * STATE), 0.25, 1.5, (), jnp.float32),
        "skip_gain": jnp.clip(jax.random.uniform(key_list[8], (2, HEADS), jnp.float32, 0.5, 1.5), 0.5, 1.5),
        "norm_gain": jnp.clip(1.0 + 0.18 * jax.random.normal(key_list[9], (INNER,), jnp.float32), 0.1, 1.9),
    }


EPSILON = 1e-05

def conv_silu(sequence, history, weights, offsets):
    length = sequence.shape[0]
    padded = jnp.concatenate([history, sequence], 0).astype(jnp.float32)
    combined_waveform = jnp.broadcast_to(offsets[None, :], (length, sequence.shape[1]))
    for offset in range(weights.shape[0]):
        combined_waveform = combined_waveform + weights[offset][None, :] * padded[offset:offset + length]
    return jax.nn.silu(combined_waveform).astype(jnp.bfloat16)

def block_parts(x_part, b_part, step_size, rate_head):
    log_decay = -step_size * rate_head[None, None, :]
    cum_log = jnp.cumsum(log_decay, axis=1)
    weight_end = jnp.exp(cum_log[:, -1:, :] - cum_log) * step_size
    b_scaled = (b_part.astype(jnp.float32)[:, :, None, :] * weight_end[..., None]).astype(jnp.bfloat16)
    states = jnp.einsum('mqhn,mqhp->mhnp', b_scaled.astype(jnp.float32), x_part.astype(jnp.float32))
    return (cum_log, states, jnp.exp(cum_log[:, -1, :]))

def prepare(x_conv, bc_conv, step_raw, rate_head):
    block_count = x_conv.shape[0] // GROUP
    x_part = x_conv.reshape(block_count, GROUP, -1, HEADDIM)
    b_part = bc_conv[:, :STATE].reshape(block_count, GROUP, STATE)
    c_part = bc_conv[:, STATE:].reshape(block_count, GROUP, STATE)
    step_size = jax.nn.softplus(step_raw.astype(jnp.float32)).reshape(block_count, GROUP, -1)
    cum_log, states, decays = block_parts(x_part, b_part, step_size, rate_head)
    return (x_part, b_part, c_part, step_size, cum_log, states, decays)

def block_outputs(parts, start, skip_head):
    block_len = parts[0].shape[1]
    causal_mask = jnp.arange(block_len)[:, None] >= jnp.arange(block_len)[None, :]

    def advance(state_in, pieces):
        x_block, b_block, c_block, step_block, cum_block, state_block, decay_block = pieces
        scores = jnp.dot(c_block, b_block.T, preferred_element_type=jnp.float32)
        differ = cum_block.T[:, :, None] - cum_block.T[:, None, :]
        masked = jnp.where(causal_mask[None], jnp.exp(jnp.minimum(differ, 0.0)), 0.0)
        mixing = (masked * scores[None] * step_block.T[:, None, :]).astype(jnp.bfloat16)
        local_out = jnp.einsum('hij,jhp->ihp', mixing.astype(jnp.float32), x_block.astype(jnp.float32))
        carried = jnp.einsum('in,hnp->ihp', c_block.astype(jnp.float32), state_in, precision=lax.Precision.HIGHEST)
        result = local_out + jnp.exp(cum_block)[:, :, None] * carried + skip_head[None, :, None] * x_block.astype(jnp.float32)
        new_state = decay_block[:, None, None] * state_in + state_block
        return (new_state, result.astype(jnp.bfloat16))
    _, outputs = lax.scan(advance, start, parts)
    return outputs.reshape(outputs.shape[0] * outputs.shape[1], -1)

def run_direction(signal_seq, bc_seq, step_seq, conv_w, conv_b, rate_head, skip_head):
    rim_rows = conv_w.shape[0] - 1
    x_conv = conv_silu(signal_seq, jnp.zeros((rim_rows, INNER), jnp.bfloat16), conv_w[:, :INNER], conv_b[:INNER])
    bc_conv = conv_silu(bc_seq, jnp.zeros((rim_rows, 2 * STATE), jnp.bfloat16), conv_w[:, INNER:], conv_b[INNER:])
    parts = prepare(x_conv, bc_conv, step_seq, rate_head)
    start = jnp.zeros((HEADS, STATE, HEADDIM), jnp.float32)
    return block_outputs(parts, start, skip_head)

def reference(signal, gate_input, bc_forward, bc_backward, step_raw, decay_rate, conv_weight, conv_bias, skip_gain, norm_gain):

    def one_record(record_args):
        signal_rec, gate_rec, bcf_rec, bcb_rec, step_rec = record_args
        forward_out = run_direction(signal_rec, bcf_rec, step_rec[:, :HEADS], conv_weight[0], conv_bias[0], decay_rate[0], skip_gain[0])
        backward_out = run_direction(signal_rec[::-1], bcb_rec[::-1], step_rec[::-1, HEADS:], conv_weight[1], conv_bias[1], decay_rate[1], skip_gain[1])[::-1]
        gated = (forward_out.astype(jnp.float32) + backward_out.astype(jnp.float32)) * jax.nn.silu(gate_rec.astype(jnp.float32))
        inv_rms = lax.rsqrt(lax.optimization_barrier(jnp.mean(gated * gated, axis=-1, keepdims=True)) + EPSILON)
        return (gated * inv_rms * norm_gain[None, :]).astype(jnp.bfloat16)
    return lax.map(one_record, (signal, gate_input, bc_forward, bc_backward, step_raw))
```

```python
import functools

import jax
import jax.numpy as jnp
from jax import lax
from jax.experimental import pallas as pl
from jax.experimental.pallas import tpu as pltpu
from jax.sharding import PartitionSpec as P

INNER = 4096
HEADDIM = 64
STATE = 64
HEADS = 64
ROWS = 128
RIM = 16
EPSILON = 1e-05
LOG2E = 1.4426950408889634
MASKED = -1e30

F32 = jnp.float32
BF16 = jnp.bfloat16


def dot(a, b, **kwargs):
    return jnp.dot(a, b, preferred_element_type=F32, **kwargs)


def split_bf16(value):
    high = value.astype(BF16)
    low = (value - high.astype(F32)).astype(BF16)
    return jnp.concatenate([high, low], axis=1)


def half_silu(half):
    return half + half * jnp.tanh(half)


def mixer_kernel(
    tm_count,
    batch_count,
    sig_ref,
    gate_ref,
    bcf_ref,
    bcb_ref,
    step_ref,
    rate_ref,
    cw_ref,
    cb_ref,
    skip_ref,
    gain_ref,
    out_ref,
    hl_sig,
    hr_sig,
    hl_bc,
    hr_bc,
    tot_buf,
    ext,
    ext_bc,
    xs,
    rt,
    roll_a,
    we_f,
    we_dw,
    keep,
    snd,
    pin,
    csnd,
    crecv,
    esnd,
    ein,
    eown,
    yloc,
    outs,
    landing,
    inv_snd,
    inv_buf,
    halo_ssem,
    halo_rsem,
    tot_ssem,
    tot_rsem,
    pin_ssem,
    pin_rsem,
    chip_ssem,
    chip_rsem,
    ein_ssem,
    ein_rsem,
    out_ssem,
    out_rsem,
    inv_ssem,
    inv_rsem,
):
    T = tm_count
    M = T // 2
    CW = INNER // T
    HG = CW // HEADDIM
    per = T // batch_count
    me = lax.axis_index("tm")
    rec = lax.axis_index("batch")
    core = lax.rem(me, 2)
    chip = me // 2
    forward = core == 1
    partner = me + 1 - 2 * core
    dest = me // per
    place = jnp.where(forward, chip, M - 1 - chip)

    def at(tm, batch=None):
        return {"tm": tm, "batch": rec if batch is None else batch}

    barrier = pltpu.get_barrier_semaphore()

    def greet(tm, batch):
        pl.semaphore_signal(
            barrier, inc=1, device_id={"tm": tm, "batch": batch},
            device_id_type=pl.DeviceIdType.MESH,
        )

    own_dest = dest == rec
    for j in range(T):

        @pl.when(j != me)
        def _():
            greet(j, rec)

        @pl.when(jnp.logical_or(j != me, jnp.logical_not(own_dest)))
        def _():
            greet(j, dest)

    for b in range(batch_count):
        for q in range(per):

            @pl.when(jnp.logical_or(b != rec, rec * per + q != me))
            def _():
                greet(rec * per + q, b)

    pl.semaphore_wait(barrier, (T - 1) + 2 * (T - jnp.where(own_dest, 1, 0)))

    def remote(src, dst, ssem, rsem, device):
        return pltpu.make_async_remote_copy(
            src_ref=src, dst_ref=dst, send_sem=ssem, recv_sem=rsem,
            device_id=device, device_id_type=pl.DeviceIdType.MESH,
        )

    to_right = [
        remote(sig_ref.at[pl.ds(ROWS - RIM, RIM)], hl_sig, halo_ssem.at[0], halo_rsem.at[0], at(me + 1)),
        remote(bcf_ref.at[pl.ds(ROWS - RIM, RIM)], hl_bc, halo_ssem.at[1], halo_rsem.at[1], at(me + 1)),
    ]
    to_left = [
        remote(sig_ref.at[pl.ds(0, RIM)], hr_sig, halo_ssem.at[2], halo_rsem.at[2], at(me - 1)),
        remote(bcb_ref.at[pl.ds(0, RIM)], hr_bc, halo_ssem.at[3], halo_rsem.at[3], at(me - 1)),
    ]

    @pl.when(me < T - 1)
    def _():
        for copy in to_right[::-1]:
            copy.start()

    @pl.when(me > 0)
    def _():
        for copy in to_left[::-1]:
            copy.start()

    raw = step_ref[...].astype(F32)
    step = jnp.maximum(raw, 0.0) + jnp.log1p(jnp.exp(-jnp.abs(raw)))
    rate = jnp.concatenate([rate_ref[0:1, :], rate_ref[1:2, :]], axis=1)
    log_decay = -step * rate
    row = lax.broadcasted_iota(jnp.int32, (ROWS, ROWS), 0)
    col = lax.broadcasted_iota(jnp.int32, (ROWS, ROWS), 1)
    lower = row >= col
    upper = row <= col
    fwd_lane = col < HEADS
    high = lax.Precision.HIGHEST
    cum = jnp.where(
        fwd_lane,
        dot(lower.astype(F32), log_decay, precision=high),
        dot(upper.astype(F32), log_decay, precision=high),
    )
    total = jnp.where(fwd_lane[0:1], cum[ROWS - 1 : ROWS], cum[0:1])
    tot_buf[me] = jnp.broadcast_to(total, (8, ROWS))

    def tot_copy(j):
        return remote(tot_buf.at[me], tot_buf.at[me], tot_ssem.at[j], tot_rsem.at[me], at(j))

    for j in range(T):

        @pl.when(j != me)
        def _():
            tot_copy(j).start()

    we_f[0:ROWS] = split_bf16(jnp.exp(total - cum) * step)
    we_f[ROWS : 2 * ROWS] = split_bf16(jnp.exp(cum))
    rt[...] = (LOG2E * (jnp.log(step) - cum)).T
    scaled_cum = LOG2E * cum
    roll_a[...] = scaled_cum
    skip = jnp.concatenate([skip_ref[0:1, :], skip_ref[1:2, :]], axis=1)
    skip_split = split_bf16(jnp.broadcast_to(skip, (16, 2 * HEADS)))
    own_dir = (lax.broadcasted_iota(jnp.int32, (1, 2 * HEADS), 1) < HEADS) == forward

    def spread(g, first):
        k = lax.broadcasted_iota(jnp.int32, (4 * HEADS, CW), 0)
        c = lax.broadcasted_iota(jnp.int32, (4 * HEADS, CW), 1)
        head = first + g * HG + c // HEADDIM
        return (lax.rem(k, 2 * HEADS) == head).astype(F32).astype(BF16)

    @pl.when(me == 0)
    def _():
        hl_sig[...] = jnp.zeros_like(hl_sig)
        hl_bc[...] = jnp.zeros_like(hl_bc)

    @pl.when(me == T - 1)
    def _():
        hr_sig[...] = jnp.zeros_like(hr_sig)
        hr_bc[...] = jnp.zeros_like(hr_bc)

    @pl.when(me > 0)
    def _():
        for copy in to_right:
            copy.wait_recv()

    @pl.when(me < T - 1)
    def _():
        for copy in to_left:
            copy.wait_recv()

    def conv(buf, direction, cols):
        half = 0.5 * cb_ref[direction : direction + 1, cols]
        for k in range(4):
            start = 5 + k if direction == 0 else 11 - k
            tap = 0.5 * cw_ref[direction, k : k + 1, cols]
            half = half + tap * buf[start : start + ROWS, :]
        return half_silu(half).astype(BF16)

    bc_cols = slice(INNER, INNER + 2 * STATE)
    ext_bc[0:8] = hl_bc[...].astype(F32)[8:16]
    ext_bc[8 : 8 + ROWS] = bcf_ref[...].astype(F32)
    bc_f = conv(ext_bc, 0, bc_cols)
    ext_bc[8 : 8 + ROWS] = bcb_ref[...].astype(F32)
    ext_bc[8 + ROWS : 16 + ROWS] = hr_bc[...].astype(F32)[0:8]
    bc_b = conv(ext_bc, 1, bc_cols)
    bt_f = bc_f.astype(F32).T[:STATE].astype(BF16)
    bt_b = bc_b.astype(F32).T[:STATE].astype(BF16)
    c_f = bc_f[:, STATE:]
    c_b = bc_b[:, STATE:]
    scores_f = dot(c_f, bt_f)
    scores_b = dot(c_b, bt_b)
    bias_f = jnp.where(lower, 0.0, MASKED)
    bias_b = jnp.where(upper, 0.0, MASKED)

    def cols_of(g):
        return pl.ds(pl.multiple_of(g * CW, CW), CW)

    def pin_copy(g):
        return remote(snd.at[g], pin.at[g], pin_ssem.at[g], pin_rsem.at[g], at(partner))

    def chip_copy(g, target):
        tm = jnp.where(forward, 2 * target + 1, 2 * (M - 1 - target))
        return remote(
            csnd.at[g], crecv.at[place, g], chip_ssem.at[target, g], chip_rsem.at[place, g], at(tm)
        )

    def recv_chip(g, source):
        return remote(
            csnd.at[g], crecv.at[source, g], chip_ssem.at[source, g], chip_rsem.at[source, g], at(partner)
        )

    own_first = jnp.where(forward, 0, HEADS)

    def combine(g):
        pin_copy(g).wait_recv()
        factor = jnp.where(
            forward,
            dot(we_f[2 * ROWS - 16 :], spread(g, 0))[15:16],
            dot(we_f[ROWS : ROWS + 16], spread(g, HEADS))[0:1],
        )
        csnd[g] = (pin[g].astype(F32) * factor + keep[g]).astype(BF16)
        for target in range(1, M):

            @pl.when(place < target)
            def _():
                chip_copy(g, target).start()

    def first(g, _):
        cols = cols_of(g)
        ext[0:8] = hl_sig[:, cols].astype(F32)[8:16]
        ext[8 : 8 + ROWS] = sig_ref[:, cols].astype(F32)
        ext[8 + ROWS : 16 + ROWS] = hr_sig[:, cols].astype(F32)[0:8]
        x_f = conv(ext, 0, cols)
        x_b = conv(ext, 1, cols)
        xs[0:ROWS, cols] = x_f
        xs[ROWS : 2 * ROWS, cols] = x_b
        w_f = dot(we_f[0:ROWS], spread(g, 0))
        w_b = dot(we_f[0:ROWS], spread(g, HEADS))
        state_f = dot(bt_f, (x_f.astype(F32) * w_f).astype(BF16))
        state_b = dot(bt_b, (x_b.astype(F32) * w_b).astype(BF16))
        snd[g] = jnp.where(forward, state_b, state_f).astype(BF16)
        keep[g] = jnp.where(forward, state_f, state_b)
        pin_copy(g).start()

        @pl.when(g > 0)
        def _():
            combine(g - 1)

        return 0

    lax.fori_loop(0, T, first, 0)
    combine(T - 1)

    lane = lax.broadcasted_iota(jnp.int32, (ROWS, 2 * HEADDIM), 1)

    def local(g, _):
        rolled = pltpu.roll(roll_a[...], lax.rem(2 * HEADS - g * HG, 2 * HEADS), 1)
        skips_f = dot(skip_split, spread(g, 0))[0:1]
        skips_b = dot(skip_split, spread(g, HEADS))[0:1]

        def mixing(h):
            a_f = rolled[:, h : h + 1]
            a_b = rolled[:, HEADS + h : HEADS + h + 1]
            r_f = rt[pl.ds(g * HG + h, 1), :]
            r_b = rt[pl.ds(HEADS + g * HG + h, 1), :]
            mix_f = (scores_f * jnp.exp2((a_f + r_f) + bias_f)).astype(BF16)
            mix_b = (scores_b * jnp.exp2((a_b + r_b) + bias_b)).astype(BF16)
            return jnp.concatenate([mix_f, mix_b], axis=1)

        for pair in range(HG // 2):
            width = 2 * HEADDIM
            cols = pl.ds(pl.multiple_of(g * CW + pair * width, width), width)
            x_pair = xs[:, cols]
            stacked = jnp.concatenate([mixing(2 * pair), mixing(2 * pair + 1)], axis=0)
            both = dot(stacked, x_pair)
            out = jnp.where(lane < HEADDIM, both[:ROWS], both[ROWS:])
            inside = slice(pair * width, (pair + 1) * width)
            out = out + skips_f[:, inside] * x_pair[:ROWS].astype(F32)
            out = out + skips_b[:, inside] * x_pair[ROWS:].astype(F32)
            yloc[:, cols] = out
        return 0

    lax.fori_loop(0, T, local, 0)

    for j in range(T):

        @pl.when(j != me)
        def _():
            remote(tot_buf.at[j], tot_buf.at[j], tot_ssem.at[j], tot_rsem.at[j], at(partner)).wait_recv()

    rows = [tot_buf[partner][0:1]]
    chips = [tot_buf[2 * q][0:1] + tot_buf[2 * q + 1][0:1] for q in range(M)]
    for source in range(M - 1):
        sum_f = jnp.zeros((1, 2 * HEADS), F32)
        sum_b = jnp.zeros((1, 2 * HEADS), F32)
        for q in range(source + 1, M):
            sum_f = sum_f + jnp.where(q < place, chips[q], 0.0)
            sum_b = sum_b + jnp.where(q < place, chips[M - 1 - q], 0.0)
        rows.append(jnp.where(forward, sum_f, sum_b))
    padding = -len(rows) % 16
    rows = jnp.exp(jnp.concatenate(rows + [jnp.zeros((padding, 2 * HEADS), F32)], axis=0))
    we_dw[...] = split_bf16(jnp.where(own_dir, rows, 0.0))

    def ein_copy(g):
        return remote(esnd.at[g], ein.at[g], ein_ssem.at[g], ein_rsem.at[g], at(partner))

    def enter(s, _):
        g = lax.rem(me + s, T)
        factors = dot(we_dw[...], spread(g, own_first))
        esnd[g] = jnp.zeros((STATE, CW), BF16)
        entering = keep.at[g]
        entering[...] = jnp.zeros((STATE, CW), F32)
        for source in range(M - 1):

            @pl.when(source < place)
            def _():
                recv_chip(g, source).wait_recv()
                entering[...] += factors[source + 1 : source + 2] * crecv[source, g].astype(F32)

        value = entering[...]
        esnd[g] = value.astype(BF16)
        ein_copy(g).start()
        eown[g] = (value * factors[0:1] + pin[g].astype(F32)).astype(BF16)
        return 0

    lax.fori_loop(0, T, enter, 0)

    slot = lax.rem(me, per)

    def out_copy(g):
        return remote(
            outs.at[g], landing.at[rec * per + slot], out_ssem.at[g], out_rsem.at[rec * per + slot],
            at(g, dest),
        )

    def last(s, squares):
        g = lax.rem(partner + s, T)
        cols = cols_of(g)
        ein_copy(g).wait_recv()
        own, other = eown[g], ein[g]
        enter_f = jnp.where(forward, own, other)
        enter_b = jnp.where(forward, other, own)
        decay_f = dot(we_f[ROWS : 2 * ROWS], spread(g, 0))
        decay_b = dot(we_f[ROWS : 2 * ROWS], spread(g, HEADS))
        y = yloc[:, cols] + decay_f * dot(c_f, enter_f) + decay_b * dot(c_b, enter_b)
        gated = y * half_silu(0.5 * gate_ref[:, cols].astype(F32))
        for part in range(CW // 128):
            piece = gated[:, part * 128 : (part + 1) * 128]
            squares = squares + piece * piece
        outs[g] = gated.astype(BF16)
        mine = jnp.logical_and(own_dest, g == me)

        @pl.when(mine)
        def _():
            landing[rec * per + slot] = outs[g]

        @pl.when(jnp.logical_not(mine))
        def _():
            out_copy(g).start()

        return squares

    squares = lax.fori_loop(0, T, last, jnp.zeros((ROWS, 128), F32))
    mean = jnp.sum(squares.T, axis=0, keepdims=True) * (1.0 / INNER)
    inv_snd[...] = jnp.broadcast_to(lax.rsqrt(mean + EPSILON), (8, ROWS))

    def inv_copy(j):
        return remote(
            inv_snd, inv_buf.at[rec * per + slot], inv_ssem.at[j], inv_rsem.at[rec * per + slot],
            at(j, dest),
        )

    for j in range(T):
        mine = jnp.logical_and(own_dest, j == me)

        @pl.when(mine)
        def _():
            inv_buf[rec * per + slot] = inv_snd[...]

        @pl.when(jnp.logical_not(mine))
        def _():
            inv_copy(j).start()

    gain = gain_ref[:, cols_of(me)]

    for b in range(batch_count):
        for q in range(per):
            n = b * per + q
            mine = jnp.logical_and(b == rec, rec * per + q == me)

            @pl.when(jnp.logical_not(mine))
            def _():
                remote(outs.at[0], landing.at[n], out_ssem.at[0], out_rsem.at[n], at(partner)).wait_recv()
                remote(inv_snd, inv_buf.at[n], inv_ssem.at[0], inv_rsem.at[n], at(partner)).wait_recv()

            scale = jnp.broadcast_to(inv_buf[n][0:1], (ROWS, ROWS)).T
            for part in range(CW // 128):
                inside = slice(part * 128, (part + 1) * 128)
                piece = landing[n, :, inside].astype(F32) * scale * gain[:, inside]
                out_ref[b, q * ROWS : (q + 1) * ROWS, inside] = piece.astype(BF16)

    @pl.when(me < T - 1)
    def _():
        for copy in to_right:
            copy.wait_send()

    @pl.when(me > 0)
    def _():
        for copy in to_left:
            copy.wait_send()

    for j in range(T):

        @pl.when(j != me)
        def _():
            tot_copy(j).wait_send()

        @pl.when(jnp.logical_not(jnp.logical_and(own_dest, j == me)))
        def _():
            inv_copy(j).wait_send()
            out_copy(j).wait_send()

    def sent(g, _):
        pin_copy(g).wait_send()
        ein_copy(g).wait_send()
        for target in range(1, M):

            @pl.when(place < target)
            def _():
                chip_copy(g, target).wait_send()

        return 0

    lax.fori_loop(0, T, sent, 0)


def shards(tm_count, batch_count, signal, gate_input, bc_forward, bc_backward, step_raw,
           decay_rate, conv_weight, conv_bias, skip_gain, norm_gain):
    T, M = tm_count, tm_count // 2
    CW = INNER // T
    per = T // batch_count
    vmem = pltpu.VMEM
    dma = pltpu.SemaphoreType.DMA
    scratch = [
        vmem((RIM, INNER), BF16),
        vmem((RIM, INNER), BF16),
        vmem((RIM, 2 * STATE), BF16),
        vmem((RIM, 2 * STATE), BF16),
        vmem((T, 8, ROWS), F32),
        vmem((ROWS + 16, CW), F32),
        vmem((ROWS + 16, 2 * STATE), F32),
        vmem((2 * ROWS, INNER), BF16),
        vmem((2 * HEADS, ROWS), F32),
        vmem((ROWS, 2 * HEADS), F32),
        vmem((2 * ROWS, 4 * HEADS), BF16),
        vmem((-(-M // 16) * 16, 4 * HEADS), BF16),
        vmem((T, STATE, CW), F32),
        vmem((T, STATE, CW), BF16),
        vmem((T, STATE, CW), BF16),
        vmem((T, STATE, CW), BF16),
        vmem((M, T, STATE, CW), BF16),
        vmem((T, STATE, CW), BF16),
        vmem((T, STATE, CW), BF16),
        vmem((T, STATE, CW), BF16),
        vmem((ROWS, INNER), F32),
        vmem((T, ROWS, CW), BF16),
        vmem((T, ROWS, CW), BF16),
        vmem((8, ROWS), F32),
        vmem((T, 8, ROWS), F32),
        dma((4,)),
        dma((4,)),
        dma((T,)),
        dma((T,)),
        dma((T,)),
        dma((T,)),
        dma((M, T)),
        dma((M, T)),
        dma((T,)),
        dma((T,)),
        dma((T,)),
        dma((T,)),
        dma((T,)),
        dma((T,)),
    ]
    return pl.pallas_call(
        functools.partial(mixer_kernel, T, batch_count),
        out_shape=jax.ShapeDtypeStruct((batch_count, per * ROWS, CW), BF16),
        in_specs=[pl.BlockSpec(memory_space=pltpu.VMEM)] * 10,
        out_specs=pl.BlockSpec(memory_space=pltpu.VMEM),
        scratch_shapes=scratch,
        compiler_params=pltpu.CompilerParams(
            collective_id=0, has_side_effects=True, vmem_limit_bytes=48 * 2**20
        ),
        cost_estimate=pl.CostEstimate(
            flops=10**9, bytes_accessed=8 * 2**20, transcendentals=4 * 10**6
        ),
    )(signal[0], gate_input[0], bc_forward[0], bc_backward[0], step_raw[0],
      decay_rate, conv_weight, conv_bias, skip_gain, norm_gain.reshape(1, INNER))


def solution(mesh):
    in_specs = (P("batch", "tm", None),) * 5 + (P(),) * 5
    return jax.shard_map(
        functools.partial(shards, mesh.shape["tm"], mesh.shape["batch"]),
        mesh=mesh, in_specs=in_specs, out_specs=P(None, "batch", "tm"), check_vma=False,
    )
```

```python
import functools

import jax
import jax.numpy as jnp
from jax import lax
from jax.experimental import pallas as pl
from jax.experimental.pallas import tpu as pltpu
from jax.sharding import PartitionSpec as P

INNER = 4096
HEADDIM = 64
STATE = 64
HEADS = 64
ROWS = 128
LAG = 2
RIM = 16
EPSILON = 1e-05
LOG2E = 1.4426950408889634
MASKED = -1e30

F32 = jnp.float32
BF16 = jnp.bfloat16


def dot(a, b, **kwargs):
    return jnp.dot(a, b, preferred_element_type=F32, **kwargs)


def split_bf16(value):
    high = value.astype(BF16)
    low = (value - high.astype(F32)).astype(BF16)
    return jnp.concatenate([high, low], axis=1)


def half_silu(half):
    return half + half * jnp.tanh(half)


def mixer_kernel(
    tm_count,
    batch_count,
    sig_hbm,
    gate_hbm,
    bcf_hbm,
    bcb_hbm,
    step_hbm,
    rate_hbm,
    cw_hbm,
    cb_hbm,
    skip_hbm,
    gain_hbm,
    out_ref,
    sig_ref,
    gate_ref,
    bcf_ref,
    bcb_ref,
    step_ref,
    rate_ref,
    cw_ref,
    cb_ref,
    skip_ref,
    gain_ref,
    hl_sig,
    hr_sig,
    hl_bc,
    hr_bc,
    tot_buf,
    ext,
    ext_bc,
    xs,
    rt,
    roll_a,
    we_f,
    we_dw,
    keep,
    snd,
    pin,
    csnd,
    crecv,
    esnd,
    ein,
    eown,
    yloc,
    outs,
    mid,
    landing,
    inv_snd,
    inv_buf,
    halo_ssem,
    halo_rsem,
    tot_ssem,
    tot_rsem,
    pin_ssem,
    pin_rsem,
    chip_ssem,
    chip_rsem,
    ein_ssem,
    ein_rsem,
    out_ssem,
    out_rsem,
    fwd_ssem,
    fwd_rsem,
    inv_ssem,
    inv_rsem,
    load_sem,
):
    T = tm_count
    M = T // 2
    CW = INNER // T
    HG = CW // HEADDIM
    per = T // batch_count
    me = lax.axis_index("tm")
    rec = lax.axis_index("batch")
    core = lax.rem(me, 2)
    chip = me // 2
    forward = core == 1
    partner = me + 1 - 2 * core
    dest = me // per
    place = jnp.where(forward, chip, M - 1 - chip)

    def at(tm, batch=None):
        return {"tm": tm, "batch": rec if batch is None else batch}

    small = [(step_hbm, step_ref), (rate_hbm, rate_ref), (bcf_hbm, bcf_ref), (bcb_hbm, bcb_ref),
             (skip_hbm, skip_ref), (cb_hbm, cb_ref), (cw_hbm, cw_ref), (sig_hbm, sig_ref)]
    late = [(gate_hbm, gate_ref), (gain_hbm, gain_ref)]
    loads = [
        pltpu.make_async_copy(src, dst, load_sem.at[k]) for k, (src, dst) in enumerate(small + late)
    ]
    for load in loads:
        load.start()

    barrier = pltpu.get_barrier_semaphore()

    def greet(tm, batch):
        pl.semaphore_signal(
            barrier, inc=1, device_id={"tm": tm, "batch": batch},
            device_id_type=pl.DeviceIdType.MESH,
        )

    own_dest = dest == rec
    for j in range(T):

        @pl.when(j != me)
        def _():
            greet(j, rec)

        @pl.when(jnp.logical_or(j != me, jnp.logical_not(own_dest)))
        def _():
            greet(j, dest)

    for b in range(batch_count):
        for q in range(per):

            @pl.when(jnp.logical_or(b != rec, rec * per + q != me))
            def _():
                greet(rec * per + q, b)

    for b in range(batch_count):

        @pl.when(b != rec)
        def _():
            greet(me, b)

    pl.semaphore_wait(barrier, (T - 1) + 2 * (T - jnp.where(own_dest, 1, 0)) + batch_count - 1)

    def remote(src, dst, ssem, rsem, device):
        return pltpu.make_async_remote_copy(
            src_ref=src, dst_ref=dst, send_sem=ssem, recv_sem=rsem,
            device_id=device, device_id_type=pl.DeviceIdType.MESH,
        )

    to_right = [
        remote(sig_hbm.at[pl.ds(ROWS - RIM, RIM)], hl_sig, halo_ssem.at[0], halo_rsem.at[0], at(me + 1)),
        remote(bcf_hbm.at[pl.ds(ROWS - RIM, RIM)], hl_bc, halo_ssem.at[1], halo_rsem.at[1], at(me + 1)),
    ]
    to_left = [
        remote(sig_hbm.at[pl.ds(0, RIM)], hr_sig, halo_ssem.at[2], halo_rsem.at[2], at(me - 1)),
        remote(bcb_hbm.at[pl.ds(0, RIM)], hr_bc, halo_ssem.at[3], halo_rsem.at[3], at(me - 1)),
    ]

    @pl.when(me < T - 1)
    def _():
        for copy in to_right[::-1]:
            copy.start()

    @pl.when(me > 0)
    def _():
        for copy in to_left[::-1]:
            copy.start()

    for load in loads[: len(small)]:
        load.wait()
    raw = step_ref[...].astype(F32)
    step = jnp.maximum(raw, 0.0) + jnp.log1p(jnp.exp(-jnp.abs(raw)))
    rate = jnp.concatenate([rate_ref[0:1, :], rate_ref[1:2, :]], axis=1)
    log_decay = -step * rate
    row = lax.broadcasted_iota(jnp.int32, (ROWS, ROWS), 0)
    col = lax.broadcasted_iota(jnp.int32, (ROWS, ROWS), 1)
    lower = row >= col
    upper = row <= col
    fwd_lane = col < HEADS
    high = lax.Precision.HIGHEST
    cum = jnp.where(
        fwd_lane,
        dot(lower.astype(F32), log_decay, precision=high),
        dot(upper.astype(F32), log_decay, precision=high),
    )
    total = jnp.where(fwd_lane[0:1], cum[ROWS - 1 : ROWS], cum[0:1])
    tot_buf[me] = jnp.broadcast_to(total, (8, ROWS))

    def tot_copy(j):
        return remote(tot_buf.at[me], tot_buf.at[me], tot_ssem.at[j], tot_rsem.at[me], at(j))

    for j in range(T):

        @pl.when(j != me)
        def _():
            tot_copy(j).start()

    we_f[0:ROWS] = split_bf16(jnp.exp(total - cum) * step)
    we_f[ROWS : 2 * ROWS] = split_bf16(jnp.exp(cum))
    rt[...] = (LOG2E * (jnp.log(step) - cum)).T
    scaled_cum = LOG2E * cum
    roll_a[...] = scaled_cum
    skip = jnp.concatenate([skip_ref[0:1, :], skip_ref[1:2, :]], axis=1)
    skip_split = split_bf16(jnp.broadcast_to(skip, (16, 2 * HEADS)))
    own_dir = (lax.broadcasted_iota(jnp.int32, (1, 2 * HEADS), 1) < HEADS) == forward

    def spread(g, first):
        k = lax.broadcasted_iota(jnp.int32, (4 * HEADS, CW), 0)
        c = lax.broadcasted_iota(jnp.int32, (4 * HEADS, CW), 1)
        head = first + g * HG + c // HEADDIM
        return (lax.rem(k, 2 * HEADS) == head).astype(F32).astype(BF16)

    @pl.when(me == 0)
    def _():
        hl_sig[...] = jnp.zeros_like(hl_sig)
        hl_bc[...] = jnp.zeros_like(hl_bc)

    @pl.when(me == T - 1)
    def _():
        hr_sig[...] = jnp.zeros_like(hr_sig)
        hr_bc[...] = jnp.zeros_like(hr_bc)

    @pl.when(me > 0)
    def _():
        for copy in to_right:
            copy.wait_recv()

    @pl.when(me < T - 1)
    def _():
        for copy in to_left:
            copy.wait_recv()

    def conv(buf, direction, cols):
        half = 0.5 * cb_ref[direction : direction + 1, cols]
        for k in range(4):
            start = 5 + k if direction == 0 else 11 - k
            tap = 0.5 * cw_ref[direction, k : k + 1, cols]
            half = half + tap * buf[start : start + ROWS, :]
        return half_silu(half).astype(BF16)

    bc_cols = slice(INNER, INNER + 2 * STATE)
    ext_bc[0:8] = hl_bc[...].astype(F32)[8:16]
    ext_bc[8 : 8 + ROWS] = bcf_ref[...].astype(F32)
    bc_f = conv(ext_bc, 0, bc_cols)
    ext_bc[8 : 8 + ROWS] = bcb_ref[...].astype(F32)
    ext_bc[8 + ROWS : 16 + ROWS] = hr_bc[...].astype(F32)[0:8]
    bc_b = conv(ext_bc, 1, bc_cols)
    bt_f = bc_f.astype(F32).T[:STATE].astype(BF16)
    bt_b = bc_b.astype(F32).T[:STATE].astype(BF16)
    c_f = bc_f[:, STATE:]
    c_b = bc_b[:, STATE:]
    scores_f = dot(c_f, bt_f)
    scores_b = dot(c_b, bt_b)
    bias_f = jnp.where(lower, 0.0, MASKED)
    bias_b = jnp.where(upper, 0.0, MASKED)

    def cols_of(g):
        return pl.ds(pl.multiple_of(g * CW, CW), CW)

    def pin_copy(g):
        return remote(snd.at[g], pin.at[g], pin_ssem.at[g], pin_rsem.at[g], at(partner))

    def chip_copy(g, target):
        tm = jnp.where(forward, 2 * target + 1, 2 * (M - 1 - target))
        return remote(
            csnd.at[g], crecv.at[place, g], chip_ssem.at[target, g], chip_rsem.at[place, g], at(tm)
        )

    def recv_chip(g, source):
        return remote(
            csnd.at[g], crecv.at[source, g], chip_ssem.at[source, g], chip_rsem.at[source, g], at(partner)
        )

    own_first = jnp.where(forward, 0, HEADS)

    def combine(g):
        pin_copy(g).wait_recv()
        factor = jnp.where(
            forward,
            dot(we_f[2 * ROWS - 16 :], spread(g, 0))[15:16],
            dot(we_f[ROWS : ROWS + 16], spread(g, HEADS))[0:1],
        )
        csnd[g] = (pin[g].astype(F32) * factor + keep[g]).astype(BF16)
        for target in range(1, M):

            @pl.when(place < target)
            def _():
                chip_copy(g, target).start()

    def first(g, _):
        cols = cols_of(g)
        ext[0:8] = hl_sig[:, cols].astype(F32)[8:16]
        ext[8 : 8 + ROWS] = sig_ref[:, cols].astype(F32)
        ext[8 + ROWS : 16 + ROWS] = hr_sig[:, cols].astype(F32)[0:8]
        x_f = conv(ext, 0, cols)
        x_b = conv(ext, 1, cols)
        xs[0:ROWS, cols] = x_f
        xs[ROWS : 2 * ROWS, cols] = x_b
        w_f = dot(we_f[0:ROWS], spread(g, 0))
        w_b = dot(we_f[0:ROWS], spread(g, HEADS))
        state_f = dot(bt_f, (x_f.astype(F32) * w_f).astype(BF16))
        state_b = dot(bt_b, (x_b.astype(F32) * w_b).astype(BF16))
        snd[g] = jnp.where(forward, state_b, state_f).astype(BF16)
        keep[g] = jnp.where(forward, state_f, state_b)
        pin_copy(g).start()

        @pl.when(g > 0)
        def _():
            combine(g - 1)

        return 0

    lax.fori_loop(0, T, first, 0)
    combine(T - 1)

    lane = lax.broadcasted_iota(jnp.int32, (ROWS, 2 * HEADDIM), 1)

    def local(g, _):
        rolled = pltpu.roll(roll_a[...], lax.rem(2 * HEADS - g * HG, 2 * HEADS), 1)
        skips_f = dot(skip_split, spread(g, 0))[0:1]
        skips_b = dot(skip_split, spread(g, HEADS))[0:1]

        def mixing(h):
            a_f = rolled[:, h : h + 1]
            a_b = rolled[:, HEADS + h : HEADS + h + 1]
            r_f = rt[pl.ds(g * HG + h, 1), :]
            r_b = rt[pl.ds(HEADS + g * HG + h, 1), :]
            mix_f = (scores_f * jnp.exp2((a_f + r_f) + bias_f)).astype(BF16)
            mix_b = (scores_b * jnp.exp2((a_b + r_b) + bias_b)).astype(BF16)
            return jnp.concatenate([mix_f, mix_b], axis=1)

        for pair in range(HG // 2):
            width = 2 * HEADDIM
            cols = pl.ds(pl.multiple_of(g * CW + pair * width, width), width)
            x_pair = xs[:, cols]
            stacked = jnp.concatenate([mixing(2 * pair), mixing(2 * pair + 1)], axis=0)
            both = dot(stacked, x_pair)
            out = jnp.where(lane < HEADDIM, both[:ROWS], both[ROWS:])
            inside = slice(pair * width, (pair + 1) * width)
            out = out + skips_f[:, inside] * x_pair[:ROWS].astype(F32)
            out = out + skips_b[:, inside] * x_pair[ROWS:].astype(F32)
            yloc[:, cols] = out
        return 0

    lax.fori_loop(0, T, local, 0)

    for j in range(T):

        @pl.when(j != me)
        def _():
            remote(tot_buf.at[j], tot_buf.at[j], tot_ssem.at[j], tot_rsem.at[j], at(partner)).wait_recv()

    rows = [tot_buf[partner][0:1]]
    chips = [tot_buf[2 * q][0:1] + tot_buf[2 * q + 1][0:1] for q in range(M)]
    for source in range(M - 1):
        sum_f = jnp.zeros((1, 2 * HEADS), F32)
        sum_b = jnp.zeros((1, 2 * HEADS), F32)
        for q in range(source + 1, M):
            sum_f = sum_f + jnp.where(q < place, chips[q], 0.0)
            sum_b = sum_b + jnp.where(q < place, chips[M - 1 - q], 0.0)
        rows.append(jnp.where(forward, sum_f, sum_b))
    padding = -len(rows) % 16
    rows = jnp.exp(jnp.concatenate(rows + [jnp.zeros((padding, 2 * HEADS), F32)], axis=0))
    we_dw[...] = split_bf16(jnp.where(own_dir, rows, 0.0))

    def ein_copy(g):
        return remote(esnd.at[g], ein.at[g], ein_ssem.at[g], ein_rsem.at[g], at(partner))

    def enter(s, _):
        g = lax.rem(me + s, T)
        factors = dot(we_dw[...], spread(g, own_first))
        esnd[g] = jnp.zeros((STATE, CW), BF16)
        entering = keep.at[g]
        entering[...] = jnp.zeros((STATE, CW), F32)
        for source in range(M - 1):

            @pl.when(source < place)
            def _():
                recv_chip(g, source).wait_recv()
                entering[...] += factors[source + 1 : source + 2] * crecv[source, g].astype(F32)

        value = entering[...]
        esnd[g] = value.astype(BF16)
        ein_copy(g).start()
        eown[g] = (value * factors[0:1] + pin[g].astype(F32)).astype(BF16)
        return 0

    lax.fori_loop(0, T, enter, 0)

    slot = lax.rem(me, per)

    def out_copy(g):
        return remote(outs.at[g], mid.at[me], out_ssem.at[g], out_rsem.at[me], at(g))

    def forward_copy(i):
        n = rec * per + lax.rem(i, per)
        return remote(mid.at[i], landing.at[n], fwd_ssem.at[i], fwd_rsem.at[n], at(me, i // per))

    def pass_on(s):
        there = lax.rem(me + T - s, T)
        i = there + 1 - 2 * lax.rem(there, 2)

        @pl.when(i != me)
        def _():
            remote(outs.at[i], mid.at[i], out_ssem.at[i], out_rsem.at[i], at(partner)).wait_recv()

        @pl.when(i // per == rec)
        def _():
            landing[rec * per + lax.rem(i, per)] = mid[i]

        @pl.when(i // per != rec)
        def _():
            forward_copy(i).start()

    for load in loads[len(small) :]:
        load.wait()

    def last(s, squares):
        g = lax.rem(partner + s, T)
        cols = cols_of(g)
        ein_copy(g).wait_recv()
        own, other = eown[g], ein[g]
        enter_f = jnp.where(forward, own, other)
        enter_b = jnp.where(forward, other, own)
        decay_f = dot(we_f[ROWS : 2 * ROWS], spread(g, 0))
        decay_b = dot(we_f[ROWS : 2 * ROWS], spread(g, HEADS))
        y = yloc[:, cols] + decay_f * dot(c_f, enter_f) + decay_b * dot(c_b, enter_b)
        gated = y * half_silu(0.5 * gate_ref[:, cols].astype(F32))
        for part in range(CW // 128):
            piece = gated[:, part * 128 : (part + 1) * 128]
            squares = squares + piece * piece
        outs[g] = gated.astype(BF16)

        @pl.when(g == me)
        def _():
            mid[me] = outs[g]

        @pl.when(g != me)
        def _():
            out_copy(g).start()

        @pl.when(s >= LAG)
        def _():
            pass_on(s - LAG)

        return squares

    squares = lax.fori_loop(0, T, last, jnp.zeros((ROWS, 128), F32))
    mean = jnp.sum(squares.T, axis=0, keepdims=True) * (1.0 / INNER)
    inv_snd[...] = jnp.broadcast_to(lax.rsqrt(mean + EPSILON), (8, ROWS))

    def inv_copy(j):
        return remote(
            inv_snd, inv_buf.at[rec * per + slot], inv_ssem.at[j], inv_rsem.at[rec * per + slot],
            at(j, dest),
        )

    for j in range(T):
        mine = jnp.logical_and(own_dest, j == me)

        @pl.when(mine)
        def _():
            inv_buf[rec * per + slot] = inv_snd[...]

        @pl.when(jnp.logical_not(mine))
        def _():
            inv_copy(j).start()

    for s in range(T - LAG, T):
        pass_on(s)

    gain = gain_ref[:, cols_of(me)]

    for b in range(batch_count):
        for q in range(per):
            n = b * per + q
            mine = jnp.logical_and(b == rec, rec * per + q == me)

            @pl.when(b != rec)
            def _():
                remote(mid.at[0], landing.at[n], fwd_ssem.at[0], fwd_rsem.at[n], at(partner)).wait_recv()

            @pl.when(jnp.logical_not(mine))
            def _():
                remote(inv_snd, inv_buf.at[n], inv_ssem.at[0], inv_rsem.at[n], at(partner)).wait_recv()

            scale = jnp.broadcast_to(inv_buf[n][0:1], (ROWS, ROWS)).T
            for part in range(CW // 128):
                inside = slice(part * 128, (part + 1) * 128)
                piece = landing[n, :, inside].astype(F32) * scale * gain[:, inside]
                out_ref[b, q * ROWS : (q + 1) * ROWS, inside] = piece.astype(BF16)

    @pl.when(me < T - 1)
    def _():
        for copy in to_right:
            copy.wait_send()

    @pl.when(me > 0)
    def _():
        for copy in to_left:
            copy.wait_send()

    for j in range(T):

        @pl.when(j != me)
        def _():
            tot_copy(j).wait_send()

        @pl.when(jnp.logical_not(jnp.logical_and(own_dest, j == me)))
        def _():
            inv_copy(j).wait_send()

        @pl.when(j != me)
        def _():
            out_copy(j).wait_send()

        @pl.when(j // per != rec)
        def _():
            forward_copy(j).wait_send()

    def sent(g, _):
        pin_copy(g).wait_send()
        ein_copy(g).wait_send()
        for target in range(1, M):

            @pl.when(place < target)
            def _():
                chip_copy(g, target).wait_send()

        return 0

    lax.fori_loop(0, T, sent, 0)


def shards(tm_count, batch_count, signal, gate_input, bc_forward, bc_backward, step_raw,
           decay_rate, conv_weight, conv_bias, skip_gain, norm_gain):
    T, M = tm_count, tm_count // 2
    CW = INNER // T
    per = T // batch_count
    vmem = pltpu.VMEM
    dma = pltpu.SemaphoreType.DMA
    args = (signal[0], gate_input[0], bc_forward[0], bc_backward[0], step_raw[0],
            decay_rate, conv_weight, conv_bias, skip_gain, norm_gain.reshape(1, INNER))
    scratch = [vmem(a.shape, a.dtype) for a in args] + [
        vmem((RIM, INNER), BF16),
        vmem((RIM, INNER), BF16),
        vmem((RIM, 2 * STATE), BF16),
        vmem((RIM, 2 * STATE), BF16),
        vmem((T, 8, ROWS), F32),
        vmem((ROWS + 16, CW), F32),
        vmem((ROWS + 16, 2 * STATE), F32),
        vmem((2 * ROWS, INNER), BF16),
        vmem((2 * HEADS, ROWS), F32),
        vmem((ROWS, 2 * HEADS), F32),
        vmem((2 * ROWS, 4 * HEADS), BF16),
        vmem((-(-M // 16) * 16, 4 * HEADS), BF16),
        vmem((T, STATE, CW), F32),
        vmem((T, STATE, CW), BF16),
        vmem((T, STATE, CW), BF16),
        vmem((T, STATE, CW), BF16),
        vmem((M, T, STATE, CW), BF16),
        vmem((T, STATE, CW), BF16),
        vmem((T, STATE, CW), BF16),
        vmem((T, STATE, CW), BF16),
        vmem((ROWS, INNER), F32),
        vmem((T, ROWS, CW), BF16),
        vmem((T, ROWS, CW), BF16),
        vmem((T, ROWS, CW), BF16),
        vmem((8, ROWS), F32),
        vmem((T, 8, ROWS), F32),
        dma((4,)),
        dma((4,)),
        dma((T,)),
        dma((T,)),
        dma((T,)),
        dma((T,)),
        dma((M, T)),
        dma((M, T)),
        dma((T,)),
        dma((T,)),
        dma((T,)),
        dma((T,)),
        dma((T,)),
        dma((T,)),
        dma((T,)),
        dma((T,)),
        dma((len(args),)),
    ]
    return pl.pallas_call(
        functools.partial(mixer_kernel, T, batch_count),
        out_shape=jax.ShapeDtypeStruct((batch_count, per * ROWS, CW), BF16),
        in_specs=[pl.BlockSpec(memory_space=pl.ANY)] * len(args),
        out_specs=pl.BlockSpec(memory_space=pltpu.VMEM),
        scratch_shapes=scratch,
        compiler_params=pltpu.CompilerParams(
            collective_id=0, has_side_effects=True, vmem_limit_bytes=60 * 2**20
        ),
        cost_estimate=pl.CostEstimate(
            flops=10**9, bytes_accessed=8 * 2**20, transcendentals=4 * 10**6
        ),
    )(*args)


def solution(mesh):
    in_specs = (P("batch", "tm", None),) * 5 + (P(),) * 5
    return jax.shard_map(
        functools.partial(shards, mesh.shape["tm"], mesh.shape["batch"]),
        mesh=mesh, in_specs=in_specs, out_specs=P(None, "batch", "tm"), check_vma=False,
    )
```

```python
import functools

import jax
import jax.numpy as jnp
from jax import lax
from jax.experimental import pallas as pl
from jax.experimental.pallas import tpu as pltpu
from jax.sharding import PartitionSpec as P

INNER = 4096
HEADDIM = 64
STATE = 64
HEADS = 64
ROWS = 128
LAG = 2
RIM = 16
EPSILON = 1e-05
LOG2E = 1.4426950408889634
MASKED = -1e30

F32 = jnp.float32
BF16 = jnp.bfloat16


def dot(a, b, **kwargs):
    return jnp.dot(a, b, preferred_element_type=F32, **kwargs)


def split_bf16(value):
    high = value.astype(BF16)
    low = (value - high.astype(F32)).astype(BF16)
    return jnp.concatenate([high, low], axis=1)


def half_silu(half):
    return half + half * jnp.tanh(half)


def mixer_kernel(
    tm_count,
    batch_count,
    sig_hbm,
    gate_hbm,
    bcf_hbm,
    bcb_hbm,
    step_hbm,
    rate_hbm,
    cw_hbm,
    cb_hbm,
    skip_hbm,
    gain_hbm,
    out_ref,
    sig_ref,
    gate_ref,
    bcf_ref,
    bcb_ref,
    step_ref,
    rate_ref,
    cw_ref,
    cb_ref,
    skip_ref,
    gain_ref,
    hl_sig,
    hr_sig,
    hl_bc,
    hr_bc,
    tot_buf,
    ext,
    ext_bc,
    xs,
    rt,
    roll_a,
    we_f,
    we_dw,
    spread_ref,
    keep,
    snd,
    pin,
    csnd,
    crecv,
    esnd,
    ein,
    eown,
    yloc,
    outs,
    mid,
    landing,
    inv_snd,
    inv_buf,
    halo_ssem,
    halo_rsem,
    right_ssem,
    right_rsem,
    left_ssem,
    left_rsem,
    tot_ssem,
    tot_rsem,
    pin_ssem,
    pin_rsem,
    chip_ssem,
    chip_rsem,
    ein_ssem,
    ein_rsem,
    out_ssem,
    out_rsem,
    fwd_ssem,
    fwd_rsem,
    inv_ssem,
    inv_rsem,
    load_sem,
):
    T = tm_count
    M = T // 2
    CW = INNER // T
    HG = CW // HEADDIM
    per = T // batch_count
    me = lax.axis_index("tm")
    rec = lax.axis_index("batch")
    core = lax.rem(me, 2)
    chip = me // 2
    forward = core == 1
    partner = me + 1 - 2 * core
    dest = me // per
    place = jnp.where(forward, chip, M - 1 - chip)

    def at(tm, batch=None):
        return {"tm": tm, "batch": rec if batch is None else batch}

    small = [(step_hbm, step_ref), (rate_hbm, rate_ref), (bcf_hbm, bcf_ref), (bcb_hbm, bcb_ref),
             (skip_hbm, skip_ref), (cb_hbm, cb_ref), (cw_hbm, cw_ref), (sig_hbm, sig_ref)]
    late = [(gate_hbm, gate_ref), (gain_hbm, gain_ref)]
    loads = [
        pltpu.make_async_copy(src, dst, load_sem.at[k]) for k, (src, dst) in enumerate(small + late)
    ]
    for load in loads:
        load.start()

    barrier = pltpu.get_barrier_semaphore()

    def greet(tm, batch):
        pl.semaphore_signal(
            barrier, inc=1, device_id={"tm": tm, "batch": batch},
            device_id_type=pl.DeviceIdType.MESH,
        )

    own_dest = dest == rec
    for j in range(T):

        @pl.when(j != me)
        def _():
            greet(j, rec)

        @pl.when(jnp.logical_or(j != me, jnp.logical_not(own_dest)))
        def _():
            greet(j, dest)

    for b in range(batch_count):
        for q in range(per):

            @pl.when(jnp.logical_or(b != rec, rec * per + q != me))
            def _():
                greet(rec * per + q, b)

    for b in range(batch_count):

        @pl.when(b != rec)
        def _():
            greet(me, b)


    def remote(src, dst, ssem, rsem, device):
        return pltpu.make_async_remote_copy(
            src_ref=src, dst_ref=dst, send_sem=ssem, recv_sem=rsem,
            device_id=device, device_id_type=pl.DeviceIdType.MESH,
        )

    offset = (lax.broadcasted_iota(jnp.int32, (4 * HEADS, CW), 0) & (2 * HEADS - 1)) - (
        lax.broadcasted_iota(jnp.int32, (4 * HEADS, CW), 1) >> 6
    )

    def lay_out(n, _):
        spread_ref[n] = jnp.where(offset == n * HG, 1.0, 0.0).astype(BF16)
        return 0

    lax.fori_loop(0, 2 * T, lay_out, 0)

    for load in loads[: len(small)]:
        load.wait()
    raw = step_ref[...].astype(F32)
    step = jnp.maximum(raw, 0.0) + jnp.log1p(jnp.exp(-jnp.abs(raw)))
    rate = jnp.concatenate([rate_ref[0:1, :], rate_ref[1:2, :]], axis=1)
    log_decay = -step * rate
    row = lax.broadcasted_iota(jnp.int32, (ROWS, ROWS), 0)
    col = lax.broadcasted_iota(jnp.int32, (ROWS, ROWS), 1)
    lower = row >= col
    upper = row <= col
    fwd_lane = col < HEADS
    high = lax.Precision.HIGHEST
    cum = jnp.where(
        fwd_lane,
        dot(lower.astype(F32), log_decay, precision=high),
        dot(upper.astype(F32), log_decay, precision=high),
    )
    total = jnp.where(fwd_lane[0:1], cum[ROWS - 1 : ROWS], cum[0:1])
    tot_buf[me] = jnp.broadcast_to(total, (8, ROWS))

    def tot_copy(j):
        return remote(tot_buf.at[me], tot_buf.at[me], tot_ssem.at[j], tot_rsem.at[me], at(j))

    we_f[0:ROWS] = split_bf16(jnp.exp(total - cum) * step)
    we_f[ROWS : 2 * ROWS] = split_bf16(jnp.exp(cum))
    rt[...] = (LOG2E * (jnp.log(step) - cum)).T
    scaled_cum = LOG2E * cum
    roll_a[...] = scaled_cum
    skip = jnp.concatenate([skip_ref[0:1, :], skip_ref[1:2, :]], axis=1)
    skip_split = split_bf16(jnp.broadcast_to(skip, (16, 2 * HEADS)))
    own_dir = (lax.broadcasted_iota(jnp.int32, (1, 2 * HEADS), 1) < HEADS) == forward

    def spread(g, direction):
        return spread_ref[direction * T + g]

    def cols_of(g):
        return pl.ds(pl.multiple_of(g * CW, CW), CW)

    bc_right = remote(
        bcf_hbm.at[pl.ds(ROWS - RIM, RIM)], hl_bc, halo_ssem.at[0], halo_rsem.at[0], at(me + 1)
    )
    bc_left = remote(bcb_hbm.at[pl.ds(0, RIM)], hr_bc, halo_ssem.at[1], halo_rsem.at[1], at(me - 1))

    def sig_right(g):
        return remote(
            sig_hbm.at[pl.ds(ROWS - RIM, RIM), cols_of(g)], hl_sig.at[:, cols_of(g)],
            right_ssem.at[g], right_rsem.at[g], at(me + 1),
        )

    def sig_left(g):
        return remote(
            sig_hbm.at[pl.ds(0, RIM), cols_of(g)], hr_sig.at[:, cols_of(g)],
            left_ssem.at[g], left_rsem.at[g], at(me - 1),
        )

    pl.semaphore_wait(barrier, (T - 1) + 2 * (T - jnp.where(own_dest, 1, 0)) + batch_count - 1)

    @pl.when(me < T - 1)
    def _():
        bc_right.start()
        sig_right(0).start()

    @pl.when(me > 0)
    def _():
        bc_left.start()
        sig_left(0).start()

    for g in range(1, T):

        @pl.when(me < T - 1)
        def _():
            sig_right(g).start()

        @pl.when(me > 0)
        def _():
            sig_left(g).start()

    for j in range(T):

        @pl.when(j != me)
        def _():
            tot_copy(j).start()

    @pl.when(me == 0)
    def _():
        hl_sig[...] = jnp.zeros_like(hl_sig)
        hl_bc[...] = jnp.zeros_like(hl_bc)

    @pl.when(me == T - 1)
    def _():
        hr_sig[...] = jnp.zeros_like(hr_sig)
        hr_bc[...] = jnp.zeros_like(hr_bc)

    @pl.when(me > 0)
    def _():
        bc_right.wait_recv()

    @pl.when(me < T - 1)
    def _():
        bc_left.wait_recv()

    def conv(buf, direction, cols):
        half = 0.5 * cb_ref[direction : direction + 1, cols]
        for k in range(4):
            start = 5 + k if direction == 0 else 11 - k
            tap = 0.5 * cw_ref[direction, k : k + 1, cols]
            half = half + tap * buf[start : start + ROWS, :]
        return half_silu(half).astype(BF16)

    bc_cols = slice(INNER, INNER + 2 * STATE)
    ext_bc[0:8] = hl_bc[...].astype(F32)[8:16]
    ext_bc[8 : 8 + ROWS] = bcf_ref[...].astype(F32)
    bc_f = conv(ext_bc, 0, bc_cols)
    ext_bc[8 : 8 + ROWS] = bcb_ref[...].astype(F32)
    ext_bc[8 + ROWS : 16 + ROWS] = hr_bc[...].astype(F32)[0:8]
    bc_b = conv(ext_bc, 1, bc_cols)
    bt_f = bc_f.astype(F32).T[:STATE].astype(BF16)
    bt_b = bc_b.astype(F32).T[:STATE].astype(BF16)
    c_f = bc_f[:, STATE:]
    c_b = bc_b[:, STATE:]
    scores_f = dot(c_f, bt_f)
    scores_b = dot(c_b, bt_b)
    bias_f = jnp.where(lower, 0.0, MASKED)
    bias_b = jnp.where(upper, 0.0, MASKED)

    def pin_copy(g):
        return remote(snd.at[g], pin.at[g], pin_ssem.at[g], pin_rsem.at[g], at(partner))

    def chip_copy(g, target):
        tm = jnp.where(forward, 2 * target + 1, 2 * (M - 1 - target))
        return remote(
            csnd.at[g], crecv.at[place, g], chip_ssem.at[target, g], chip_rsem.at[place, g], at(tm)
        )

    def recv_chip(g, source):
        return remote(
            csnd.at[g], crecv.at[source, g], chip_ssem.at[source, g], chip_rsem.at[source, g], at(partner)
        )

    own_direction = jnp.where(forward, 0, 1)

    def combine(g):
        pin_copy(g).wait_recv()
        factor = jnp.where(
            forward,
            dot(we_f[2 * ROWS - 16 :], spread(g, 0))[15:16],
            dot(we_f[ROWS : ROWS + 16], spread(g, 1))[0:1],
        )
        csnd[g] = (pin[g].astype(F32) * factor + keep[g]).astype(BF16)
        for target in range(1, M):

            @pl.when(place < target)
            def _():
                chip_copy(g, target).start()

    def first(g, _):
        cols = cols_of(g)

        @pl.when(me > 0)
        def _():
            sig_right(g).wait_recv()

        @pl.when(me < T - 1)
        def _():
            sig_left(g).wait_recv()

        ext[0:8] = hl_sig[:, cols].astype(F32)[8:16]
        ext[8 : 8 + ROWS] = sig_ref[:, cols].astype(F32)
        ext[8 + ROWS : 16 + ROWS] = hr_sig[:, cols].astype(F32)[0:8]
        x_f = conv(ext, 0, cols)
        x_b = conv(ext, 1, cols)
        xs[0:ROWS, cols] = x_f
        xs[ROWS : 2 * ROWS, cols] = x_b
        w_f = dot(we_f[0:ROWS], spread(g, 0))
        w_b = dot(we_f[0:ROWS], spread(g, 1))
        state_f = dot(bt_f, (x_f.astype(F32) * w_f).astype(BF16))
        state_b = dot(bt_b, (x_b.astype(F32) * w_b).astype(BF16))
        snd[g] = jnp.where(forward, state_b, state_f).astype(BF16)
        keep[g] = jnp.where(forward, state_f, state_b)
        pin_copy(g).start()

        @pl.when(g > 0)
        def _():
            combine(g - 1)

        return 0

    lax.fori_loop(0, T, first, 0)
    combine(T - 1)

    lane = lax.broadcasted_iota(jnp.int32, (ROWS, 2 * HEADDIM), 1)

    def local(g, _):
        rolled = pltpu.roll(roll_a[...], lax.rem(2 * HEADS - g * HG, 2 * HEADS), 1)
        skips_f = dot(skip_split, spread(g, 0))[0:1]
        skips_b = dot(skip_split, spread(g, 1))[0:1]

        def mixing(h):
            a_f = rolled[:, h : h + 1]
            a_b = rolled[:, HEADS + h : HEADS + h + 1]
            r_f = rt[pl.ds(g * HG + h, 1), :]
            r_b = rt[pl.ds(HEADS + g * HG + h, 1), :]
            mix_f = (scores_f * jnp.exp2((a_f + r_f) + bias_f)).astype(BF16)
            mix_b = (scores_b * jnp.exp2((a_b + r_b) + bias_b)).astype(BF16)
            return jnp.concatenate([mix_f, mix_b], axis=1)

        for pair in range(HG // 2):
            width = 2 * HEADDIM
            cols = pl.ds(pl.multiple_of(g * CW + pair * width, width), width)
            x_pair = xs[:, cols]
            stacked = jnp.concatenate([mixing(2 * pair), mixing(2 * pair + 1)], axis=0)
            both = dot(stacked, x_pair)
            out = jnp.where(lane < HEADDIM, both[:ROWS], both[ROWS:])
            inside = slice(pair * width, (pair + 1) * width)
            out = out + skips_f[:, inside] * x_pair[:ROWS].astype(F32)
            out = out + skips_b[:, inside] * x_pair[ROWS:].astype(F32)
            yloc[:, cols] = out
        return 0

    lax.fori_loop(0, T, local, 0)

    for j in range(T):

        @pl.when(j != me)
        def _():
            remote(tot_buf.at[j], tot_buf.at[j], tot_ssem.at[j], tot_rsem.at[j], at(partner)).wait_recv()

    rows = [tot_buf[partner][0:1]]
    chips = [tot_buf[2 * q][0:1] + tot_buf[2 * q + 1][0:1] for q in range(M)]
    for source in range(M - 1):
        sum_f = jnp.zeros((1, 2 * HEADS), F32)
        sum_b = jnp.zeros((1, 2 * HEADS), F32)
        for q in range(source + 1, M):
            sum_f = sum_f + jnp.where(q < place, chips[q], 0.0)
            sum_b = sum_b + jnp.where(q < place, chips[M - 1 - q], 0.0)
        rows.append(jnp.where(forward, sum_f, sum_b))
    padding = -len(rows) % 16
    rows = jnp.exp(jnp.concatenate(rows + [jnp.zeros((padding, 2 * HEADS), F32)], axis=0))
    we_dw[...] = split_bf16(jnp.where(own_dir, rows, 0.0))

    def ein_copy(g):
        return remote(esnd.at[g], ein.at[g], ein_ssem.at[g], ein_rsem.at[g], at(partner))

    def enter(s, _):
        g = lax.rem(me + s, T)
        factors = dot(we_dw[...], spread(g, own_direction))
        esnd[g] = jnp.zeros((STATE, CW), BF16)
        entering = keep.at[g]
        entering[...] = jnp.zeros((STATE, CW), F32)
        for source in range(M - 1):

            @pl.when(source < place)
            def _():
                recv_chip(g, source).wait_recv()
                entering[...] += factors[source + 1 : source + 2] * crecv[source, g].astype(F32)

        value = entering[...]
        esnd[g] = value.astype(BF16)
        ein_copy(g).start()
        eown[g] = (value * factors[0:1] + pin[g].astype(F32)).astype(BF16)
        return 0

    lax.fori_loop(0, T, enter, 0)

    slot = lax.rem(me, per)

    def out_copy(g):
        return remote(outs.at[g], mid.at[me], out_ssem.at[g], out_rsem.at[me], at(g))

    def forward_copy(i):
        n = rec * per + lax.rem(i, per)
        return remote(mid.at[i], landing.at[n], fwd_ssem.at[i], fwd_rsem.at[n], at(me, i // per))

    def pass_on(s):
        there = lax.rem(me + T - s, T)
        i = there + 1 - 2 * lax.rem(there, 2)

        @pl.when(i != me)
        def _():
            remote(outs.at[i], mid.at[i], out_ssem.at[i], out_rsem.at[i], at(partner)).wait_recv()

        @pl.when(i // per == rec)
        def _():
            landing[rec * per + lax.rem(i, per)] = mid[i]

        @pl.when(i // per != rec)
        def _():
            forward_copy(i).start()

    for load in loads[len(small) :]:
        load.wait()

    def last(s, squares):
        g = lax.rem(partner + s, T)
        cols = cols_of(g)
        ein_copy(g).wait_recv()
        own, other = eown[g], ein[g]
        enter_f = jnp.where(forward, own, other)
        enter_b = jnp.where(forward, other, own)
        decay_f = dot(we_f[ROWS : 2 * ROWS], spread(g, 0))
        decay_b = dot(we_f[ROWS : 2 * ROWS], spread(g, 1))
        y = yloc[:, cols] + decay_f * dot(c_f, enter_f) + decay_b * dot(c_b, enter_b)
        gated = y * half_silu(0.5 * gate_ref[:, cols].astype(F32))
        for part in range(CW // 128):
            piece = gated[:, part * 128 : (part + 1) * 128]
            squares = squares + piece * piece
        outs[g] = gated.astype(BF16)

        @pl.when(g == me)
        def _():
            mid[me] = outs[g]

        @pl.when(g != me)
        def _():
            out_copy(g).start()

        @pl.when(s >= LAG)
        def _():
            pass_on(s - LAG)

        return squares

    squares = lax.fori_loop(0, T, last, jnp.zeros((ROWS, 128), F32))
    mean = jnp.sum(squares.T, axis=0, keepdims=True) * (1.0 / INNER)
    inv_snd[...] = jnp.broadcast_to(lax.rsqrt(mean + EPSILON), (8, ROWS))

    def inv_copy(j):
        return remote(
            inv_snd, inv_buf.at[rec * per + slot], inv_ssem.at[j], inv_rsem.at[rec * per + slot],
            at(j, dest),
        )

    for j in range(T):
        mine = jnp.logical_and(own_dest, j == me)

        @pl.when(mine)
        def _():
            inv_buf[rec * per + slot] = inv_snd[...]

        @pl.when(jnp.logical_not(mine))
        def _():
            inv_copy(j).start()

    for s in range(T - LAG, T):
        pass_on(s)

    gain = gain_ref[:, cols_of(me)]

    for b in range(batch_count):
        for q in range(per):
            n = b * per + q
            mine = jnp.logical_and(b == rec, rec * per + q == me)

            @pl.when(b != rec)
            def _():
                remote(mid.at[0], landing.at[n], fwd_ssem.at[0], fwd_rsem.at[n], at(partner)).wait_recv()

            @pl.when(jnp.logical_not(mine))
            def _():
                remote(inv_snd, inv_buf.at[n], inv_ssem.at[0], inv_rsem.at[n], at(partner)).wait_recv()

            scale = jnp.broadcast_to(inv_buf[n][0:1], (ROWS, ROWS)).T
            for part in range(CW // 128):
                inside = slice(part * 128, (part + 1) * 128)
                piece = landing[n, :, inside].astype(F32) * scale * gain[:, inside]
                out_ref[b, q * ROWS : (q + 1) * ROWS, inside] = piece.astype(BF16)

    @pl.when(me < T - 1)
    def _():
        bc_right.wait_send()
        for g in range(T):
            sig_right(g).wait_send()

    @pl.when(me > 0)
    def _():
        bc_left.wait_send()
        for g in range(T):
            sig_left(g).wait_send()

    for j in range(T):

        @pl.when(j != me)
        def _():
            tot_copy(j).wait_send()

        @pl.when(jnp.logical_not(jnp.logical_and(own_dest, j == me)))
        def _():
            inv_copy(j).wait_send()

        @pl.when(j != me)
        def _():
            out_copy(j).wait_send()

        @pl.when(j // per != rec)
        def _():
            forward_copy(j).wait_send()

    def sent(g, _):
        pin_copy(g).wait_send()
        ein_copy(g).wait_send()
        for target in range(1, M):

            @pl.when(place < target)
            def _():
                chip_copy(g, target).wait_send()

        return 0

    lax.fori_loop(0, T, sent, 0)


def shards(tm_count, batch_count, signal, gate_input, bc_forward, bc_backward, step_raw,
           decay_rate, conv_weight, conv_bias, skip_gain, norm_gain):
    T, M = tm_count, tm_count // 2
    CW = INNER // T
    per = T // batch_count
    vmem = pltpu.VMEM
    dma = pltpu.SemaphoreType.DMA
    args = (signal[0], gate_input[0], bc_forward[0], bc_backward[0], step_raw[0],
            decay_rate, conv_weight, conv_bias, skip_gain, norm_gain.reshape(1, INNER))
    scratch = [vmem(a.shape, a.dtype) for a in args] + [
        vmem((RIM, INNER), BF16),
        vmem((RIM, INNER), BF16),
        vmem((RIM, 2 * STATE), BF16),
        vmem((RIM, 2 * STATE), BF16),
        vmem((T, 8, ROWS), F32),
        vmem((ROWS + 16, CW), F32),
        vmem((ROWS + 16, 2 * STATE), F32),
        vmem((2 * ROWS, INNER), BF16),
        vmem((2 * HEADS, ROWS), F32),
        vmem((ROWS, 2 * HEADS), F32),
        vmem((2 * ROWS, 4 * HEADS), BF16),
        vmem((-(-M // 16) * 16, 4 * HEADS), BF16),
        vmem((2 * T, 4 * HEADS, CW), BF16),
        vmem((T, STATE, CW), F32),
        vmem((T, STATE, CW), BF16),
        vmem((T, STATE, CW), BF16),
        vmem((T, STATE, CW), BF16),
        vmem((M, T, STATE, CW), BF16),
        vmem((T, STATE, CW), BF16),
        vmem((T, STATE, CW), BF16),
        vmem((T, STATE, CW), BF16),
        vmem((ROWS, INNER), F32),
        vmem((T, ROWS, CW), BF16),
        vmem((T, ROWS, CW), BF16),
        vmem((T, ROWS, CW), BF16),
        vmem((8, ROWS), F32),
        vmem((T, 8, ROWS), F32),
        dma((2,)),
        dma((2,)),
        dma((T,)),
        dma((T,)),
        dma((T,)),
        dma((T,)),
        dma((T,)),
        dma((T,)),
        dma((T,)),
        dma((T,)),
        dma((M, T)),
        dma((M, T)),
        dma((T,)),
        dma((T,)),
        dma((T,)),
        dma((T,)),
        dma((T,)),
        dma((T,)),
        dma((T,)),
        dma((T,)),
        dma((len(args),)),
    ]
    return pl.pallas_call(
        functools.partial(mixer_kernel, T, batch_count),
        out_shape=pltpu.VMEM((batch_count, per * ROWS, CW), BF16),
        in_specs=[pl.BlockSpec(memory_space=pltpu.HBM)] * len(args),
        out_specs=pl.BlockSpec(memory_space=pltpu.VMEM),
        scratch_shapes=scratch,
        compiler_params=pltpu.CompilerParams(
            collective_id=0, has_side_effects=True, vmem_limit_bytes=62 * 2**20
        ),
        cost_estimate=pl.CostEstimate(
            flops=10**9, bytes_accessed=8 * 2**20, transcendentals=4 * 10**6
        ),
    )(*args)


def solution(mesh):
    in_specs = (P("batch", "tm", None),) * 5 + (P(),) * 5
    return jax.shard_map(
        functools.partial(shards, mesh.shape["tm"], mesh.shape["batch"]),
        mesh=mesh, in_specs=in_specs, out_specs=P(None, "batch", "tm"), check_vma=False,
    )
```

```python
import functools

import jax
import jax.numpy as jnp
from jax import lax
from jax.experimental import pallas as pl
from jax.experimental.pallas import tpu as pltpu
from jax.sharding import PartitionSpec as P

INNER = 4096
HEADDIM = 64
STATE = 64
HEADS = 64
ROWS = 128
PIECE = 128
GROUP = 512
SPAN = GROUP // PIECE
LAG_LOCAL, LAG_ENTER, LAG_LAST, LAG_PASS = 2, 3, 4, 6
RIM = 16
EPSILON = 1e-05
LOG2E = 1.4426950408889634
MASKED = -1e30

F32 = jnp.float32
BF16 = jnp.bfloat16


def dot(a, b, **kwargs):
    return jnp.dot(a, b, preferred_element_type=F32, **kwargs)


def split_bf16(value):
    high = value.astype(BF16)
    low = (value - high.astype(F32)).astype(BF16)
    return jnp.concatenate([high, low], axis=1)


def half_silu(half):
    return half + half * jnp.tanh(half)


def mixer_kernel(
    tm_count,
    batch_count,
    sig_hbm,
    gate_hbm,
    bcf_hbm,
    bcb_hbm,
    step_hbm,
    rate_hbm,
    cw_hbm,
    cb_hbm,
    skip_hbm,
    gain_hbm,
    out_ref,
    sig_ref,
    gate_ref,
    bcf_ref,
    bcb_ref,
    step_ref,
    rate_ref,
    cw_ref,
    cb_ref,
    skip_ref,
    gain_ref,
    hl_sig,
    hr_sig,
    hl_bc,
    hr_bc,
    tot_buf,
    ext,
    ext_bc,
    xs,
    rt,
    roll_a,
    we,
    we_dw,
    extra,
    dec_f,
    dec_b,
    sgate,
    acc,
    spread_ref,
    keep,
    snd,
    pin,
    csnd,
    crecv,
    esnd,
    ein,
    eown,
    yloc,
    outs,
    mid,
    landing,
    inv_snd,
    inv_buf,
    halo_ssem,
    halo_rsem,
    right_ssem,
    right_rsem,
    left_ssem,
    left_rsem,
    tot_ssem,
    tot_rsem,
    pin_ssem,
    pin_rsem,
    chip_ssem,
    chip_rsem,
    ein_ssem,
    ein_rsem,
    out_ssem,
    out_rsem,
    fwd_ssem,
    fwd_rsem,
    inv_ssem,
    inv_rsem,
    load_sem,
):
    T = tm_count
    M = T // 2
    CW = INNER // T
    HG = CW // HEADDIM
    N = INNER // GROUP
    lap = T // SPAN
    per = T // batch_count
    me = lax.axis_index("tm")
    rec = lax.axis_index("batch")
    core = lax.rem(me, 2)
    chip = me // 2
    forward = core == 1
    partner = me + 1 - 2 * core
    dest = me // per
    place = jnp.where(forward, chip, M - 1 - chip)

    def at(tm, batch=None):
        return {"tm": tm, "batch": rec if batch is None else batch}

    small = [(step_hbm, step_ref), (rate_hbm, rate_ref), (bcf_hbm, bcf_ref), (bcb_hbm, bcb_ref),
             (skip_hbm, skip_ref), (cb_hbm, cb_ref), (cw_hbm, cw_ref), (sig_hbm, sig_ref)]
    late = [(gate_hbm, gate_ref), (gain_hbm, gain_ref)]
    loads = [
        pltpu.make_async_copy(src, dst, load_sem.at[k]) for k, (src, dst) in enumerate(small + late)
    ]
    for load in loads:
        load.start()

    barrier = pltpu.get_barrier_semaphore()

    def greet(tm, batch):
        pl.semaphore_signal(
            barrier, inc=1, device_id={"tm": tm, "batch": batch},
            device_id_type=pl.DeviceIdType.MESH,
        )

    own_dest = dest == rec
    for j in range(T):

        @pl.when(j != me)
        def _():
            greet(j, rec)

        @pl.when(jnp.logical_or(j != me, jnp.logical_not(own_dest)))
        def _():
            greet(j, dest)

    for b in range(batch_count):
        for q in range(per):

            @pl.when(jnp.logical_or(b != rec, rec * per + q != me))
            def _():
                greet(rec * per + q, b)

    for b in range(batch_count):

        @pl.when(b != rec)
        def _():
            greet(me, b)


    def remote(src, dst, ssem, rsem, device):
        return pltpu.make_async_remote_copy(
            src_ref=src, dst_ref=dst, send_sem=ssem, recv_sem=rsem,
            device_id=device, device_id_type=pl.DeviceIdType.MESH,
        )

    spot = lax.broadcasted_iota(jnp.int32, (4 * HEADS, GROUP), 1)
    offset = (lax.broadcasted_iota(jnp.int32, (4 * HEADS, GROUP), 0) & (2 * HEADS - 1)) - (
        (spot >> 7) * HG + ((spot >> 6) & 1)
    )

    def head_of(g):
        return lax.rem(g, lap) * SPAN * HG + 2 * (g // lap)

    def lay_out(g, _):
        spread_ref[0, g] = jnp.where(offset == head_of(g), 1.0, 0.0).astype(BF16)
        spread_ref[1, g] = jnp.where(offset == head_of(g) + HEADS, 1.0, 0.0).astype(BF16)
        return 0

    lax.fori_loop(0, N, lay_out, 0)

    for load in loads[: len(small)]:
        load.wait()
    raw = step_ref[...].astype(F32)
    step = jnp.maximum(raw, 0.0) + jnp.log1p(jnp.exp(-jnp.abs(raw)))
    rate = jnp.concatenate([rate_ref[0:1, :], rate_ref[1:2, :]], axis=1)
    log_decay = -step * rate
    row = lax.broadcasted_iota(jnp.int32, (ROWS, ROWS), 0)
    col = lax.broadcasted_iota(jnp.int32, (ROWS, ROWS), 1)
    lower = row >= col
    upper = row <= col
    fwd_lane = col < HEADS
    high = lax.Precision.HIGHEST
    cum = jnp.where(
        fwd_lane,
        dot(lower.astype(F32), log_decay, precision=high),
        dot(upper.astype(F32), log_decay, precision=high),
    )
    total = jnp.where(fwd_lane[0:1], cum[ROWS - 1 : ROWS], cum[0:1])
    tot_buf[me] = jnp.broadcast_to(total, (8, ROWS))

    def tot_copy(j):
        return remote(tot_buf.at[me], tot_buf.at[me], tot_ssem.at[j], tot_rsem.at[me], at(j))

    skip = jnp.concatenate([skip_ref[0:1, :], skip_ref[1:2, :]], axis=1)
    we[0:ROWS] = split_bf16(jnp.exp(total - cum) * step)
    we[ROWS : 2 * ROWS] = split_bf16(jnp.exp(cum))
    we[2 * ROWS :] = split_bf16(
        jnp.concatenate([jnp.exp(total), skip, jnp.zeros((14, 2 * HEADS), F32)], axis=0)
    )
    rt[...] = (LOG2E * (jnp.log(step) - cum)).T
    roll_a[...] = LOG2E * cum
    own_dir = (lax.broadcasted_iota(jnp.int32, (1, 2 * HEADS), 1) < HEADS) == forward
    acc[...] = jnp.zeros_like(acc)

    def spread(g, direction):
        return spread_ref[direction, g]

    def wide(k):
        return pl.ds(pl.multiple_of(k * SPAN * CW, SPAN * CW), SPAN * CW)

    bc_right = remote(
        bcf_hbm.at[pl.ds(ROWS - RIM, RIM)], hl_bc, halo_ssem.at[0], halo_rsem.at[0], at(me + 1)
    )
    bc_left = remote(bcb_hbm.at[pl.ds(0, RIM)], hr_bc, halo_ssem.at[1], halo_rsem.at[1], at(me - 1))

    def sig_right(g):
        return remote(
            sig_hbm.at[pl.ds(ROWS - RIM, RIM), wide(g)], hl_sig.at[:, wide(g)],
            right_ssem.at[g], right_rsem.at[g], at(me + 1),
        )

    def sig_left(g):
        return remote(
            sig_hbm.at[pl.ds(0, RIM), wide(g)], hr_sig.at[:, wide(g)],
            left_ssem.at[g], left_rsem.at[g], at(me - 1),
        )

    pl.semaphore_wait(barrier, (T - 1) + 2 * (T - jnp.where(own_dest, 1, 0)) + batch_count - 1)

    @pl.when(me < T - 1)
    def _():
        bc_right.start()
        sig_right(0).start()

    @pl.when(me > 0)
    def _():
        bc_left.start()
        sig_left(0).start()

    for g in range(1, lap):

        @pl.when(me < T - 1)
        def _():
            sig_right(g).start()

        @pl.when(me > 0)
        def _():
            sig_left(g).start()

    for j in range(T):

        @pl.when(j != me)
        def _():
            tot_copy(j).start()

    @pl.when(me == 0)
    def _():
        hl_sig[...] = jnp.zeros_like(hl_sig)
        hl_bc[...] = jnp.zeros_like(hl_bc)

    @pl.when(me == T - 1)
    def _():
        hr_sig[...] = jnp.zeros_like(hr_sig)
        hr_bc[...] = jnp.zeros_like(hr_bc)

    @pl.when(me > 0)
    def _():
        bc_right.wait_recv()

    @pl.when(me < T - 1)
    def _():
        bc_left.wait_recv()

    def conv(buf, direction, cols):
        half = 0.5 * cb_ref[direction : direction + 1, cols]
        for k in range(4):
            start = 5 + k if direction == 0 else 11 - k
            tap = 0.5 * cw_ref[direction, k : k + 1, cols]
            half = half + tap * buf[start : start + ROWS, :]
        return half_silu(half).astype(BF16)

    bc_cols = slice(INNER, INNER + 2 * STATE)
    ext_bc[0:8] = hl_bc[...].astype(F32)[8:16]
    ext_bc[8 : 8 + ROWS] = bcf_ref[...].astype(F32)
    bc_f = conv(ext_bc, 0, bc_cols)
    ext_bc[8 : 8 + ROWS] = bcb_ref[...].astype(F32)
    ext_bc[8 + ROWS : 16 + ROWS] = hr_bc[...].astype(F32)[0:8]
    bc_b = conv(ext_bc, 1, bc_cols)
    bt_f = bc_f.astype(F32).T[:STATE].astype(BF16)
    bt_b = bc_b.astype(F32).T[:STATE].astype(BF16)
    c_f = bc_f[:, STATE:]
    c_b = bc_b[:, STATE:]
    scores_f = dot(c_f, bt_f)
    scores_b = dot(c_b, bt_b)
    bias_f = jnp.where(lower, 0.0, MASKED)
    bias_b = jnp.where(upper, 0.0, MASKED)

    def pin_copy(g):
        return remote(snd.at[g], pin.at[g], pin_ssem.at[g], pin_rsem.at[g], at(partner))

    def chip_copy(g, target):
        tm = jnp.where(forward, 2 * target + 1, 2 * (M - 1 - target))
        return remote(
            csnd.at[g], crecv.at[place, g], chip_ssem.at[target, g], chip_rsem.at[place, g], at(tm)
        )

    def recv_chip(g, source):
        return remote(
            csnd.at[g], crecv.at[source, g], chip_ssem.at[source, g], chip_rsem.at[source, g], at(partner)
        )

    own_direction = jnp.where(forward, 0, 1)

    def place_of(g, piece):
        start = (lax.rem(g, lap) * SPAN + piece) * CW + (g // lap) * PIECE
        return (
            pl.ds(pl.multiple_of(start, PIECE), PIECE),
            pl.ds(pl.multiple_of(g * GROUP + piece * PIECE, PIECE), PIECE),
        )

    def cols_of(g):
        return pl.ds(pl.multiple_of(g * GROUP, GROUP), GROUP)

    def first(g):
        @pl.when(jnp.logical_and(me > 0, g < lap))
        def _():
            sig_right(g).wait_recv()

        @pl.when(jnp.logical_and(me < T - 1, g < lap))
        def _():
            sig_left(g).wait_recv()

        for piece in range(SPAN):
            cols, inside = place_of(g, piece)
            buf = ext.at[piece]
            buf[0:8] = hl_sig[:, cols].astype(F32)[8:16]
            buf[8 : 8 + ROWS] = sig_ref[:, cols].astype(F32)
            buf[8 + ROWS : 16 + ROWS] = hr_sig[:, cols].astype(F32)[0:8]
            xs[0:ROWS, inside] = conv(buf, 0, cols)
            xs[ROWS : 2 * ROWS, inside] = conv(buf, 1, cols)
        cols = cols_of(g)
        by_f = dot(we[...], spread(g, 0))
        by_b = dot(we[...], spread(g, 1))
        state_f = dot(bt_f, (xs[0:ROWS, cols].astype(F32) * by_f[0:ROWS]).astype(BF16))
        state_b = dot(bt_b, (xs[ROWS : 2 * ROWS, cols].astype(F32) * by_b[0:ROWS]).astype(BF16))
        snd[g] = jnp.where(forward, state_b, state_f).astype(BF16)
        pin_copy(g).start()
        keep[g] = jnp.where(forward, state_f, state_b)
        dec_f[:, cols] = by_f[ROWS : 2 * ROWS]
        dec_b[:, cols] = by_b[ROWS : 2 * ROWS]
        extra[g, 0:1] = jnp.where(forward, by_f[2 * ROWS : 2 * ROWS + 1], by_b[2 * ROWS : 2 * ROWS + 1])
        extra[g, 1:2] = by_f[2 * ROWS + 1 : 2 * ROWS + 2]
        extra[g, 2:3] = by_b[2 * ROWS + 1 : 2 * ROWS + 2]

    def combine(g):
        pin_copy(g).wait_recv()
        csnd[g] = (pin[g].astype(F32) * extra[g, 0:1] + keep[g]).astype(BF16)
        for target in range(1, M):

            @pl.when(place < target)
            def _():
                chip_copy(g, target).start()

    lane = lax.broadcasted_iota(jnp.int32, (ROWS, 2 * HEADDIM), 1)

    def local(g):
        rolled = pltpu.roll(roll_a[...], lax.rem(2 * HEADS - head_of(g), 2 * HEADS), 1)
        skips = extra[g, 1:3]

        def mixing(h):
            a_f = rolled[:, h : h + 1]
            a_b = rolled[:, HEADS + h : HEADS + h + 1]
            r_f = rt[pl.ds(head_of(g) + h, 1), :]
            r_b = rt[pl.ds(HEADS + head_of(g) + h, 1), :]
            mix_f = (scores_f * jnp.exp2((a_f + r_f) + bias_f)).astype(BF16)
            mix_b = (scores_b * jnp.exp2((a_b + r_b) + bias_b)).astype(BF16)
            return jnp.concatenate([mix_f, mix_b], axis=1)

        for piece in range(SPAN):
            cols, inside = place_of(g, piece)
            x_pair = xs[:, inside]
            head = piece * HG
            stacked = jnp.concatenate([mixing(head), mixing(head + 1)], axis=0)
            both = dot(stacked, x_pair)
            out = jnp.where(lane < HEADDIM, both[:ROWS], both[ROWS:])
            part = slice(piece * PIECE, (piece + 1) * PIECE)
            out = out + skips[0:1, part] * x_pair[:ROWS].astype(F32)
            out = out + skips[1:2, part] * x_pair[ROWS:].astype(F32)
            yloc[:, inside] = out
            sgate[:, inside] = half_silu(0.5 * gate_ref[:, cols].astype(F32))

    for j in range(T):

        @pl.when(j != me)
        def _():
            remote(tot_buf.at[j], tot_buf.at[j], tot_ssem.at[j], tot_rsem.at[j], at(partner)).wait_recv()

    rows = [tot_buf[partner][0:1]]
    chips = [tot_buf[2 * q][0:1] + tot_buf[2 * q + 1][0:1] for q in range(M)]
    for source in range(M - 1):
        sum_f = jnp.zeros((1, 2 * HEADS), F32)
        sum_b = jnp.zeros((1, 2 * HEADS), F32)
        for q in range(source + 1, M):
            sum_f = sum_f + jnp.where(q < place, chips[q], 0.0)
            sum_b = sum_b + jnp.where(q < place, chips[M - 1 - q], 0.0)
        rows.append(jnp.where(forward, sum_f, sum_b))
    padding = -len(rows) % 16
    rows = jnp.exp(jnp.concatenate(rows + [jnp.zeros((padding, 2 * HEADS), F32)], axis=0))
    we_dw[...] = split_bf16(jnp.where(own_dir, rows, 0.0))

    def ein_copy(g):
        return remote(esnd.at[g], ein.at[g], ein_ssem.at[g], ein_rsem.at[g], at(partner))

    def enter(g):
        factors = dot(we_dw[...], spread(g, own_direction))
        entering = keep.at[g]
        entering[...] = jnp.zeros((STATE, GROUP), F32)
        for source in range(M - 1):

            @pl.when(source < place)
            def _():
                recv_chip(g, source).wait_recv()
                entering[...] += factors[source + 1 : source + 2] * crecv[source, g].astype(F32)

        value = entering[...]
        esnd[g] = value.astype(BF16)
        ein_copy(g).start()
        eown[g] = (value * factors[0:1] + pin[g].astype(F32)).astype(BF16)

    slot = lax.rem(me, per)

    def out_copy(step, j):
        return remote(
            outs.at[step * T + j], mid.at[step * T + me],
            out_ssem.at[step * T + j], out_rsem.at[step * T + me], at(j),
        )

    def forward_copy(step, i):
        n = step * T + rec * per + lax.rem(i, per)
        return remote(
            mid.at[step * T + i], landing.at[n], fwd_ssem.at[step * T + i], fwd_rsem.at[n],
            at(me, i // per),
        )

    def pass_on(g):
        for piece in range(SPAN):
            step, i = g // lap, lax.rem(g, lap) * SPAN + piece
            n = step * T + i

            @pl.when(i != me)
            def _():
                remote(outs.at[n], mid.at[n], out_ssem.at[n], out_rsem.at[n], at(partner)).wait_recv()

            @pl.when(i // per == rec)
            def _():
                landing[n] = mid[n]

            @pl.when(i // per != rec)
            def _():
                forward_copy(step, i).start()

    for load in loads[len(small) :]:
        load.wait()

    def last(g):
        cols = cols_of(g)
        ein_copy(g).wait_recv()
        own, other = eown[g], ein[g]
        enter_f = jnp.where(forward, own, other)
        enter_b = jnp.where(forward, other, own)
        y = yloc[:, cols] + dec_f[:, cols] * dot(c_f, enter_f) + dec_b[:, cols] * dot(c_b, enter_b)
        gated = y * sgate[:, cols]
        squares = acc[...]
        for piece in range(SPAN):
            step, j = g // lap, lax.rem(g, lap) * SPAN + piece
            part = gated[:, piece * PIECE : (piece + 1) * PIECE]
            squares = squares + part * part
            outs[step * T + j] = part.astype(BF16)

            @pl.when(j == me)
            def _():
                mid[step * T + j] = outs[step * T + j]

            @pl.when(j != me)
            def _():
                out_copy(step, j).start()

        acc[...] = squares

    def turn(t, _):
        for stage, lag in (
            (first, 0), (combine, 1), (local, LAG_LOCAL), (enter, LAG_ENTER), (last, LAG_LAST),
            (pass_on, LAG_PASS),
        ):

            @pl.when(jnp.logical_and(t >= lag, t < N + lag))
            def _():
                stage(t - lag)

        return 0

    lax.fori_loop(0, N + LAG_LAST, turn, 0)
    mean = jnp.sum(acc[...].T, axis=0, keepdims=True) * (1.0 / INNER)
    inv_snd[...] = jnp.broadcast_to(lax.rsqrt(mean + EPSILON), (8, ROWS))

    def inv_copy(j):
        return remote(
            inv_snd, inv_buf.at[rec * per + slot], inv_ssem.at[j], inv_rsem.at[rec * per + slot],
            at(j, dest),
        )

    for j in range(T):
        mine = jnp.logical_and(own_dest, j == me)

        @pl.when(mine)
        def _():
            inv_buf[rec * per + slot] = inv_snd[...]

        @pl.when(jnp.logical_not(mine))
        def _():
            inv_copy(j).start()

    def rest(t, _):
        pass_on(t)
        return 0

    lax.fori_loop(N + LAG_LAST - LAG_PASS, N, rest, 0)

    gain = gain_ref[:, pl.ds(pl.multiple_of(me * CW, CW), CW)]

    for b in range(batch_count):
        for q in range(per):
            n = b * per + q
            mine = jnp.logical_and(b == rec, rec * per + q == me)

            @pl.when(jnp.logical_not(mine))
            def _():
                remote(inv_snd, inv_buf.at[n], inv_ssem.at[0], inv_rsem.at[n], at(partner)).wait_recv()

            scale = jnp.broadcast_to(inv_buf[n][0:1], (ROWS, ROWS)).T
            for step in range(CW // PIECE):
                k = step * T + n

                @pl.when(b != rec)
                def _():
                    remote(
                        mid.at[0], landing.at[k], fwd_ssem.at[0], fwd_rsem.at[k], at(partner)
                    ).wait_recv()

                inside = slice(step * PIECE, (step + 1) * PIECE)
                piece = landing[k].astype(F32) * scale * gain[:, inside]
                out_ref[b, q * ROWS : (q + 1) * ROWS, inside] = piece.astype(BF16)

    @pl.when(me < T - 1)
    def _():
        bc_right.wait_send()
        for g in range(lap):
            sig_right(g).wait_send()

    @pl.when(me > 0)
    def _():
        bc_left.wait_send()
        for g in range(lap):
            sig_left(g).wait_send()

    for j in range(T):

        @pl.when(j != me)
        def _():
            tot_copy(j).wait_send()

        @pl.when(jnp.logical_not(jnp.logical_and(own_dest, j == me)))
        def _():
            inv_copy(j).wait_send()

        for step in range(CW // PIECE):

            @pl.when(j != me)
            def _():
                out_copy(step, j).wait_send()

            @pl.when(j // per != rec)
            def _():
                forward_copy(step, j).wait_send()

    def sent(g, _):
        pin_copy(g).wait_send()
        ein_copy(g).wait_send()
        for target in range(1, M):

            @pl.when(place < target)
            def _():
                chip_copy(g, target).wait_send()

        return 0

    lax.fori_loop(0, N, sent, 0)


def shards(tm_count, batch_count, signal, gate_input, bc_forward, bc_backward, step_raw,
           decay_rate, conv_weight, conv_bias, skip_gain, norm_gain):
    T, M = tm_count, tm_count // 2
    CW = INNER // T
    per = T // batch_count
    N, lap, pieces = INNER // GROUP, T // SPAN, INNER // PIECE
    vmem = pltpu.VMEM
    dma = pltpu.SemaphoreType.DMA
    args = (signal[0], gate_input[0], bc_forward[0], bc_backward[0], step_raw[0],
            decay_rate, conv_weight, conv_bias, skip_gain, norm_gain.reshape(1, INNER))
    scratch = [vmem(a.shape, a.dtype) for a in args] + [
        vmem((RIM, INNER), BF16),
        vmem((RIM, INNER), BF16),
        vmem((RIM, 2 * STATE), BF16),
        vmem((RIM, 2 * STATE), BF16),
        vmem((T, 8, ROWS), F32),
        vmem((SPAN, ROWS + 16, PIECE), F32),
        vmem((ROWS + 16, 2 * STATE), F32),
        vmem((2 * ROWS, INNER), BF16),
        vmem((2 * HEADS, ROWS), F32),
        vmem((ROWS, 2 * HEADS), F32),
        vmem((2 * ROWS + 16, 4 * HEADS), BF16),
        vmem((-(-M // 16) * 16, 4 * HEADS), BF16),
        vmem((N, 8, GROUP), F32),
        vmem((ROWS, INNER), F32),
        vmem((ROWS, INNER), F32),
        vmem((ROWS, INNER), F32),
        vmem((ROWS, PIECE), F32),
        vmem((2, N, 4 * HEADS, GROUP), BF16),
        vmem((N, STATE, GROUP), F32),
        vmem((N, STATE, GROUP), BF16),
        vmem((N, STATE, GROUP), BF16),
        vmem((N, STATE, GROUP), BF16),
        vmem((M, N, STATE, GROUP), BF16),
        vmem((N, STATE, GROUP), BF16),
        vmem((N, STATE, GROUP), BF16),
        vmem((N, STATE, GROUP), BF16),
        vmem((ROWS, INNER), F32),
        vmem((pieces, ROWS, PIECE), BF16),
        vmem((pieces, ROWS, PIECE), BF16),
        vmem((pieces, ROWS, PIECE), BF16),
        vmem((8, ROWS), F32),
        vmem((T, 8, ROWS), F32),
        dma((2,)),
        dma((2,)),
        dma((lap,)),
        dma((lap,)),
        dma((lap,)),
        dma((lap,)),
        dma((T,)),
        dma((T,)),
        dma((N,)),
        dma((N,)),
        dma((M, N)),
        dma((M, N)),
        dma((N,)),
        dma((N,)),
        dma((pieces,)),
        dma((pieces,)),
        dma((pieces,)),
        dma((pieces,)),
        dma((T,)),
        dma((T,)),
        dma((len(args),)),
    ]
    return pl.pallas_call(
        functools.partial(mixer_kernel, T, batch_count),
        out_shape=pltpu.VMEM((batch_count, per * ROWS, CW), BF16),
        in_specs=[pl.BlockSpec(memory_space=pltpu.HBM)] * len(args),
        out_specs=pl.BlockSpec(memory_space=pltpu.VMEM),
        scratch_shapes=scratch,
        compiler_params=pltpu.CompilerParams(
            collective_id=0, has_side_effects=True, vmem_limit_bytes=62 * 2**20
        ),
        cost_estimate=pl.CostEstimate(
            flops=10**9, bytes_accessed=8 * 2**20, transcendentals=4 * 10**6
        ),
    )(*args)


def solution(mesh):
    in_specs = (P("batch", "tm", None),) * 5 + (P(),) * 5
    return jax.shard_map(
        functools.partial(shards, mesh.shape["tm"], mesh.shape["batch"]),
        mesh=mesh, in_specs=in_specs, out_specs=P(None, "batch", "tm"), check_vma=False,
    )
```

```python
import functools

import jax
import jax.numpy as jnp
from jax import lax
from jax.experimental import pallas as pl
from jax.experimental.pallas import tpu as pltpu
from jax.sharding import PartitionSpec as P

INNER = 4096
HEADDIM = 64
STATE = 64
HEADS = 64
ROWS = 128
PIECE = 128
GROUP = 512
SPAN = GROUP // PIECE
LAG_LOCAL, LAG_ENTER, LAG_LAST, LAG_PASS = 2, 3, 4, 6
RIM = 16
EPSILON = 1e-05
MASKED = -1e30

F32 = jnp.float32
BF16 = jnp.bfloat16


def dot(a, b, **kwargs):
    return jnp.dot(a, b, preferred_element_type=F32, **kwargs)


def split_bf16(value):
    high = value.astype(BF16).astype(F32)
    return jnp.concatenate([high, value - high], axis=1).astype(BF16)


def half_silu(half):
    return half + half * jnp.tanh(half)


def mixer_kernel(
    tm_count,
    batch_count,
    sig_hbm,
    gate_hbm,
    bcf_hbm,
    bcb_hbm,
    step_hbm,
    rate_hbm,
    cw_hbm,
    cb_hbm,
    skip_hbm,
    gain_hbm,
    out_ref,
    sig_ref,
    gate_ref,
    bcf_ref,
    bcb_ref,
    step_ref,
    rate_ref,
    cw_ref,
    cb_ref,
    skip_ref,
    gain_ref,
    hl_sig,
    hr_sig,
    hl_bc,
    hr_bc,
    tot_buf,
    ext,
    ext_bc,
    xs,
    rt,
    roll_a,
    we,
    extra,
    dec_f,
    dec_b,
    sgate,
    acc,
    spread_ref,
    keep,
    snd,
    pin,
    csnd,
    crecv,
    esnd,
    ein,
    eown,
    yloc,
    outs,
    mid,
    landing,
    inv_snd,
    inv_buf,
    halo_ssem,
    halo_rsem,
    right_ssem,
    right_rsem,
    left_ssem,
    left_rsem,
    tot_ssem,
    tot_rsem,
    pin_ssem,
    pin_rsem,
    chip_ssem,
    chip_rsem,
    ein_ssem,
    ein_rsem,
    out_ssem,
    out_rsem,
    fwd_ssem,
    fwd_rsem,
    inv_ssem,
    inv_rsem,
    load_sem,
):
    T = tm_count
    M = T // 2
    CW = INNER // T
    HG = CW // HEADDIM
    N = INNER // GROUP
    lap = T // SPAN
    per = T // batch_count
    me = lax.axis_index("tm")
    rec = lax.axis_index("batch")
    core = lax.rem(me, 2)
    chip = me // 2
    forward = core == 1
    partner = me + 1 - 2 * core
    dest = me // per
    place = jnp.where(forward, chip, M - 1 - chip)

    def at(tm, batch=None):
        return {"tm": tm, "batch": rec if batch is None else batch}

    small = [(step_hbm, step_ref), (rate_hbm, rate_ref), (bcf_hbm, bcf_ref), (bcb_hbm, bcb_ref),
             (skip_hbm, skip_ref), (cb_hbm, cb_ref), (cw_hbm, cw_ref), (sig_hbm, sig_ref)]
    late = [(gate_hbm, gate_ref), (gain_hbm, gain_ref)]
    loads = [
        pltpu.make_async_copy(src, dst, load_sem.at[k]) for k, (src, dst) in enumerate(small + late)
    ]
    for load in loads:
        load.start()

    barrier = pltpu.get_barrier_semaphore()

    def greet(tm, batch):
        pl.semaphore_signal(
            barrier, inc=1, device_id={"tm": tm, "batch": batch},
            device_id_type=pl.DeviceIdType.MESH,
        )

    own_dest = dest == rec
    for j in range(T):

        @pl.when(j != me)
        def _():
            greet(j, rec)

        @pl.when(jnp.logical_or(j != me, jnp.logical_not(own_dest)))
        def _():
            greet(j, dest)

    for b in range(batch_count):
        for q in range(per):

            @pl.when(jnp.logical_or(b != rec, rec * per + q != me))
            def _():
                greet(rec * per + q, b)

    for b in range(batch_count):

        @pl.when(b != rec)
        def _():
            greet(me, b)


    def remote(src, dst, ssem, rsem, device):
        return pltpu.make_async_remote_copy(
            src_ref=src, dst_ref=dst, send_sem=ssem, recv_sem=rsem,
            device_id=device, device_id_type=pl.DeviceIdType.MESH,
        )

    spot = lax.broadcasted_iota(jnp.int32, (2 * HEADS, GROUP), 1)
    offset = (lax.broadcasted_iota(jnp.int32, (2 * HEADS, GROUP), 0) & (HEADS - 1)) - (
        (spot >> 7) * HG + ((spot >> 6) & 1)
    )

    def head_of(g):
        return lax.rem(g, lap) * SPAN * HG + 2 * (g // lap)

    def lay_out(g, _):
        spread_ref[g] = jnp.where(offset == head_of(g), 1.0, 0.0).astype(BF16)
        return 0

    lax.fori_loop(0, N, lay_out, 0)

    for load in loads[: len(small)]:
        load.wait()
    raw = step_ref[...].astype(F32)
    step = jnp.maximum(raw, 0.0) + jnp.log1p(jnp.exp(-jnp.abs(raw)))
    rate = jnp.concatenate([rate_ref[0:1, :], rate_ref[1:2, :]], axis=1)
    log_decay = -step * rate
    row = lax.broadcasted_iota(jnp.int32, (ROWS, ROWS), 0)
    col = lax.broadcasted_iota(jnp.int32, (ROWS, ROWS), 1)
    lower = row >= col
    upper = row <= col
    fwd_lane = col < HEADS
    high = lax.Precision.HIGHEST
    cum = jnp.where(
        fwd_lane,
        dot(lower.astype(F32), log_decay, precision=high),
        dot(upper.astype(F32), log_decay, precision=high),
    )
    total = jnp.where(fwd_lane[0:1], cum[ROWS - 1 : ROWS], cum[0:1])
    tot_buf[me] = jnp.broadcast_to(total, (8, ROWS))

    def tot_copy(j):
        return remote(tot_buf.at[me], tot_buf.at[me], tot_ssem.at[j], tot_rsem.at[me], at(j))

    at_end, entered = jnp.exp(total - cum) * step, jnp.exp(cum)
    we[0:ROWS] = split_bf16(at_end[:, :HEADS])
    we[ROWS : 2 * ROWS] = split_bf16(entered[:, :HEADS])
    we[2 * ROWS : 3 * ROWS] = split_bf16(at_end[:, HEADS:])
    we[3 * ROWS : 4 * ROWS] = split_bf16(entered[:, HEADS:])
    rt[...] = (jnp.log(step) - cum).T
    roll_a[...] = cum
    acc[...] = jnp.zeros_like(acc)

    def own_heads(value):
        return jnp.where(forward, value[:, :HEADS], value[:, HEADS:])

    def wide(k):
        return pl.ds(pl.multiple_of(k * SPAN * CW, SPAN * CW), SPAN * CW)

    bc_right = remote(
        bcf_hbm.at[pl.ds(ROWS - RIM, RIM)], hl_bc, halo_ssem.at[0], halo_rsem.at[0], at(me + 1)
    )
    bc_left = remote(bcb_hbm.at[pl.ds(0, RIM)], hr_bc, halo_ssem.at[1], halo_rsem.at[1], at(me - 1))

    def sig_right(g):
        return remote(
            sig_hbm.at[pl.ds(ROWS - RIM, RIM), wide(g)], hl_sig.at[:, wide(g)],
            right_ssem.at[g], right_rsem.at[g], at(me + 1),
        )

    def sig_left(g):
        return remote(
            sig_hbm.at[pl.ds(0, RIM), wide(g)], hr_sig.at[:, wide(g)],
            left_ssem.at[g], left_rsem.at[g], at(me - 1),
        )

    pl.semaphore_wait(barrier, (T - 1) + 2 * (T - jnp.where(own_dest, 1, 0)) + batch_count - 1)

    @pl.when(me < T - 1)
    def _():
        bc_right.start()
        sig_right(0).start()

    @pl.when(me > 0)
    def _():
        bc_left.start()
        sig_left(0).start()

    for g in range(1, lap):

        @pl.when(me < T - 1)
        def _():
            sig_right(g).start()

        @pl.when(me > 0)
        def _():
            sig_left(g).start()

    for j in range(T):

        @pl.when(j != me)
        def _():
            tot_copy(j).start()

    @pl.when(me == 0)
    def _():
        hl_sig[...] = jnp.zeros_like(hl_sig)
        hl_bc[...] = jnp.zeros_like(hl_bc)

    @pl.when(me == T - 1)
    def _():
        hr_sig[...] = jnp.zeros_like(hr_sig)
        hr_bc[...] = jnp.zeros_like(hr_bc)

    @pl.when(me > 0)
    def _():
        bc_right.wait_recv()

    @pl.when(me < T - 1)
    def _():
        bc_left.wait_recv()

    def conv(buf, direction, cols):
        half = 0.5 * cb_ref[direction : direction + 1, cols]
        for k in range(4):
            start = 5 + k if direction == 0 else 11 - k
            tap = 0.5 * cw_ref[direction, k : k + 1, cols]
            half = half + tap * buf[start : start + ROWS, :]
        return half_silu(half).astype(BF16)

    bc_cols = slice(INNER, INNER + 2 * STATE)
    ext_bc[0:8] = hl_bc[...].astype(F32)[8:16]
    ext_bc[8 : 8 + ROWS] = bcf_ref[...].astype(F32)
    bc_f = conv(ext_bc, 0, bc_cols)
    ext_bc[8 : 8 + ROWS] = bcb_ref[...].astype(F32)
    ext_bc[8 + ROWS : 16 + ROWS] = hr_bc[...].astype(F32)[0:8]
    bc_b = conv(ext_bc, 1, bc_cols)
    bt_f = bc_f.astype(F32).T[:STATE].astype(BF16)
    bt_b = bc_b.astype(F32).T[:STATE].astype(BF16)
    c_f = bc_f[:, STATE:]
    c_b = bc_b[:, STATE:]
    scores_f = dot(c_f, bt_f)
    scores_b = dot(c_b, bt_b)
    bias_f = jnp.where(lower, 0.0, MASKED)
    bias_b = jnp.where(upper, 0.0, MASKED)

    for j in range(T):

        @pl.when(j != me)
        def _():
            remote(tot_buf.at[j], tot_buf.at[j], tot_ssem.at[j], tot_rsem.at[j], at(partner)).wait_recv()

    rows = [total, tot_buf[partner][0:1]]
    chips = [tot_buf[2 * q][0:1] + tot_buf[2 * q + 1][0:1] for q in range(M)]
    for source in range(M - 1):
        sum_f = jnp.zeros((1, 2 * HEADS), F32)
        sum_b = jnp.zeros((1, 2 * HEADS), F32)
        for q in range(source + 1, M):
            sum_f = sum_f + jnp.where(q < place, chips[q], 0.0)
            sum_b = sum_b + jnp.where(q < place, chips[M - 1 - q], 0.0)
        rows.append(jnp.where(forward, sum_f, sum_b))
    rows = jnp.exp(own_heads(jnp.concatenate(rows, axis=0)))
    rows = jnp.concatenate([skip_ref[...], rows], axis=0)
    padding = jnp.zeros((we.shape[0] - 4 * ROWS - rows.shape[0], HEADS), F32)
    we[4 * ROWS :] = split_bf16(jnp.concatenate([rows, padding], axis=0))

    def pin_copy(g):
        return remote(snd.at[g], pin.at[g], pin_ssem.at[g], pin_rsem.at[g], at(partner))

    def chip_copy(g, target):
        tm = jnp.where(forward, 2 * target + 1, 2 * (M - 1 - target))
        return remote(
            csnd.at[g], crecv.at[place, g], chip_ssem.at[target, g], chip_rsem.at[place, g], at(tm)
        )

    def recv_chip(g, source):
        return remote(
            csnd.at[g], crecv.at[source, g], chip_ssem.at[source, g], chip_rsem.at[source, g], at(partner)
        )

    def place_of(g, piece):
        start = (lax.rem(g, lap) * SPAN + piece) * CW + (g // lap) * PIECE
        return (
            pl.ds(pl.multiple_of(start, PIECE), PIECE),
            pl.ds(pl.multiple_of(g * GROUP + piece * PIECE, PIECE), PIECE),
        )

    def cols_of(g):
        return pl.ds(pl.multiple_of(g * GROUP, GROUP), GROUP)

    def first(g):
        @pl.when(jnp.logical_and(me > 0, g < lap))
        def _():
            sig_right(g).wait_recv()

        @pl.when(jnp.logical_and(me < T - 1, g < lap))
        def _():
            sig_left(g).wait_recv()

        for piece in range(SPAN):
            cols, inside = place_of(g, piece)
            buf = ext.at[piece]
            buf[0:8] = hl_sig[:, cols].astype(F32)[8:16]
            buf[8 : 8 + ROWS] = sig_ref[:, cols].astype(F32)
            buf[8 + ROWS : 16 + ROWS] = hr_sig[:, cols].astype(F32)[0:8]
            xs[0:ROWS, inside] = conv(buf, 0, cols)
            xs[ROWS : 2 * ROWS, inside] = conv(buf, 1, cols)
        cols = cols_of(g)
        by = dot(we[...], spread_ref[g])
        x_f, x_b = xs[0:ROWS, cols].astype(F32), xs[ROWS : 2 * ROWS, cols].astype(F32)
        state_f = dot(bt_f, (x_f * by[0:ROWS]).astype(BF16))
        state_b = dot(bt_b, (x_b * by[2 * ROWS : 3 * ROWS]).astype(BF16))
        snd[g] = jnp.where(forward, state_b, state_f).astype(BF16)
        pin_copy(g).start()
        keep[g] = jnp.where(forward, state_f, state_b)
        dec_f[:, cols] = by[ROWS : 2 * ROWS]
        dec_b[:, cols] = by[3 * ROWS : 4 * ROWS]
        extra[g] = by[4 * ROWS :]

    def combine(g):
        pin_copy(g).wait_recv()
        csnd[g] = (pin[g].astype(F32) * extra[g, 2:3] + keep[g]).astype(BF16)
        for target in range(1, M):

            @pl.when(place < target)
            def _():
                chip_copy(g, target).start()

    lane = lax.broadcasted_iota(jnp.int32, (ROWS, 2 * HEADDIM), 1)

    def local(g):
        rolled = pltpu.roll(roll_a[...], lax.rem(2 * HEADS - head_of(g), 2 * HEADS), 1)
        skips = extra[g, 0:2]

        def mixing(h):
            a_f = rolled[:, h : h + 1]
            a_b = rolled[:, HEADS + h : HEADS + h + 1]
            r_f = rt[pl.ds(head_of(g) + h, 1), :]
            r_b = rt[pl.ds(HEADS + head_of(g) + h, 1), :]
            mix_f = (scores_f * jnp.exp((a_f + r_f) + bias_f)).astype(BF16)
            mix_b = (scores_b * jnp.exp((a_b + r_b) + bias_b)).astype(BF16)
            return jnp.concatenate([mix_f, mix_b], axis=1)

        for piece in range(SPAN):
            cols, inside = place_of(g, piece)
            x_pair = xs[:, inside]
            head = piece * HG
            stacked = jnp.concatenate([mixing(head), mixing(head + 1)], axis=0)
            both = dot(stacked, x_pair)
            out = jnp.where(lane < HEADDIM, both[:ROWS], both[ROWS:])
            part = slice(piece * PIECE, (piece + 1) * PIECE)
            out = out + skips[0:1, part] * x_pair[:ROWS].astype(F32)
            out = out + skips[1:2, part] * x_pair[ROWS:].astype(F32)
            yloc[:, inside] = out
            sgate[:, inside] = half_silu(0.5 * gate_ref[:, cols].astype(F32))

    def ein_copy(g):
        return remote(esnd.at[g], ein.at[g], ein_ssem.at[g], ein_rsem.at[g], at(partner))

    def enter(g):
        factors = extra[g, 3 : 3 + M]
        entering = keep.at[g]
        entering[...] = jnp.zeros((STATE, GROUP), F32)
        for source in range(M - 1):

            @pl.when(source < place)
            def _():
                recv_chip(g, source).wait_recv()
                entering[...] += factors[source + 1 : source + 2] * crecv[source, g].astype(F32)

        value = entering[...]
        esnd[g] = value.astype(BF16)
        ein_copy(g).start()
        eown[g] = (value * factors[0:1] + pin[g].astype(F32)).astype(BF16)

    slot = lax.rem(me, per)

    def out_copy(step, j):
        return remote(
            outs.at[step * T + j], mid.at[step * T + me],
            out_ssem.at[step * T + j], out_rsem.at[step * T + me], at(j),
        )

    def forward_copy(step, i):
        n = step * T + rec * per + lax.rem(i, per)
        return remote(
            mid.at[step * T + i], landing.at[n], fwd_ssem.at[step * T + i], fwd_rsem.at[n],
            at(me, i // per),
        )

    def pass_on(g):
        for piece in range(SPAN):
            step, i = g // lap, lax.rem(g, lap) * SPAN + piece
            n = step * T + i

            @pl.when(i != me)
            def _():
                remote(outs.at[n], mid.at[n], out_ssem.at[n], out_rsem.at[n], at(partner)).wait_recv()

            @pl.when(i // per == rec)
            def _():
                landing[n] = mid[n]

            @pl.when(i // per != rec)
            def _():
                forward_copy(step, i).start()

    for load in loads[len(small) :]:
        load.wait()

    def last(g):
        cols = cols_of(g)
        ein_copy(g).wait_recv()
        own, other = eown[g], ein[g]
        enter_f = jnp.where(forward, own, other)
        enter_b = jnp.where(forward, other, own)
        y = yloc[:, cols] + dec_f[:, cols] * dot(c_f, enter_f) + dec_b[:, cols] * dot(c_b, enter_b)
        gated = y * sgate[:, cols]
        squares = acc[...]
        for piece in range(SPAN):
            step, j = g // lap, lax.rem(g, lap) * SPAN + piece
            part = gated[:, piece * PIECE : (piece + 1) * PIECE]
            squares = squares + part * part
            outs[step * T + j] = part.astype(BF16)

            @pl.when(j == me)
            def _():
                mid[step * T + j] = outs[step * T + j]

            @pl.when(j != me)
            def _():
                out_copy(step, j).start()

        acc[...] = squares

    def turn(t, _):
        for stage, lag in (
            (first, 0), (combine, 1), (local, LAG_LOCAL), (enter, LAG_ENTER), (last, LAG_LAST),
            (pass_on, LAG_PASS),
        ):

            @pl.when(jnp.logical_and(t >= lag, t < N + lag))
            def _():
                stage(t - lag)

        return 0

    lax.fori_loop(0, N + LAG_LAST, turn, 0)
    mean = jnp.sum(acc[...].T, axis=0, keepdims=True) * (1.0 / INNER)
    inv_snd[...] = jnp.broadcast_to(lax.rsqrt(mean + EPSILON), (8, ROWS))

    def inv_copy(j):
        return remote(
            inv_snd, inv_buf.at[rec * per + slot], inv_ssem.at[j], inv_rsem.at[rec * per + slot],
            at(j, dest),
        )

    for j in range(T):
        mine = jnp.logical_and(own_dest, j == me)

        @pl.when(mine)
        def _():
            inv_buf[rec * per + slot] = inv_snd[...]

        @pl.when(jnp.logical_not(mine))
        def _():
            inv_copy(j).start()

    def rest(t, _):
        pass_on(t)
        return 0

    lax.fori_loop(N + LAG_LAST - LAG_PASS, N, rest, 0)

    gain = gain_ref[:, pl.ds(pl.multiple_of(me * CW, CW), CW)]

    for b in range(batch_count):
        for q in range(per):
            n = b * per + q
            mine = jnp.logical_and(b == rec, rec * per + q == me)

            @pl.when(jnp.logical_not(mine))
            def _():
                remote(inv_snd, inv_buf.at[n], inv_ssem.at[0], inv_rsem.at[n], at(partner)).wait_recv()

            scale = jnp.broadcast_to(inv_buf[n][0:1], (ROWS, ROWS)).T
            for step in range(CW // PIECE):
                k = step * T + n

                @pl.when(b != rec)
                def _():
                    remote(
                        mid.at[0], landing.at[k], fwd_ssem.at[0], fwd_rsem.at[k], at(partner)
                    ).wait_recv()

                inside = slice(step * PIECE, (step + 1) * PIECE)
                piece = landing[k].astype(F32) * scale * gain[:, inside]
                out_ref[b, q * ROWS : (q + 1) * ROWS, inside] = piece.astype(BF16)

    @pl.when(me < T - 1)
    def _():
        bc_right.wait_send()
        for g in range(lap):
            sig_right(g).wait_send()

    @pl.when(me > 0)
    def _():
        bc_left.wait_send()
        for g in range(lap):
            sig_left(g).wait_send()

    for j in range(T):

        @pl.when(j != me)
        def _():
            tot_copy(j).wait_send()

        @pl.when(jnp.logical_not(jnp.logical_and(own_dest, j == me)))
        def _():
            inv_copy(j).wait_send()

        for step in range(CW // PIECE):

            @pl.when(j != me)
            def _():
                out_copy(step, j).wait_send()

            @pl.when(j // per != rec)
            def _():
                forward_copy(step, j).wait_send()

    def sent(g, _):
        pin_copy(g).wait_send()
        ein_copy(g).wait_send()
        for target in range(1, M):

            @pl.when(place < target)
            def _():
                chip_copy(g, target).wait_send()

        return 0

    lax.fori_loop(0, N, sent, 0)


def shards(tm_count, batch_count, signal, gate_input, bc_forward, bc_backward, step_raw,
           decay_rate, conv_weight, conv_bias, skip_gain, norm_gain):
    T, M = tm_count, tm_count // 2
    CW = INNER // T
    per = T // batch_count
    N, lap, pieces = INNER // GROUP, T // SPAN, INNER // PIECE
    few = -(-(M + 3) // 16) * 16
    vmem = pltpu.VMEM
    dma = pltpu.SemaphoreType.DMA
    args = (signal[0], gate_input[0], bc_forward[0], bc_backward[0], step_raw[0],
            decay_rate, conv_weight, conv_bias, skip_gain, norm_gain.reshape(1, INNER))
    scratch = [vmem(a.shape, a.dtype) for a in args] + [
        vmem((RIM, INNER), BF16),
        vmem((RIM, INNER), BF16),
        vmem((RIM, 2 * STATE), BF16),
        vmem((RIM, 2 * STATE), BF16),
        vmem((T, 8, ROWS), F32),
        vmem((SPAN, ROWS + 16, PIECE), F32),
        vmem((ROWS + 16, 2 * STATE), F32),
        vmem((2 * ROWS, INNER), BF16),
        vmem((2 * HEADS, ROWS), F32),
        vmem((ROWS, 2 * HEADS), F32),
        vmem((4 * ROWS + few, 2 * HEADS), BF16),
        vmem((N, few, GROUP), F32),
        vmem((ROWS, INNER), F32),
        vmem((ROWS, INNER), F32),
        vmem((ROWS, INNER), F32),
        vmem((ROWS, PIECE), F32),
        vmem((N, 2 * HEADS, GROUP), BF16),
        vmem((N, STATE, GROUP), F32),
        vmem((N, STATE, GROUP), BF16),
        vmem((N, STATE, GROUP), BF16),
        vmem((N, STATE, GROUP), BF16),
        vmem((M, N, STATE, GROUP), BF16),
        vmem((N, STATE, GROUP), BF16),
        vmem((N, STATE, GROUP), BF16),
        vmem((N, STATE, GROUP), BF16),
        vmem((ROWS, INNER), F32),
        vmem((pieces, ROWS, PIECE), BF16),
        vmem((pieces, ROWS, PIECE), BF16),
        vmem((pieces, ROWS, PIECE), BF16),
        vmem((8, ROWS), F32),
        vmem((T, 8, ROWS), F32),
        dma((2,)),
        dma((2,)),
        dma((lap,)),
        dma((lap,)),
        dma((lap,)),
        dma((lap,)),
        dma((T,)),
        dma((T,)),
        dma((N,)),
        dma((N,)),
        dma((M, N)),
        dma((M, N)),
        dma((N,)),
        dma((N,)),
        dma((pieces,)),
        dma((pieces,)),
        dma((pieces,)),
        dma((pieces,)),
        dma((T,)),
        dma((T,)),
        dma((len(args),)),
    ]
    return pl.pallas_call(
        functools.partial(mixer_kernel, T, batch_count),
        out_shape=pltpu.VMEM((batch_count, per * ROWS, CW), BF16),
        in_specs=[pl.BlockSpec(memory_space=pltpu.HBM)] * len(args),
        out_specs=pl.BlockSpec(memory_space=pltpu.VMEM),
        scratch_shapes=scratch,
        compiler_params=pltpu.CompilerParams(
            collective_id=0, has_side_effects=True, vmem_limit_bytes=62 * 2**20
        ),
        cost_estimate=pl.CostEstimate(
            flops=10**9, bytes_accessed=8 * 2**20, transcendentals=4 * 10**6
        ),
    )(*args)


def solution(mesh):
    in_specs = (P("batch", "tm", None),) * 5 + (P(),) * 5
    return jax.shard_map(
        functools.partial(shards, mesh.shape["tm"], mesh.shape["batch"]),
        mesh=mesh, in_specs=in_specs, out_specs=P(None, "batch", "tm"), check_vma=False,
    )
```

```python
import functools

import jax
import jax.numpy as jnp
from jax import lax
from jax.experimental import pallas as pl
from jax.experimental.pallas import tpu as pltpu
from jax.sharding import PartitionSpec as P

INNER = 4096
HEADDIM = 64
STATE = 64
HEADS = 64
ROWS = 128
PIECE = 128
GROUP = 512
SPAN = GROUP // PIECE
LAG_COMBINE, LAG_ENTER, LAG_LOCAL, LAG_LAST, LAG_PASS = 2, 4, 3, 6, 8
RIM = 16
EPSILON = 1e-05
MASKED = -1e30

F32 = jnp.float32
BF16 = jnp.bfloat16


def dot(a, b, **kwargs):
    return jnp.dot(a, b, preferred_element_type=F32, **kwargs)


def split_bf16(value):
    high = value.astype(BF16).astype(F32)
    return jnp.concatenate([high, value - high], axis=1).astype(BF16)


def half_silu(half):
    return half + half * jnp.tanh(half)


def mixer_kernel(
    tm_count,
    batch_count,
    sig_hbm,
    gate_hbm,
    bcf_hbm,
    bcb_hbm,
    step_hbm,
    rate_hbm,
    cw_hbm,
    cb_hbm,
    skip_hbm,
    gain_hbm,
    out_ref,
    sig_ref,
    gate_ref,
    bcf_ref,
    bcb_ref,
    step_ref,
    rate_ref,
    cw_ref,
    cb_ref,
    skip_ref,
    gain_ref,
    hl_sig,
    hr_sig,
    hl_bc,
    hr_bc,
    tot_buf,
    ext,
    ext_bc,
    xs,
    rt,
    roll_a,
    we,
    extra,
    dec_f,
    dec_b,
    sgate,
    acc,
    spread_ref,
    keep,
    snd,
    pin,
    csnd,
    crecv,
    esnd,
    ein,
    eown,
    yloc,
    outs,
    mid,
    landing,
    inv_snd,
    inv_buf,
    halo_ssem,
    halo_rsem,
    right_ssem,
    right_rsem,
    left_ssem,
    left_rsem,
    tot_ssem,
    tot_rsem,
    pin_ssem,
    pin_rsem,
    chip_ssem,
    chip_rsem,
    ein_ssem,
    ein_rsem,
    out_ssem,
    out_rsem,
    fwd_ssem,
    fwd_rsem,
    inv_ssem,
    inv_rsem,
    load_sem,
):
    T = tm_count
    M = T // 2
    CW = INNER // T
    HG = CW // HEADDIM
    N = INNER // GROUP
    lap = T // SPAN
    per = T // batch_count
    me = lax.axis_index("tm")
    rec = lax.axis_index("batch")
    core = lax.rem(me, 2)
    chip = me // 2
    forward = core == 1
    partner = me + 1 - 2 * core
    dest = me // per
    place = jnp.where(forward, chip, M - 1 - chip)

    def at(tm, batch=None):
        return {"tm": tm, "batch": rec if batch is None else batch}

    small = [(step_hbm, step_ref), (rate_hbm, rate_ref), (bcf_hbm, bcf_ref), (bcb_hbm, bcb_ref),
             (skip_hbm, skip_ref), (cb_hbm, cb_ref), (cw_hbm, cw_ref), (sig_hbm, sig_ref)]
    late = [(gate_hbm, gate_ref), (gain_hbm, gain_ref)]
    loads = [
        pltpu.make_async_copy(src, dst, load_sem.at[k]) for k, (src, dst) in enumerate(small + late)
    ]
    for load in loads:
        load.start()

    barrier = pltpu.get_barrier_semaphore()

    def greet(tm, batch):
        pl.semaphore_signal(
            barrier, inc=1, device_id={"tm": tm, "batch": batch},
            device_id_type=pl.DeviceIdType.MESH,
        )

    own_dest = dest == rec
    for j in range(T):

        @pl.when(j != me)
        def _():
            greet(j, rec)

        @pl.when(jnp.logical_or(j != me, jnp.logical_not(own_dest)))
        def _():
            greet(j, dest)

    for b in range(batch_count):
        for q in range(per):

            @pl.when(jnp.logical_or(b != rec, rec * per + q != me))
            def _():
                greet(rec * per + q, b)

    for b in range(batch_count):

        @pl.when(b != rec)
        def _():
            greet(me, b)


    def remote(src, dst, ssem, rsem, device):
        return pltpu.make_async_remote_copy(
            src_ref=src, dst_ref=dst, send_sem=ssem, recv_sem=rsem,
            device_id=device, device_id_type=pl.DeviceIdType.MESH,
        )

    spot = lax.broadcasted_iota(jnp.int32, (2 * HEADS, GROUP), 1)
    offset = (lax.broadcasted_iota(jnp.int32, (2 * HEADS, GROUP), 0) & (HEADS - 1)) - (
        (spot >> 7) * HG + ((spot >> 6) & 1)
    )

    def head_of(g):
        return lax.rem(g, lap) * SPAN * HG + 2 * (g // lap)

    def lay_out(g, _):
        spread_ref[g] = jnp.where(offset == head_of(g), 1.0, 0.0).astype(BF16)
        return 0

    lax.fori_loop(0, N, lay_out, 0)

    def wide(k):
        return pl.ds(pl.multiple_of(k * SPAN * CW, SPAN * CW), SPAN * CW)

    bc_right = remote(
        bcf_hbm.at[pl.ds(ROWS - RIM, RIM)], hl_bc, halo_ssem.at[0], halo_rsem.at[0], at(me + 1)
    )
    bc_left = remote(bcb_hbm.at[pl.ds(0, RIM)], hr_bc, halo_ssem.at[1], halo_rsem.at[1], at(me - 1))

    def sig_right(g):
        return remote(
            sig_hbm.at[pl.ds(ROWS - RIM, RIM), wide(g)], hl_sig.at[:, wide(g)],
            right_ssem.at[g], right_rsem.at[g], at(me + 1),
        )

    def sig_left(g):
        return remote(
            sig_hbm.at[pl.ds(0, RIM), wide(g)], hr_sig.at[:, wide(g)],
            left_ssem.at[g], left_rsem.at[g], at(me - 1),
        )

    pl.semaphore_wait(barrier, (T - 1) + 2 * (T - jnp.where(own_dest, 1, 0)) + batch_count - 1)

    @pl.when(me < T - 1)
    def _():
        bc_right.start()
        sig_right(0).start()

    @pl.when(me > 0)
    def _():
        bc_left.start()
        sig_left(0).start()

    for g in range(1, lap):

        @pl.when(me < T - 1)
        def _():
            sig_right(g).start()

        @pl.when(me > 0)
        def _():
            sig_left(g).start()

    for load in loads[: len(small)]:
        load.wait()
    raw = step_ref[...].astype(F32)
    step = jnp.maximum(raw, 0.0) + jnp.log1p(jnp.exp(-jnp.abs(raw)))
    rate = jnp.concatenate([rate_ref[0:1, :], rate_ref[1:2, :]], axis=1)
    log_decay = -step * rate
    row = lax.broadcasted_iota(jnp.int32, (ROWS, ROWS), 0)
    col = lax.broadcasted_iota(jnp.int32, (ROWS, ROWS), 1)
    lower = row >= col
    upper = row <= col
    fwd_lane = col < HEADS
    high = lax.Precision.HIGHEST
    cum = jnp.where(
        fwd_lane,
        dot(lower.astype(F32), log_decay, precision=high),
        dot(upper.astype(F32), log_decay, precision=high),
    )
    total = jnp.where(fwd_lane[0:1], cum[ROWS - 1 : ROWS], cum[0:1])
    tot_buf[me] = jnp.broadcast_to(total, (8, ROWS))

    def tot_copy(j):
        return remote(tot_buf.at[me], tot_buf.at[me], tot_ssem.at[j], tot_rsem.at[me], at(j))

    at_end, entered = jnp.exp(total - cum) * step, jnp.exp(cum)
    we[0:ROWS] = split_bf16(at_end[:, :HEADS])
    we[ROWS : 2 * ROWS] = split_bf16(entered[:, :HEADS])
    we[2 * ROWS : 3 * ROWS] = split_bf16(at_end[:, HEADS:])
    we[3 * ROWS : 4 * ROWS] = split_bf16(entered[:, HEADS:])
    rt[...] = (jnp.log(step) - cum).T
    roll_a[...] = cum
    acc[...] = jnp.zeros_like(acc)

    def own_heads(value):
        return jnp.where(forward, value[:, :HEADS], value[:, HEADS:])

    for j in range(T):

        @pl.when(j != me)
        def _():
            tot_copy(j).start()

    @pl.when(me == 0)
    def _():
        hl_sig[...] = jnp.zeros_like(hl_sig)
        hl_bc[...] = jnp.zeros_like(hl_bc)

    @pl.when(me == T - 1)
    def _():
        hr_sig[...] = jnp.zeros_like(hr_sig)
        hr_bc[...] = jnp.zeros_like(hr_bc)

    @pl.when(me > 0)
    def _():
        bc_right.wait_recv()

    @pl.when(me < T - 1)
    def _():
        bc_left.wait_recv()

    def conv(buf, direction, cols):
        half = 0.5 * cb_ref[direction : direction + 1, cols]
        for k in range(4):
            start = 5 + k if direction == 0 else 11 - k
            tap = 0.5 * cw_ref[direction, k : k + 1, cols]
            half = half + tap * buf[start : start + ROWS, :]
        return half_silu(half).astype(BF16)

    bc_cols = slice(INNER, INNER + 2 * STATE)
    ext_bc[0:8] = hl_bc[...].astype(F32)[8:16]
    ext_bc[8 : 8 + ROWS] = bcf_ref[...].astype(F32)
    bc_f = conv(ext_bc, 0, bc_cols)
    ext_bc[8 : 8 + ROWS] = bcb_ref[...].astype(F32)
    ext_bc[8 + ROWS : 16 + ROWS] = hr_bc[...].astype(F32)[0:8]
    bc_b = conv(ext_bc, 1, bc_cols)
    bt_f = bc_f.astype(F32).T[:STATE].astype(BF16)
    bt_b = bc_b.astype(F32).T[:STATE].astype(BF16)
    c_f = bc_f[:, STATE:]
    c_b = bc_b[:, STATE:]
    scores_f = dot(c_f, bt_f)
    scores_b = dot(c_b, bt_b)
    bias_f = jnp.where(lower, 0.0, MASKED)
    bias_b = jnp.where(upper, 0.0, MASKED)

    for j in range(T):

        @pl.when(j != me)
        def _():
            remote(tot_buf.at[j], tot_buf.at[j], tot_ssem.at[j], tot_rsem.at[j], at(partner)).wait_recv()

    rows = [total, tot_buf[partner][0:1]]
    chips = [tot_buf[2 * q][0:1] + tot_buf[2 * q + 1][0:1] for q in range(M)]
    for source in range(M - 1):
        sum_f = jnp.zeros((1, 2 * HEADS), F32)
        sum_b = jnp.zeros((1, 2 * HEADS), F32)
        for q in range(source + 1, M):
            sum_f = sum_f + jnp.where(q < place, chips[q], 0.0)
            sum_b = sum_b + jnp.where(q < place, chips[M - 1 - q], 0.0)
        rows.append(jnp.where(forward, sum_f, sum_b))
    rows = jnp.exp(own_heads(jnp.concatenate(rows, axis=0)))
    rows = jnp.concatenate([skip_ref[...], rows], axis=0)
    padding = jnp.zeros((we.shape[0] - 4 * ROWS - rows.shape[0], HEADS), F32)
    we[4 * ROWS :] = split_bf16(jnp.concatenate([rows, padding], axis=0))

    def pin_copy(g):
        return remote(snd.at[g], pin.at[g], pin_ssem.at[g], pin_rsem.at[g], at(partner))

    def chip_copy(g, target):
        tm = jnp.where(forward, 2 * target + 1, 2 * (M - 1 - target))
        return remote(
            csnd.at[g], crecv.at[place, g], chip_ssem.at[target, g], chip_rsem.at[place, g], at(tm)
        )

    def recv_chip(g, source):
        return remote(
            csnd.at[g], crecv.at[source, g], chip_ssem.at[source, g], chip_rsem.at[source, g], at(partner)
        )

    def place_of(g, piece):
        start = (lax.rem(g, lap) * SPAN + piece) * CW + (g // lap) * PIECE
        return (
            pl.ds(pl.multiple_of(start, PIECE), PIECE),
            pl.ds(pl.multiple_of(g * GROUP + piece * PIECE, PIECE), PIECE),
        )

    def cols_of(g):
        return pl.ds(pl.multiple_of(g * GROUP, GROUP), GROUP)

    def first(g):
        @pl.when(jnp.logical_and(me > 0, g < lap))
        def _():
            sig_right(g).wait_recv()

        @pl.when(jnp.logical_and(me < T - 1, g < lap))
        def _():
            sig_left(g).wait_recv()

        for piece in range(SPAN):
            cols, inside = place_of(g, piece)
            buf = ext.at[piece]
            buf[0:8] = hl_sig[:, cols].astype(F32)[8:16]
            buf[8 : 8 + ROWS] = sig_ref[:, cols].astype(F32)
            buf[8 + ROWS : 16 + ROWS] = hr_sig[:, cols].astype(F32)[0:8]
            xs[0:ROWS, inside] = conv(buf, 0, cols)
            xs[ROWS : 2 * ROWS, inside] = conv(buf, 1, cols)
        cols = cols_of(g)
        by = dot(we[...], spread_ref[g])
        x_f, x_b = xs[0:ROWS, cols].astype(F32), xs[ROWS : 2 * ROWS, cols].astype(F32)
        state_f = dot(bt_f, (x_f * by[0:ROWS]).astype(BF16))
        state_b = dot(bt_b, (x_b * by[2 * ROWS : 3 * ROWS]).astype(BF16))
        snd[g] = jnp.where(forward, state_b, state_f).astype(BF16)
        pin_copy(g).start()
        keep[g] = jnp.where(forward, state_f, state_b)
        dec_f[:, cols] = by[ROWS : 2 * ROWS]
        dec_b[:, cols] = by[3 * ROWS : 4 * ROWS]
        extra[g] = by[4 * ROWS :]

    def combine(g):
        pin_copy(g).wait_recv()
        csnd[g] = (pin[g].astype(F32) * extra[g, 2:3] + keep[g]).astype(BF16)
        for target in range(1, M):

            @pl.when(place < target)
            def _():
                chip_copy(g, target).start()

    lane = lax.broadcasted_iota(jnp.int32, (ROWS, 2 * HEADDIM), 1)

    def local(g):
        rolled = pltpu.roll(roll_a[...], lax.rem(2 * HEADS - head_of(g), 2 * HEADS), 1)
        skips = extra[g, 0:2]

        def mixing(h):
            a_f = rolled[:, h : h + 1]
            a_b = rolled[:, HEADS + h : HEADS + h + 1]
            r_f = rt[pl.ds(head_of(g) + h, 1), :]
            r_b = rt[pl.ds(HEADS + head_of(g) + h, 1), :]
            mix_f = (scores_f * jnp.exp((a_f + r_f) + bias_f)).astype(BF16)
            mix_b = (scores_b * jnp.exp((a_b + r_b) + bias_b)).astype(BF16)
            return jnp.concatenate([mix_f, mix_b], axis=1)

        for piece in range(SPAN):
            cols, inside = place_of(g, piece)
            x_pair = xs[:, inside]
            head = piece * HG
            stacked = jnp.concatenate([mixing(head), mixing(head + 1)], axis=0)
            both = dot(stacked, x_pair)
            out = jnp.where(lane < HEADDIM, both[:ROWS], both[ROWS:])
            part = slice(piece * PIECE, (piece + 1) * PIECE)
            out = out + skips[0:1, part] * x_pair[:ROWS].astype(F32)
            out = out + skips[1:2, part] * x_pair[ROWS:].astype(F32)
            yloc[:, inside] = out
            sgate[:, inside] = half_silu(0.5 * gate_ref[:, cols].astype(F32))

    def ein_copy(g):
        return remote(esnd.at[g], ein.at[g], ein_ssem.at[g], ein_rsem.at[g], at(partner))

    def enter(g):
        factors = extra[g, 3 : 3 + M]
        entering = keep.at[g]
        entering[...] = jnp.zeros((STATE, GROUP), F32)
        for source in range(M - 1):

            @pl.when(source < place)
            def _():
                recv_chip(g, source).wait_recv()
                entering[...] += factors[source + 1 : source + 2] * crecv[source, g].astype(F32)

        value = entering[...]
        esnd[g] = value.astype(BF16)
        ein_copy(g).start()
        eown[g] = (value * factors[0:1] + pin[g].astype(F32)).astype(BF16)

    slot = lax.rem(me, per)

    def out_copy(step, j):
        return remote(
            outs.at[step * T + j], mid.at[step * T + me],
            out_ssem.at[step * T + j], out_rsem.at[step * T + me], at(j),
        )

    def forward_copy(step, i):
        n = step * T + rec * per + lax.rem(i, per)
        return remote(
            mid.at[step * T + i], landing.at[n], fwd_ssem.at[step * T + i], fwd_rsem.at[n],
            at(me, i // per),
        )

    def pass_on(g):
        for piece in range(SPAN):
            step, i = g // lap, lax.rem(g, lap) * SPAN + piece
            n = step * T + i

            @pl.when(i != me)
            def _():
                remote(outs.at[n], mid.at[n], out_ssem.at[n], out_rsem.at[n], at(partner)).wait_recv()

            @pl.when(i // per == rec)
            def _():
                landing[n] = mid[n]

            @pl.when(i // per != rec)
            def _():
                forward_copy(step, i).start()

    for load in loads[len(small) :]:
        load.wait()

    def last(g):
        cols = cols_of(g)
        ein_copy(g).wait_recv()
        own, other = eown[g], ein[g]
        enter_f = jnp.where(forward, own, other)
        enter_b = jnp.where(forward, other, own)
        y = yloc[:, cols] + dec_f[:, cols] * dot(c_f, enter_f) + dec_b[:, cols] * dot(c_b, enter_b)
        gated = y * sgate[:, cols]
        squares = acc[...]
        for piece in range(SPAN):
            step, j = g // lap, lax.rem(g, lap) * SPAN + piece
            part = gated[:, piece * PIECE : (piece + 1) * PIECE]
            squares = squares + part * part
            outs[step * T + j] = part.astype(BF16)

            @pl.when(j == me)
            def _():
                mid[step * T + j] = outs[step * T + j]

            @pl.when(j != me)
            def _():
                out_copy(step, j).start()

        acc[...] = squares

    def turn(t, _):
        for stage, lag in (
            (first, 0), (combine, LAG_COMBINE), (enter, LAG_ENTER), (local, LAG_LOCAL),
            (last, LAG_LAST), (pass_on, LAG_PASS),
        ):

            @pl.when(jnp.logical_and(t >= lag, t < N + lag))
            def _():
                stage(t - lag)

        return 0

    lax.fori_loop(0, N + LAG_LAST, turn, 0)
    mean = jnp.sum(acc[...].T, axis=0, keepdims=True) * (1.0 / INNER)
    inv_snd[...] = jnp.broadcast_to(lax.rsqrt(mean + EPSILON), (8, ROWS))

    def inv_copy(j):
        return remote(
            inv_snd, inv_buf.at[rec * per + slot], inv_ssem.at[j], inv_rsem.at[rec * per + slot],
            at(j, dest),
        )

    for j in range(T):
        mine = jnp.logical_and(own_dest, j == me)

        @pl.when(mine)
        def _():
            inv_buf[rec * per + slot] = inv_snd[...]

        @pl.when(jnp.logical_not(mine))
        def _():
            inv_copy(j).start()

    def rest(t, _):
        pass_on(t)
        return 0

    lax.fori_loop(N + LAG_LAST - LAG_PASS, N, rest, 0)

    gain = gain_ref[:, pl.ds(pl.multiple_of(me * CW, CW), CW)]

    for b in range(batch_count):
        for q in range(per):
            n = b * per + q
            mine = jnp.logical_and(b == rec, rec * per + q == me)

            @pl.when(jnp.logical_not(mine))
            def _():
                remote(inv_snd, inv_buf.at[n], inv_ssem.at[0], inv_rsem.at[n], at(partner)).wait_recv()

            scale = jnp.broadcast_to(inv_buf[n][0:1], (ROWS, ROWS)).T
            for step in range(CW // PIECE):
                k = step * T + n

                @pl.when(b != rec)
                def _():
                    remote(
                        mid.at[0], landing.at[k], fwd_ssem.at[0], fwd_rsem.at[k], at(partner)
                    ).wait_recv()

                inside = slice(step * PIECE, (step + 1) * PIECE)
                piece = landing[k].astype(F32) * scale * gain[:, inside]
                out_ref[b, q * ROWS : (q + 1) * ROWS, inside] = piece.astype(BF16)

    @pl.when(me < T - 1)
    def _():
        bc_right.wait_send()
        for g in range(lap):
            sig_right(g).wait_send()

    @pl.when(me > 0)
    def _():
        bc_left.wait_send()
        for g in range(lap):
            sig_left(g).wait_send()

    for j in range(T):

        @pl.when(j != me)
        def _():
            tot_copy(j).wait_send()

        @pl.when(jnp.logical_not(jnp.logical_and(own_dest, j == me)))
        def _():
            inv_copy(j).wait_send()

        for step in range(CW // PIECE):

            @pl.when(j != me)
            def _():
                out_copy(step, j).wait_send()

            @pl.when(j // per != rec)
            def _():
                forward_copy(step, j).wait_send()

    def sent(g, _):
        pin_copy(g).wait_send()
        ein_copy(g).wait_send()
        for target in range(1, M):

            @pl.when(place < target)
            def _():
                chip_copy(g, target).wait_send()

        return 0

    lax.fori_loop(0, N, sent, 0)


def shards(tm_count, batch_count, signal, gate_input, bc_forward, bc_backward, step_raw,
           decay_rate, conv_weight, conv_bias, skip_gain, norm_gain):
    T, M = tm_count, tm_count // 2
    CW = INNER // T
    per = T // batch_count
    N, lap, pieces = INNER // GROUP, T // SPAN, INNER // PIECE
    few = -(-(M + 3) // 16) * 16
    vmem = pltpu.VMEM
    dma = pltpu.SemaphoreType.DMA
    args = (signal[0], gate_input[0], bc_forward[0], bc_backward[0], step_raw[0],
            decay_rate, conv_weight, conv_bias, skip_gain, norm_gain.reshape(1, INNER))
    scratch = [vmem(a.shape, a.dtype) for a in args] + [
        vmem((RIM, INNER), BF16),
        vmem((RIM, INNER), BF16),
        vmem((RIM, 2 * STATE), BF16),
        vmem((RIM, 2 * STATE), BF16),
        vmem((T, 8, ROWS), F32),
        vmem((SPAN, ROWS + 16, PIECE), F32),
        vmem((ROWS + 16, 2 * STATE), F32),
        vmem((2 * ROWS, INNER), BF16),
        vmem((2 * HEADS, ROWS), F32),
        vmem((ROWS, 2 * HEADS), F32),
        vmem((4 * ROWS + few, 2 * HEADS), BF16),
        vmem((N, few, GROUP), F32),
        vmem((ROWS, INNER), F32),
        vmem((ROWS, INNER), F32),
        vmem((ROWS, INNER), F32),
        vmem((ROWS, PIECE), F32),
        vmem((N, 2 * HEADS, GROUP), BF16),
        vmem((N, STATE, GROUP), F32),
        vmem((N, STATE, GROUP), BF16),
        vmem((N, STATE, GROUP), BF16),
        vmem((N, STATE, GROUP), BF16),
        vmem((M, N, STATE, GROUP), BF16),
        vmem((N, STATE, GROUP), BF16),
        vmem((N, STATE, GROUP), BF16),
        vmem((N, STATE, GROUP), BF16),
        vmem((ROWS, INNER), F32),
        vmem((pieces, ROWS, PIECE), BF16),
        vmem((pieces, ROWS, PIECE), BF16),
        vmem((pieces, ROWS, PIECE), BF16),
        vmem((8, ROWS), F32),
        vmem((T, 8, ROWS), F32),
        dma((2,)),
        dma((2,)),
        dma((lap,)),
        dma((lap,)),
        dma((lap,)),
        dma((lap,)),
        dma((T,)),
        dma((T,)),
        dma((N,)),
        dma((N,)),
        dma((M, N)),
        dma((M, N)),
        dma((N,)),
        dma((N,)),
        dma((pieces,)),
        dma((pieces,)),
        dma((pieces,)),
        dma((pieces,)),
        dma((T,)),
        dma((T,)),
        dma((len(args),)),
    ]
    return pl.pallas_call(
        functools.partial(mixer_kernel, T, batch_count),
        out_shape=pltpu.VMEM((batch_count, per * ROWS, CW), BF16),
        in_specs=[pl.BlockSpec(memory_space=pltpu.HBM)] * len(args),
        out_specs=pl.BlockSpec(memory_space=pltpu.VMEM),
        scratch_shapes=scratch,
        compiler_params=pltpu.CompilerParams(
            collective_id=0, has_side_effects=True, vmem_limit_bytes=62 * 2**20
        ),
        cost_estimate=pl.CostEstimate(
            flops=10**9, bytes_accessed=8 * 2**20, transcendentals=4 * 10**6
        ),
    )(*args)


def solution(mesh):
    in_specs = (P("batch", "tm", None),) * 5 + (P(),) * 5
    return jax.shard_map(
        functools.partial(shards, mesh.shape["tm"], mesh.shape["batch"]),
        mesh=mesh, in_specs=in_specs, out_specs=P(None, "batch", "tm"), check_vma=False,
    )
```

```python
import functools

import jax
import jax.numpy as jnp
from jax import lax
from jax.experimental import pallas as pl
from jax.experimental.pallas import tpu as pltpu
from jax.sharding import PartitionSpec as P

INNER = 4096
HEADDIM = 64
STATE = 64
HEADS = 64
ROWS = 128
PIECE = 128
GROUP = 1024
SPAN = GROUP // PIECE
LAG_COMBINE, LAG_LOCAL, LAG_ENTER, LAG_LAST, LAG_PASS = 1, 2, 3, 4, 5
RIM = 16
EPSILON = 1e-05
MASKED = -1e30

F32 = jnp.float32
BF16 = jnp.bfloat16


def dot(a, b, **kwargs):
    return jnp.dot(a, b, preferred_element_type=F32, **kwargs)


def split_bf16(value):
    high = value.astype(BF16).astype(F32)
    return jnp.concatenate([high, value - high], axis=1).astype(BF16)


def half_silu(half):
    return half + half * jnp.tanh(half)


def mixer_kernel(
    tm_count,
    batch_count,
    sig_hbm,
    gate_hbm,
    bcf_hbm,
    bcb_hbm,
    step_hbm,
    rate_hbm,
    cw_hbm,
    cb_hbm,
    skip_hbm,
    gain_hbm,
    out_ref,
    sig_ref,
    gate_ref,
    bcf_ref,
    bcb_ref,
    step_ref,
    rate_ref,
    cw_ref,
    cb_ref,
    skip_ref,
    gain_ref,
    hl_sig,
    hr_sig,
    hl_bc,
    hr_bc,
    tot_buf,
    ext,
    ext_bc,
    xs,
    rt,
    roll_a,
    we,
    extra,
    dec_f,
    dec_b,
    sgate,
    acc,
    spread_ref,
    keep,
    snd,
    pin,
    csnd,
    crecv,
    esnd,
    ein,
    eown,
    yloc,
    outs,
    mid,
    landing,
    inv_snd,
    inv_buf,
    halo_ssem,
    halo_rsem,
    right_ssem,
    right_rsem,
    left_ssem,
    left_rsem,
    tot_ssem,
    tot_rsem,
    pin_ssem,
    pin_rsem,
    chip_ssem,
    chip_rsem,
    ein_ssem,
    ein_rsem,
    out_ssem,
    out_rsem,
    fwd_ssem,
    fwd_rsem,
    inv_ssem,
    inv_rsem,
    load_sem,
):
    T = tm_count
    M = T // 2
    CW = INNER // T
    HG = CW // HEADDIM
    N = INNER // GROUP
    lap = T // SPAN
    per = T // batch_count
    me = lax.axis_index("tm")
    rec = lax.axis_index("batch")
    core = lax.rem(me, 2)
    chip = me // 2
    forward = core == 1
    partner = me + 1 - 2 * core
    dest = me // per
    place = jnp.where(forward, chip, M - 1 - chip)

    def at(tm, batch=None):
        return {"tm": tm, "batch": rec if batch is None else batch}

    small = [(step_hbm, step_ref), (rate_hbm, rate_ref), (bcf_hbm, bcf_ref), (bcb_hbm, bcb_ref),
             (skip_hbm, skip_ref), (cb_hbm, cb_ref), (cw_hbm, cw_ref), (sig_hbm, sig_ref)]
    late = [(gate_hbm, gate_ref), (gain_hbm, gain_ref)]
    loads = [
        pltpu.make_async_copy(src, dst, load_sem.at[k]) for k, (src, dst) in enumerate(small + late)
    ]
    for load in loads:
        load.start()

    barrier = pltpu.get_barrier_semaphore()

    def greet(tm, batch):
        pl.semaphore_signal(
            barrier, inc=1, device_id={"tm": tm, "batch": batch},
            device_id_type=pl.DeviceIdType.MESH,
        )

    own_dest = dest == rec
    for j in range(T):

        @pl.when(j != me)
        def _():
            greet(j, rec)

        @pl.when(jnp.logical_or(j != me, jnp.logical_not(own_dest)))
        def _():
            greet(j, dest)

    for b in range(batch_count):
        for q in range(per):

            @pl.when(jnp.logical_or(b != rec, rec * per + q != me))
            def _():
                greet(rec * per + q, b)

    for b in range(batch_count):

        @pl.when(b != rec)
        def _():
            greet(me, b)


    def remote(src, dst, ssem, rsem, device):
        return pltpu.make_async_remote_copy(
            src_ref=src, dst_ref=dst, send_sem=ssem, recv_sem=rsem,
            device_id=device, device_id_type=pl.DeviceIdType.MESH,
        )

    spot = lax.broadcasted_iota(jnp.int32, (2 * HEADS, GROUP), 1)
    offset = (lax.broadcasted_iota(jnp.int32, (2 * HEADS, GROUP), 0) & (HEADS - 1)) - (
        (spot >> 7) * HG + ((spot >> 6) & 1)
    )

    def head_of(g):
        return lax.rem(g, lap) * SPAN * HG + 2 * (g // lap)

    def lay_out(g, _):
        spread_ref[g] = jnp.where(offset == head_of(g), 1.0, 0.0).astype(BF16)
        return 0

    lax.fori_loop(0, N, lay_out, 0)

    def wide(k):
        return pl.ds(pl.multiple_of(k * SPAN * CW, SPAN * CW), SPAN * CW)

    bc_right = remote(
        bcf_hbm.at[pl.ds(ROWS - RIM, RIM)], hl_bc, halo_ssem.at[0], halo_rsem.at[0], at(me + 1)
    )
    bc_left = remote(bcb_hbm.at[pl.ds(0, RIM)], hr_bc, halo_ssem.at[1], halo_rsem.at[1], at(me - 1))

    def sig_right(g):
        return remote(
            sig_hbm.at[pl.ds(ROWS - RIM, RIM), wide(g)], hl_sig.at[:, wide(g)],
            right_ssem.at[g], right_rsem.at[g], at(me + 1),
        )

    def sig_left(g):
        return remote(
            sig_hbm.at[pl.ds(0, RIM), wide(g)], hr_sig.at[:, wide(g)],
            left_ssem.at[g], left_rsem.at[g], at(me - 1),
        )

    pl.semaphore_wait(barrier, (T - 1) + 2 * (T - jnp.where(own_dest, 1, 0)) + batch_count - 1)

    @pl.when(me < T - 1)
    def _():
        bc_right.start()
        sig_right(0).start()

    @pl.when(me > 0)
    def _():
        bc_left.start()
        sig_left(0).start()

    for g in range(1, lap):

        @pl.when(me < T - 1)
        def _():
            sig_right(g).start()

        @pl.when(me > 0)
        def _():
            sig_left(g).start()

    for load in loads[: len(small)]:
        load.wait()
    raw = step_ref[...].astype(F32)
    step = jnp.maximum(raw, 0.0) + jnp.log1p(jnp.exp(-jnp.abs(raw)))
    rate = jnp.concatenate([rate_ref[0:1, :], rate_ref[1:2, :]], axis=1)
    log_decay = -step * rate
    row = lax.broadcasted_iota(jnp.int32, (ROWS, ROWS), 0)
    col = lax.broadcasted_iota(jnp.int32, (ROWS, ROWS), 1)
    lower = row >= col
    upper = row <= col
    fwd_lane = col < HEADS
    high = lax.Precision.HIGHEST
    cum = jnp.where(
        fwd_lane,
        dot(lower.astype(F32), log_decay, precision=high),
        dot(upper.astype(F32), log_decay, precision=high),
    )
    total = jnp.where(fwd_lane[0:1], cum[ROWS - 1 : ROWS], cum[0:1])
    tot_buf[me] = jnp.broadcast_to(total, (8, ROWS))

    def tot_copy(j):
        return remote(tot_buf.at[me], tot_buf.at[me], tot_ssem.at[j], tot_rsem.at[me], at(j))

    at_end, entered = jnp.exp(total - cum) * step, jnp.exp(cum)
    we[0:ROWS] = split_bf16(at_end[:, :HEADS])
    we[ROWS : 2 * ROWS] = split_bf16(entered[:, :HEADS])
    we[2 * ROWS : 3 * ROWS] = split_bf16(at_end[:, HEADS:])
    we[3 * ROWS : 4 * ROWS] = split_bf16(entered[:, HEADS:])
    rt[...] = (jnp.log(step) - cum).T
    roll_a[...] = cum
    acc[...] = jnp.zeros_like(acc)

    def own_heads(value):
        return jnp.where(forward, value[:, :HEADS], value[:, HEADS:])

    for j in range(T):

        @pl.when(j != me)
        def _():
            tot_copy(j).start()

    def place_of(g, piece):
        start = (lax.rem(g, lap) * SPAN + piece) * CW + (g // lap) * PIECE
        return (
            pl.ds(pl.multiple_of(start, PIECE), PIECE),
            pl.ds(pl.multiple_of(g * GROUP + piece * PIECE, PIECE), PIECE),
        )

    for load in loads[len(small) :]:
        load.wait()

    def gate_of(g, _):
        for piece in range(SPAN):
            cols, inside = place_of(g, piece)
            sgate[:, inside] = half_silu(0.5 * gate_ref[:, cols].astype(F32))
        return 0

    lax.fori_loop(0, N, gate_of, 0)

    @pl.when(me == 0)
    def _():
        hl_sig[...] = jnp.zeros_like(hl_sig)
        hl_bc[...] = jnp.zeros_like(hl_bc)

    @pl.when(me == T - 1)
    def _():
        hr_sig[...] = jnp.zeros_like(hr_sig)
        hr_bc[...] = jnp.zeros_like(hr_bc)

    @pl.when(me > 0)
    def _():
        bc_right.wait_recv()

    @pl.when(me < T - 1)
    def _():
        bc_left.wait_recv()

    def conv(buf, direction, cols):
        half = 0.5 * cb_ref[direction : direction + 1, cols]
        for k in range(4):
            start = 5 + k if direction == 0 else 11 - k
            tap = 0.5 * cw_ref[direction, k : k + 1, cols]
            half = half + tap * buf[start : start + ROWS, :]
        return half_silu(half).astype(BF16)

    bc_cols = slice(INNER, INNER + 2 * STATE)
    ext_bc[0:8] = hl_bc[...].astype(F32)[8:16]
    ext_bc[8 : 8 + ROWS] = bcf_ref[...].astype(F32)
    bc_f = conv(ext_bc, 0, bc_cols)
    ext_bc[8 : 8 + ROWS] = bcb_ref[...].astype(F32)
    ext_bc[8 + ROWS : 16 + ROWS] = hr_bc[...].astype(F32)[0:8]
    bc_b = conv(ext_bc, 1, bc_cols)
    bt_f = bc_f.astype(F32).T[:STATE].astype(BF16)
    bt_b = bc_b.astype(F32).T[:STATE].astype(BF16)
    c_f = bc_f[:, STATE:]
    c_b = bc_b[:, STATE:]
    scores_f = dot(c_f, bt_f)
    scores_b = dot(c_b, bt_b)
    bias_f = jnp.where(lower, 0.0, MASKED)
    bias_b = jnp.where(upper, 0.0, MASKED)

    for j in range(T):

        @pl.when(j != me)
        def _():
            remote(tot_buf.at[j], tot_buf.at[j], tot_ssem.at[j], tot_rsem.at[j], at(partner)).wait_recv()

    rows = [total, tot_buf[partner][0:1]]
    chips = [tot_buf[2 * q][0:1] + tot_buf[2 * q + 1][0:1] for q in range(M)]
    for source in range(M - 1):
        sum_f = jnp.zeros((1, 2 * HEADS), F32)
        sum_b = jnp.zeros((1, 2 * HEADS), F32)
        for q in range(source + 1, M):
            sum_f = sum_f + jnp.where(q < place, chips[q], 0.0)
            sum_b = sum_b + jnp.where(q < place, chips[M - 1 - q], 0.0)
        rows.append(jnp.where(forward, sum_f, sum_b))
    rows = jnp.exp(own_heads(jnp.concatenate(rows, axis=0)))
    rows = jnp.concatenate([skip_ref[...], rows], axis=0)
    padding = jnp.zeros((we.shape[0] - 4 * ROWS - rows.shape[0], HEADS), F32)
    we[4 * ROWS :] = split_bf16(jnp.concatenate([rows, padding], axis=0))

    def pin_copy(g):
        return remote(snd.at[g], pin.at[g], pin_ssem.at[g], pin_rsem.at[g], at(partner))

    def chip_copy(g, target):
        tm = jnp.where(forward, 2 * target + 1, 2 * (M - 1 - target))
        return remote(
            csnd.at[g], crecv.at[place, g], chip_ssem.at[target, g], chip_rsem.at[place, g], at(tm)
        )

    def recv_chip(g, source):
        return remote(
            csnd.at[g], crecv.at[source, g], chip_ssem.at[source, g], chip_rsem.at[source, g], at(partner)
        )

    def cols_of(g):
        return pl.ds(pl.multiple_of(g * GROUP, GROUP), GROUP)

    def first(g):
        @pl.when(jnp.logical_and(me > 0, g < lap))
        def _():
            sig_right(g).wait_recv()

        @pl.when(jnp.logical_and(me < T - 1, g < lap))
        def _():
            sig_left(g).wait_recv()

        for piece in range(SPAN):
            cols, inside = place_of(g, piece)
            buf = ext.at[piece]
            buf[0:8] = hl_sig[:, cols].astype(F32)[8:16]
            buf[8 : 8 + ROWS] = sig_ref[:, cols].astype(F32)
            buf[8 + ROWS : 16 + ROWS] = hr_sig[:, cols].astype(F32)[0:8]
            xs[0:ROWS, inside] = conv(buf, 0, cols)
            xs[ROWS : 2 * ROWS, inside] = conv(buf, 1, cols)
        cols = cols_of(g)
        by = dot(we[...], spread_ref[g])
        x_f, x_b = xs[0:ROWS, cols].astype(F32), xs[ROWS : 2 * ROWS, cols].astype(F32)
        state_f = dot(bt_f, (x_f * by[0:ROWS]).astype(BF16))
        state_b = dot(bt_b, (x_b * by[2 * ROWS : 3 * ROWS]).astype(BF16))
        snd[g] = jnp.where(forward, state_b, state_f).astype(BF16)
        pin_copy(g).start()
        keep[g] = jnp.where(forward, state_f, state_b)
        dec_f[:, cols] = by[ROWS : 2 * ROWS]
        dec_b[:, cols] = by[3 * ROWS : 4 * ROWS]
        extra[g] = by[4 * ROWS :]

    def combine(g):
        pin_copy(g).wait_recv()
        csnd[g] = (pin[g].astype(F32) * extra[g, 2:3] + keep[g]).astype(BF16)
        for target in range(1, M):

            @pl.when(place < target)
            def _():
                chip_copy(g, target).start()

    lane = lax.broadcasted_iota(jnp.int32, (ROWS, 2 * HEADDIM), 1)

    def local(g):
        rolled = pltpu.roll(roll_a[...], lax.rem(2 * HEADS - head_of(g), 2 * HEADS), 1)
        skips = extra[g, 0:2]

        def mixing(h):
            a_f = rolled[:, h : h + 1]
            a_b = rolled[:, HEADS + h : HEADS + h + 1]
            r_f = rt[pl.ds(head_of(g) + h, 1), :]
            r_b = rt[pl.ds(HEADS + head_of(g) + h, 1), :]
            mix_f = (scores_f * jnp.exp((a_f + r_f) + bias_f)).astype(BF16)
            mix_b = (scores_b * jnp.exp((a_b + r_b) + bias_b)).astype(BF16)
            return jnp.concatenate([mix_f, mix_b], axis=1)

        for piece in range(SPAN):
            _, inside = place_of(g, piece)
            x_pair = xs[:, inside]
            head = piece * HG
            stacked = jnp.concatenate([mixing(head), mixing(head + 1)], axis=0)
            both = dot(stacked, x_pair)
            out = jnp.where(lane < HEADDIM, both[:ROWS], both[ROWS:])
            part = slice(piece * PIECE, (piece + 1) * PIECE)
            out = out + skips[0:1, part] * x_pair[:ROWS].astype(F32)
            out = out + skips[1:2, part] * x_pair[ROWS:].astype(F32)
            yloc[:, inside] = out

    def ein_copy(g):
        return remote(esnd.at[g], ein.at[g], ein_ssem.at[g], ein_rsem.at[g], at(partner))

    def enter(g):
        factors = extra[g, 3 : 3 + M]
        entering = keep.at[g]
        entering[...] = jnp.zeros((STATE, GROUP), F32)
        for source in range(M - 1):

            @pl.when(source < place)
            def _():
                recv_chip(g, source).wait_recv()
                entering[...] += factors[source + 1 : source + 2] * crecv[source, g].astype(F32)

        value = entering[...]
        esnd[g] = value.astype(BF16)
        ein_copy(g).start()
        eown[g] = (value * factors[0:1] + pin[g].astype(F32)).astype(BF16)

    slot = lax.rem(me, per)

    def out_copy(step, j):
        return remote(
            outs.at[step * T + j], mid.at[step * T + me],
            out_ssem.at[step * T + j], out_rsem.at[step * T + me], at(j),
        )

    def forward_copy(step, i):
        n = step * T + rec * per + lax.rem(i, per)
        return remote(
            mid.at[step * T + i], landing.at[n], fwd_ssem.at[step * T + i], fwd_rsem.at[n],
            at(me, i // per),
        )

    def pass_on(g):
        for piece in range(SPAN):
            step, i = g // lap, lax.rem(g, lap) * SPAN + piece
            n = step * T + i

            @pl.when(i != me)
            def _():
                remote(outs.at[n], mid.at[n], out_ssem.at[n], out_rsem.at[n], at(partner)).wait_recv()

            @pl.when(i // per == rec)
            def _():
                landing[n] = mid[n]

            @pl.when(i // per != rec)
            def _():
                forward_copy(step, i).start()

    def last(g):
        cols = cols_of(g)
        ein_copy(g).wait_recv()
        own, other = eown[g], ein[g]
        enter_f = jnp.where(forward, own, other)
        enter_b = jnp.where(forward, other, own)
        y = yloc[:, cols] + dec_f[:, cols] * dot(c_f, enter_f) + dec_b[:, cols] * dot(c_b, enter_b)
        gated = y * sgate[:, cols]
        squares = acc[...]
        for piece in range(SPAN):
            step, j = g // lap, lax.rem(g, lap) * SPAN + piece
            part = gated[:, piece * PIECE : (piece + 1) * PIECE]
            squares = squares + part * part
            outs[step * T + j] = part.astype(BF16)

            @pl.when(j == me)
            def _():
                mid[step * T + j] = outs[step * T + j]

            @pl.when(j != me)
            def _():
                out_copy(step, j).start()

        acc[...] = squares

    def turn(t, _):
        for stage, lag in (
            (first, 0), (combine, LAG_COMBINE), (local, LAG_LOCAL), (enter, LAG_ENTER),
            (last, LAG_LAST), (pass_on, LAG_PASS),
        ):

            @pl.when(jnp.logical_and(t >= lag, t < N + lag))
            def _():
                stage(t - lag)

        return 0

    lax.fori_loop(0, N + LAG_LAST, turn, 0)
    mean = jnp.sum(acc[...].T, axis=0, keepdims=True) * (1.0 / INNER)
    inv_snd[...] = jnp.broadcast_to(lax.rsqrt(mean + EPSILON), (8, ROWS))

    def inv_copy(j):
        return remote(
            inv_snd, inv_buf.at[rec * per + slot], inv_ssem.at[j], inv_rsem.at[rec * per + slot],
            at(j, dest),
        )

    for j in range(T):
        mine = jnp.logical_and(own_dest, j == me)

        @pl.when(mine)
        def _():
            inv_buf[rec * per + slot] = inv_snd[...]

        @pl.when(jnp.logical_not(mine))
        def _():
            inv_copy(j).start()

    def rest(t, _):
        pass_on(t)
        return 0

    lax.fori_loop(N + LAG_LAST - LAG_PASS, N, rest, 0)

    gain = gain_ref[:, pl.ds(pl.multiple_of(me * CW, CW), CW)]

    for b in range(batch_count):
        for q in range(per):
            n = b * per + q
            mine = jnp.logical_and(b == rec, rec * per + q == me)

            @pl.when(jnp.logical_not(mine))
            def _():
                remote(inv_snd, inv_buf.at[n], inv_ssem.at[0], inv_rsem.at[n], at(partner)).wait_recv()

            scale = jnp.broadcast_to(inv_buf[n][0:1], (ROWS, ROWS)).T
            for step in range(CW // PIECE):
                k = step * T + n

                @pl.when(b != rec)
                def _():
                    remote(
                        mid.at[0], landing.at[k], fwd_ssem.at[0], fwd_rsem.at[k], at(partner)
                    ).wait_recv()

                inside = slice(step * PIECE, (step + 1) * PIECE)
                piece = landing[k].astype(F32) * scale * gain[:, inside]
                out_ref[b, q * ROWS : (q + 1) * ROWS, inside] = piece.astype(BF16)

    @pl.when(me < T - 1)
    def _():
        bc_right.wait_send()
        for g in range(lap):
            sig_right(g).wait_send()

    @pl.when(me > 0)
    def _():
        bc_left.wait_send()
        for g in range(lap):
            sig_left(g).wait_send()

    for j in range(T):

        @pl.when(j != me)
        def _():
            tot_copy(j).wait_send()

        @pl.when(jnp.logical_not(jnp.logical_and(own_dest, j == me)))
        def _():
            inv_copy(j).wait_send()

        for step in range(CW // PIECE):

            @pl.when(j != me)
            def _():
                out_copy(step, j).wait_send()

            @pl.when(j // per != rec)
            def _():
                forward_copy(step, j).wait_send()

    def sent(g, _):
        pin_copy(g).wait_send()
        ein_copy(g).wait_send()
        for target in range(1, M):

            @pl.when(place < target)
            def _():
                chip_copy(g, target).wait_send()

        return 0

    lax.fori_loop(0, N, sent, 0)


def shards(tm_count, batch_count, signal, gate_input, bc_forward, bc_backward, step_raw,
           decay_rate, conv_weight, conv_bias, skip_gain, norm_gain):
    T, M = tm_count, tm_count // 2
    CW = INNER // T
    per = T // batch_count
    N, lap, pieces = INNER // GROUP, T // SPAN, INNER // PIECE
    few = -(-(M + 3) // 16) * 16
    vmem = pltpu.VMEM
    dma = pltpu.SemaphoreType.DMA
    args = (signal[0], gate_input[0], bc_forward[0], bc_backward[0], step_raw[0],
            decay_rate, conv_weight, conv_bias, skip_gain, norm_gain.reshape(1, INNER))
    scratch = [vmem(a.shape, a.dtype) for a in args] + [
        vmem((RIM, INNER), BF16),
        vmem((RIM, INNER), BF16),
        vmem((RIM, 2 * STATE), BF16),
        vmem((RIM, 2 * STATE), BF16),
        vmem((T, 8, ROWS), F32),
        vmem((SPAN, ROWS + 16, PIECE), F32),
        vmem((ROWS + 16, 2 * STATE), F32),
        vmem((2 * ROWS, INNER), BF16),
        vmem((2 * HEADS, ROWS), F32),
        vmem((ROWS, 2 * HEADS), F32),
        vmem((4 * ROWS + few, 2 * HEADS), BF16),
        vmem((N, few, GROUP), F32),
        vmem((ROWS, INNER), F32),
        vmem((ROWS, INNER), F32),
        vmem((ROWS, INNER), F32),
        vmem((ROWS, PIECE), F32),
        vmem((N, 2 * HEADS, GROUP), BF16),
        vmem((N, STATE, GROUP), F32),
        vmem((N, STATE, GROUP), BF16),
        vmem((N, STATE, GROUP), BF16),
        vmem((N, STATE, GROUP), BF16),
        vmem((M, N, STATE, GROUP), BF16),
        vmem((N, STATE, GROUP), BF16),
        vmem((N, STATE, GROUP), BF16),
        vmem((N, STATE, GROUP), BF16),
        vmem((ROWS, INNER), F32),
        vmem((pieces, ROWS, PIECE), BF16),
        vmem((pieces, ROWS, PIECE), BF16),
        vmem((pieces, ROWS, PIECE), BF16),
        vmem((8, ROWS), F32),
        vmem((T, 8, ROWS), F32),
        dma((2,)),
        dma((2,)),
        dma((lap,)),
        dma((lap,)),
        dma((lap,)),
        dma((lap,)),
        dma((T,)),
        dma((T,)),
        dma((N,)),
        dma((N,)),
        dma((M, N)),
        dma((M, N)),
        dma((N,)),
        dma((N,)),
        dma((pieces,)),
        dma((pieces,)),
        dma((pieces,)),
        dma((pieces,)),
        dma((T,)),
        dma((T,)),
        dma((len(args),)),
    ]
    return pl.pallas_call(
        functools.partial(mixer_kernel, T, batch_count),
        out_shape=pltpu.VMEM((batch_count, per * ROWS, CW), BF16),
        in_specs=[pl.BlockSpec(memory_space=pltpu.HBM)] * len(args),
        out_specs=pl.BlockSpec(memory_space=pltpu.VMEM),
        scratch_shapes=scratch,
        compiler_params=pltpu.CompilerParams(
            collective_id=0, has_side_effects=True, vmem_limit_bytes=62 * 2**20
        ),
        cost_estimate=pl.CostEstimate(
            flops=10**9, bytes_accessed=8 * 2**20, transcendentals=4 * 10**6
        ),
    )(*args)


def solution(mesh):
    in_specs = (P("batch", "tm", None),) * 5 + (P(),) * 5
    return jax.shard_map(
        functools.partial(shards, mesh.shape["tm"], mesh.shape["batch"]),
        mesh=mesh, in_specs=in_specs, out_specs=P(None, "batch", "tm"), check_vma=False,
    )
```

```python
import functools

import jax
import jax.numpy as jnp
from jax import lax
from jax.experimental import pallas as pl
from jax.experimental.pallas import tpu as pltpu
from jax.sharding import PartitionSpec as P

INNER = 4096
HEADDIM = 64
STATE = 64
HEADS = 64
ROWS = 128
PIECE = 128
GROUP = 512
SPAN = GROUP // PIECE
LAG_COMBINE, LAG_LOCAL, LAG_ENTER, LAG_LAST, LAG_PASS = 1, 2, 3, 4, 6
RIM = 16
EPSILON = 1e-05
MASKED = -1e30

F32 = jnp.float32
BF16 = jnp.bfloat16


def dot(a, b, **kwargs):
    return jnp.dot(a, b, preferred_element_type=F32, **kwargs)


def split_bf16(value):
    high = value.astype(BF16).astype(F32)
    return jnp.concatenate([high, value - high], axis=1).astype(BF16)


def half_silu(half):
    return half + half * jnp.tanh(half)


def mixer_kernel(
    tm_count,
    batch_count,
    sig_hbm,
    gate_hbm,
    bcf_hbm,
    bcb_hbm,
    step_hbm,
    rate_hbm,
    cw_hbm,
    cb_hbm,
    skip_hbm,
    gain_hbm,
    out_ref,
    sig_ref,
    gate_ref,
    bcf_ref,
    bcb_ref,
    step_ref,
    rate_ref,
    cw_ref,
    cb_ref,
    skip_ref,
    gain_ref,
    hl_sig,
    hr_sig,
    hl_bc,
    hr_bc,
    tot_buf,
    ext,
    ext_bc,
    xs,
    rt,
    roll_a,
    we,
    extra,
    dec_f,
    dec_b,
    sgate,
    acc,
    spread_ref,
    keep,
    snd,
    pin,
    csnd,
    crecv,
    esnd,
    ein,
    eown,
    yloc,
    outs,
    mid,
    landing,
    inv_snd,
    inv_buf,
    halo_ssem,
    halo_rsem,
    right_ssem,
    right_rsem,
    left_ssem,
    left_rsem,
    tot_ssem,
    tot_rsem,
    pin_ssem,
    pin_rsem,
    chip_ssem,
    chip_rsem,
    ein_ssem,
    ein_rsem,
    out_ssem,
    out_rsem,
    fwd_ssem,
    fwd_rsem,
    inv_ssem,
    inv_rsem,
    load_sem,
):
    T = tm_count
    M = T // 2
    CW = INNER // T
    HG = CW // HEADDIM
    N = INNER // GROUP
    lap = T // SPAN
    per = T // batch_count
    me = lax.axis_index("tm")
    rec = lax.axis_index("batch")
    core = lax.rem(me, 2)
    chip = me // 2
    forward = core == 1
    partner = me + 1 - 2 * core
    dest = me // per
    place = jnp.where(forward, chip, M - 1 - chip)

    def at(tm, batch=None):
        return {"tm": tm, "batch": rec if batch is None else batch}

    small = [(step_hbm, step_ref), (rate_hbm, rate_ref), (bcf_hbm, bcf_ref), (bcb_hbm, bcb_ref),
             (skip_hbm, skip_ref), (cb_hbm, cb_ref), (cw_hbm, cw_ref), (sig_hbm, sig_ref)]
    late = [(gate_hbm, gate_ref), (gain_hbm, gain_ref)]
    loads = [
        pltpu.make_async_copy(src, dst, load_sem.at[k]) for k, (src, dst) in enumerate(small + late)
    ]
    for load in loads:
        load.start()

    barrier = pltpu.get_barrier_semaphore()

    def greet(tm, batch):
        pl.semaphore_signal(
            barrier, inc=1, device_id={"tm": tm, "batch": batch},
            device_id_type=pl.DeviceIdType.MESH,
        )

    own_dest = dest == rec
    for j in range(T):

        @pl.when(j != me)
        def _():
            greet(j, rec)

        @pl.when(jnp.logical_or(j != me, jnp.logical_not(own_dest)))
        def _():
            greet(j, dest)

    for b in range(batch_count):
        for q in range(per):

            @pl.when(jnp.logical_or(b != rec, rec * per + q != me))
            def _():
                greet(rec * per + q, b)

    for b in range(batch_count):

        @pl.when(b != rec)
        def _():
            greet(me, b)


    def remote(src, dst, ssem, rsem, device):
        return pltpu.make_async_remote_copy(
            src_ref=src, dst_ref=dst, send_sem=ssem, recv_sem=rsem,
            device_id=device, device_id_type=pl.DeviceIdType.MESH,
        )

    spot = lax.broadcasted_iota(jnp.int32, (2 * HEADS, GROUP), 1)
    offset = (lax.broadcasted_iota(jnp.int32, (2 * HEADS, GROUP), 0) & (HEADS - 1)) - (
        (spot >> 7) * HG + ((spot >> 6) & 1)
    )

    def head_of(g):
        return lax.rem(g, lap) * SPAN * HG + 2 * (g // lap)

    def lay_out(g, _):
        spread_ref[g] = jnp.where(offset == head_of(g), 1.0, 0.0).astype(BF16)
        return 0

    lax.fori_loop(0, N, lay_out, 0)

    def wide(k):
        return pl.ds(pl.multiple_of(k * SPAN * CW, SPAN * CW), SPAN * CW)

    bc_right = remote(
        bcf_hbm.at[pl.ds(ROWS - RIM, RIM)], hl_bc, halo_ssem.at[0], halo_rsem.at[0], at(me + 1)
    )
    bc_left = remote(bcb_hbm.at[pl.ds(0, RIM)], hr_bc, halo_ssem.at[1], halo_rsem.at[1], at(me - 1))

    def sig_right(g):
        return remote(
            sig_hbm.at[pl.ds(ROWS - RIM, RIM), wide(g)], hl_sig.at[:, wide(g)],
            right_ssem.at[g], right_rsem.at[g], at(me + 1),
        )

    def sig_left(g):
        return remote(
            sig_hbm.at[pl.ds(0, RIM), wide(g)], hr_sig.at[:, wide(g)],
            left_ssem.at[g], left_rsem.at[g], at(me - 1),
        )

    pl.semaphore_wait(barrier, (T - 1) + 2 * (T - jnp.where(own_dest, 1, 0)) + batch_count - 1)

    @pl.when(me < T - 1)
    def _():
        bc_right.start()
        sig_right(0).start()

    @pl.when(me > 0)
    def _():
        bc_left.start()
        sig_left(0).start()

    for g in range(1, lap):

        @pl.when(me < T - 1)
        def _():
            sig_right(g).start()

        @pl.when(me > 0)
        def _():
            sig_left(g).start()

    for load in loads[: len(small)]:
        load.wait()
    raw = step_ref[...].astype(F32)
    step = jnp.maximum(raw, 0.0) + jnp.log1p(jnp.exp(-jnp.abs(raw)))
    rate = jnp.concatenate([rate_ref[0:1, :], rate_ref[1:2, :]], axis=1)
    log_decay = -step * rate
    row = lax.broadcasted_iota(jnp.int32, (ROWS, ROWS), 0)
    col = lax.broadcasted_iota(jnp.int32, (ROWS, ROWS), 1)
    lower = row >= col
    upper = row <= col
    fwd_lane = col < HEADS
    high = lax.Precision.HIGHEST
    cum = jnp.where(
        fwd_lane,
        dot(lower.astype(F32), log_decay, precision=high),
        dot(upper.astype(F32), log_decay, precision=high),
    )
    total = jnp.where(fwd_lane[0:1], cum[ROWS - 1 : ROWS], cum[0:1])
    tot_buf[me] = jnp.broadcast_to(total, (8, ROWS))

    def tot_copy(j):
        return remote(tot_buf.at[me], tot_buf.at[me], tot_ssem.at[j], tot_rsem.at[me], at(j))

    at_end, entered = jnp.exp(total - cum) * step, jnp.exp(cum)
    we[0:ROWS] = split_bf16(at_end[:, :HEADS])
    we[ROWS : 2 * ROWS] = split_bf16(entered[:, :HEADS])
    we[2 * ROWS : 3 * ROWS] = split_bf16(at_end[:, HEADS:])
    we[3 * ROWS : 4 * ROWS] = split_bf16(entered[:, HEADS:])
    rt[...] = (jnp.log(step) - cum).T
    roll_a[...] = cum
    acc[...] = jnp.zeros_like(acc)

    def own_heads(value):
        return jnp.where(forward, value[:, :HEADS], value[:, HEADS:])

    for j in range(T):

        @pl.when(j != me)
        def _():
            tot_copy(j).start()

    def place_of(g, piece):
        start = (lax.rem(g, lap) * SPAN + piece) * CW + (g // lap) * PIECE
        return (
            pl.ds(pl.multiple_of(start, PIECE), PIECE),
            pl.ds(pl.multiple_of(g * GROUP + piece * PIECE, PIECE), PIECE),
        )

    for load in loads[len(small) :]:
        load.wait()

    def gate_of(g, _):
        for piece in range(SPAN):
            cols, inside = place_of(g, piece)
            sgate[:, inside] = half_silu(0.5 * gate_ref[:, cols].astype(F32))
        return 0

    lax.fori_loop(0, N, gate_of, 0)

    @pl.when(me == 0)
    def _():
        hl_sig[...] = jnp.zeros_like(hl_sig)
        hl_bc[...] = jnp.zeros_like(hl_bc)

    @pl.when(me == T - 1)
    def _():
        hr_sig[...] = jnp.zeros_like(hr_sig)
        hr_bc[...] = jnp.zeros_like(hr_bc)

    @pl.when(me > 0)
    def _():
        bc_right.wait_recv()

    @pl.when(me < T - 1)
    def _():
        bc_left.wait_recv()

    def conv(buf, direction, cols):
        half = 0.5 * cb_ref[direction : direction + 1, cols]
        for k in range(4):
            start = 5 + k if direction == 0 else 11 - k
            tap = 0.5 * cw_ref[direction, k : k + 1, cols]
            half = half + tap * buf[start : start + ROWS, :]
        return half_silu(half).astype(BF16)

    bc_cols = slice(INNER, INNER + 2 * STATE)
    ext_bc[0:8] = hl_bc[...].astype(F32)[8:16]
    ext_bc[8 : 8 + ROWS] = bcf_ref[...].astype(F32)
    bc_f = conv(ext_bc, 0, bc_cols)
    ext_bc[8 : 8 + ROWS] = bcb_ref[...].astype(F32)
    ext_bc[8 + ROWS : 16 + ROWS] = hr_bc[...].astype(F32)[0:8]
    bc_b = conv(ext_bc, 1, bc_cols)
    bt_f = bc_f.astype(F32).T[:STATE].astype(BF16)
    bt_b = bc_b.astype(F32).T[:STATE].astype(BF16)
    c_f = bc_f[:, STATE:]
    c_b = bc_b[:, STATE:]
    scores_f = dot(c_f, bt_f)
    scores_b = dot(c_b, bt_b)
    bias_f = jnp.where(lower, 0.0, MASKED)
    bias_b = jnp.where(upper, 0.0, MASKED)

    for j in range(T):

        @pl.when(j != me)
        def _():
            remote(tot_buf.at[j], tot_buf.at[j], tot_ssem.at[j], tot_rsem.at[j], at(partner)).wait_recv()

    rows = [total, tot_buf[partner][0:1]]
    chips = [tot_buf[2 * q][0:1] + tot_buf[2 * q + 1][0:1] for q in range(M)]
    for source in range(M - 1):
        sum_f = jnp.zeros((1, 2 * HEADS), F32)
        sum_b = jnp.zeros((1, 2 * HEADS), F32)
        for q in range(source + 1, M):
            sum_f = sum_f + jnp.where(q < place, chips[q], 0.0)
            sum_b = sum_b + jnp.where(q < place, chips[M - 1 - q], 0.0)
        rows.append(jnp.where(forward, sum_f, sum_b))
    rows = jnp.exp(own_heads(jnp.concatenate(rows, axis=0)))
    rows = jnp.concatenate([skip_ref[...], rows], axis=0)
    padding = jnp.zeros((we.shape[0] - 4 * ROWS - rows.shape[0], HEADS), F32)
    we[4 * ROWS :] = split_bf16(jnp.concatenate([rows, padding], axis=0))

    def pin_copy(g):
        return remote(snd.at[g], pin.at[g], pin_ssem.at[g], pin_rsem.at[g], at(partner))

    def chip_copy(g, target):
        tm = jnp.where(forward, 2 * target + 1, 2 * (M - 1 - target))
        return remote(
            csnd.at[g], crecv.at[place, g], chip_ssem.at[target, g], chip_rsem.at[place, g], at(tm)
        )

    def recv_chip(g, source):
        return remote(
            csnd.at[g], crecv.at[source, g], chip_ssem.at[source, g], chip_rsem.at[source, g], at(partner)
        )

    def cols_of(g):
        return pl.ds(pl.multiple_of(g * GROUP, GROUP), GROUP)

    def first(g):
        @pl.when(jnp.logical_and(me > 0, g < lap))
        def _():
            sig_right(g).wait_recv()

        @pl.when(jnp.logical_and(me < T - 1, g < lap))
        def _():
            sig_left(g).wait_recv()

        for piece in range(SPAN):
            cols, inside = place_of(g, piece)
            buf = ext.at[piece]
            buf[0:8] = hl_sig[:, cols].astype(F32)[8:16]
            buf[8 : 8 + ROWS] = sig_ref[:, cols].astype(F32)
            buf[8 + ROWS : 16 + ROWS] = hr_sig[:, cols].astype(F32)[0:8]
            xs[0:ROWS, inside] = conv(buf, 0, cols)
            xs[ROWS : 2 * ROWS, inside] = conv(buf, 1, cols)
        cols = cols_of(g)
        by = dot(we[...], spread_ref[g])
        x_f, x_b = xs[0:ROWS, cols].astype(F32), xs[ROWS : 2 * ROWS, cols].astype(F32)
        state_f = dot(bt_f, (x_f * by[0:ROWS]).astype(BF16))
        state_b = dot(bt_b, (x_b * by[2 * ROWS : 3 * ROWS]).astype(BF16))
        snd[g] = jnp.where(forward, state_b, state_f).astype(BF16)
        pin_copy(g).start()
        keep[g] = jnp.where(forward, state_f, state_b)
        dec_f[:, cols] = by[ROWS : 2 * ROWS]
        dec_b[:, cols] = by[3 * ROWS : 4 * ROWS]
        extra[g] = by[4 * ROWS :]

    def combine(g):
        pin_copy(g).wait_recv()
        csnd[g] = (pin[g].astype(F32) * extra[g, 2:3] + keep[g]).astype(BF16)
        for target in range(1, M):

            @pl.when(place < target)
            def _():
                chip_copy(g, target).start()

    lane = lax.broadcasted_iota(jnp.int32, (ROWS, 2 * HEADDIM), 1)

    def local(g):
        rolled = pltpu.roll(roll_a[...], lax.rem(2 * HEADS - head_of(g), 2 * HEADS), 1)
        skips = extra[g, 0:2]

        def mixing(h):
            a_f = rolled[:, h : h + 1]
            a_b = rolled[:, HEADS + h : HEADS + h + 1]
            r_f = rt[pl.ds(head_of(g) + h, 1), :]
            r_b = rt[pl.ds(HEADS + head_of(g) + h, 1), :]
            mix_f = (scores_f * jnp.exp((a_f + r_f) + bias_f)).astype(BF16)
            mix_b = (scores_b * jnp.exp((a_b + r_b) + bias_b)).astype(BF16)
            return jnp.concatenate([mix_f, mix_b], axis=1)

        for piece in range(SPAN):
            _, inside = place_of(g, piece)
            x_pair = xs[:, inside]
            head = piece * HG
            stacked = jnp.concatenate([mixing(head), mixing(head + 1)], axis=0)
            both = dot(stacked, x_pair)
            out = jnp.where(lane < HEADDIM, both[:ROWS], both[ROWS:])
            part = slice(piece * PIECE, (piece + 1) * PIECE)
            out = out + skips[0:1, part] * x_pair[:ROWS].astype(F32)
            out = out + skips[1:2, part] * x_pair[ROWS:].astype(F32)
            yloc[:, inside] = out

    def ein_copy(g):
        return remote(esnd.at[g], ein.at[g], ein_ssem.at[g], ein_rsem.at[g], at(partner))

    def enter(g):
        factors = extra[g, 3 : 3 + M]
        entering = keep.at[g]
        entering[...] = jnp.zeros((STATE, GROUP), F32)
        for source in range(M - 1):

            @pl.when(source < place)
            def _():
                recv_chip(g, source).wait_recv()
                entering[...] += factors[source + 1 : source + 2] * crecv[source, g].astype(F32)

        value = entering[...]
        esnd[g] = value.astype(BF16)
        ein_copy(g).start()
        eown[g] = (value * factors[0:1] + pin[g].astype(F32)).astype(BF16)

    slot = lax.rem(me, per)

    def out_copy(step, j):
        return remote(
            outs.at[step * T + j], mid.at[step * T + me],
            out_ssem.at[step * T + j], out_rsem.at[step * T + me], at(j),
        )

    def forward_copy(step, i):
        n = step * T + rec * per + lax.rem(i, per)
        return remote(
            mid.at[step * T + i], landing.at[n], fwd_ssem.at[step * T + i], fwd_rsem.at[n],
            at(me, i // per),
        )

    def pass_on(g):
        for piece in range(SPAN):
            step, i = g // lap, lax.rem(g, lap) * SPAN + piece
            n = step * T + i

            @pl.when(i != me)
            def _():
                remote(outs.at[n], mid.at[n], out_ssem.at[n], out_rsem.at[n], at(partner)).wait_recv()

            @pl.when(i // per == rec)
            def _():
                landing[n] = mid[n]

            @pl.when(i // per != rec)
            def _():
                forward_copy(step, i).start()

    def last(g):
        cols = cols_of(g)
        ein_copy(g).wait_recv()
        own, other = eown[g], ein[g]
        enter_f = jnp.where(forward, own, other)
        enter_b = jnp.where(forward, other, own)
        y = yloc[:, cols] + dec_f[:, cols] * dot(c_f, enter_f) + dec_b[:, cols] * dot(c_b, enter_b)
        gated = y * sgate[:, cols]
        squares = acc[...]
        for piece in range(SPAN):
            step, j = g // lap, lax.rem(g, lap) * SPAN + piece
            part = gated[:, piece * PIECE : (piece + 1) * PIECE]
            squares = squares + part * part
            outs[step * T + j] = part.astype(BF16)

            @pl.when(j == me)
            def _():
                mid[step * T + j] = outs[step * T + j]

            @pl.when(j != me)
            def _():
                out_copy(step, j).start()

        acc[...] = squares

    def turn(t, _):
        for stage, lag in (
            (first, 0), (combine, LAG_COMBINE), (local, LAG_LOCAL), (enter, LAG_ENTER),
            (last, LAG_LAST), (pass_on, LAG_PASS),
        ):

            @pl.when(jnp.logical_and(t >= lag, t < N + lag))
            def _():
                stage(t - lag)

        return 0

    lax.fori_loop(0, N + LAG_LAST, turn, 0)
    mean = jnp.sum(acc[...].T, axis=0, keepdims=True) * (1.0 / INNER)
    inv_snd[...] = jnp.broadcast_to(lax.rsqrt(mean + EPSILON), (8, ROWS))

    def inv_copy(j):
        return remote(
            inv_snd, inv_buf.at[rec * per + slot], inv_ssem.at[j], inv_rsem.at[rec * per + slot],
            at(j, dest),
        )

    for j in range(T):
        mine = jnp.logical_and(own_dest, j == me)

        @pl.when(mine)
        def _():
            inv_buf[rec * per + slot] = inv_snd[...]

        @pl.when(jnp.logical_not(mine))
        def _():
            inv_copy(j).start()

    def rest(t, _):
        pass_on(t)
        return 0

    lax.fori_loop(N + LAG_LAST - LAG_PASS, N, rest, 0)

    gain = gain_ref[:, pl.ds(pl.multiple_of(me * CW, CW), CW)]

    for b in range(batch_count):
        for q in range(per):
            n = b * per + q
            mine = jnp.logical_and(b == rec, rec * per + q == me)

            @pl.when(jnp.logical_not(mine))
            def _():
                remote(inv_snd, inv_buf.at[n], inv_ssem.at[0], inv_rsem.at[n], at(partner)).wait_recv()

            scale = jnp.broadcast_to(inv_buf[n][0:1], (ROWS, ROWS)).T
            for step in range(CW // PIECE):
                k = step * T + n

                @pl.when(b != rec)
                def _():
                    remote(
                        mid.at[0], landing.at[k], fwd_ssem.at[0], fwd_rsem.at[k], at(partner)
                    ).wait_recv()

                inside = slice(step * PIECE, (step + 1) * PIECE)
                piece = landing[k].astype(F32) * scale * gain[:, inside]
                out_ref[b, q * ROWS : (q + 1) * ROWS, inside] = piece.astype(BF16)

    @pl.when(me < T - 1)
    def _():
        bc_right.wait_send()
        for g in range(lap):
            sig_right(g).wait_send()

    @pl.when(me > 0)
    def _():
        bc_left.wait_send()
        for g in range(lap):
            sig_left(g).wait_send()

    for j in range(T):

        @pl.when(j != me)
        def _():
            tot_copy(j).wait_send()

        @pl.when(jnp.logical_not(jnp.logical_and(own_dest, j == me)))
        def _():
            inv_copy(j).wait_send()

        for step in range(CW // PIECE):

            @pl.when(j != me)
            def _():
                out_copy(step, j).wait_send()

            @pl.when(j // per != rec)
            def _():
                forward_copy(step, j).wait_send()

    def sent(g, _):
        pin_copy(g).wait_send()
        ein_copy(g).wait_send()
        for target in range(1, M):

            @pl.when(place < target)
            def _():
                chip_copy(g, target).wait_send()

        return 0

    lax.fori_loop(0, N, sent, 0)


def shards(tm_count, batch_count, signal, gate_input, bc_forward, bc_backward, step_raw,
           decay_rate, conv_weight, conv_bias, skip_gain, norm_gain):
    T, M = tm_count, tm_count // 2
    CW = INNER // T
    per = T // batch_count
    N, lap, pieces = INNER // GROUP, T // SPAN, INNER // PIECE
    few = -(-(M + 3) // 16) * 16
    vmem = pltpu.VMEM
    dma = pltpu.SemaphoreType.DMA
    args = (signal[0], gate_input[0], bc_forward[0], bc_backward[0], step_raw[0],
            decay_rate, conv_weight, conv_bias, skip_gain, norm_gain.reshape(1, INNER))
    scratch = [vmem(a.shape, a.dtype) for a in args] + [
        vmem((RIM, INNER), BF16),
        vmem((RIM, INNER), BF16),
        vmem((RIM, 2 * STATE), BF16),
        vmem((RIM, 2 * STATE), BF16),
        vmem((T, 8, ROWS), F32),
        vmem((SPAN, ROWS + 16, PIECE), F32),
        vmem((ROWS + 16, 2 * STATE), F32),
        vmem((2 * ROWS, INNER), BF16),
        vmem((2 * HEADS, ROWS), F32),
        vmem((ROWS, 2 * HEADS), F32),
        vmem((4 * ROWS + few, 2 * HEADS), BF16),
        vmem((N, few, GROUP), F32),
        vmem((ROWS, INNER), F32),
        vmem((ROWS, INNER), F32),
        vmem((ROWS, INNER), F32),
        vmem((ROWS, PIECE), F32),
        vmem((N, 2 * HEADS, GROUP), BF16),
        vmem((N, STATE, GROUP), F32),
        vmem((N, STATE, GROUP), BF16),
        vmem((N, STATE, GROUP), BF16),
        vmem((N, STATE, GROUP), BF16),
        vmem((M, N, STATE, GROUP), BF16),
        vmem((N, STATE, GROUP), BF16),
        vmem((N, STATE, GROUP), BF16),
        vmem((N, STATE, GROUP), BF16),
        vmem((ROWS, INNER), F32),
        vmem((pieces, ROWS, PIECE), BF16),
        vmem((pieces, ROWS, PIECE), BF16),
        vmem((pieces, ROWS, PIECE), BF16),
        vmem((8, ROWS), F32),
        vmem((T, 8, ROWS), F32),
        dma((2,)),
        dma((2,)),
        dma((lap,)),
        dma((lap,)),
        dma((lap,)),
        dma((lap,)),
        dma((T,)),
        dma((T,)),
        dma((N,)),
        dma((N,)),
        dma((M, N)),
        dma((M, N)),
        dma((N,)),
        dma((N,)),
        dma((pieces,)),
        dma((pieces,)),
        dma((pieces,)),
        dma((pieces,)),
        dma((T,)),
        dma((T,)),
        dma((len(args),)),
    ]
    return pl.pallas_call(
        functools.partial(mixer_kernel, T, batch_count),
        out_shape=pltpu.VMEM((batch_count, per * ROWS, CW), BF16),
        in_specs=[pl.BlockSpec(memory_space=pltpu.HBM)] * len(args),
        out_specs=pl.BlockSpec(memory_space=pltpu.VMEM),
        scratch_shapes=scratch,
        compiler_params=pltpu.CompilerParams(
            collective_id=0, has_side_effects=True, vmem_limit_bytes=62 * 2**20
        ),
        cost_estimate=pl.CostEstimate(
            flops=10**9, bytes_accessed=8 * 2**20, transcendentals=4 * 10**6
        ),
    )(*args)


def solution(mesh):
    in_specs = (P("batch", "tm", None),) * 5 + (P(),) * 5
    return jax.shard_map(
        functools.partial(shards, mesh.shape["tm"], mesh.shape["batch"]),
        mesh=mesh, in_specs=in_specs, out_specs=P(None, "batch", "tm"), check_vma=False,
    )
```

```python
import functools

import jax
import jax.numpy as jnp
from jax import lax
from jax.experimental import pallas as pl
from jax.experimental.pallas import tpu as pltpu
from jax.sharding import PartitionSpec as P

INNER = 4096
HEADDIM = 64
STATE = 64
HEADS = 64
ROWS = 128
PIECE = 128
GROUP = 512
SPAN = GROUP // PIECE
LAG_COMBINE, LAG_LOCAL, LAG_ENTER, LAG_LAST, LAG_PASS = 1, 2, 3, 4, 5
RIM = 16
EPSILON = 1e-05
MASKED = -1e30

F32 = jnp.float32
BF16 = jnp.bfloat16


def dot(a, b, **kwargs):
    return jnp.dot(a, b, preferred_element_type=F32, **kwargs)


def split_bf16(value):
    high = value.astype(BF16).astype(F32)
    return jnp.concatenate([high, value - high], axis=1).astype(BF16)


def half_silu(half):
    return half + half * jnp.tanh(half)


def mixer_kernel(
    tm_count,
    batch_count,
    sig_hbm,
    gate_hbm,
    bcf_hbm,
    bcb_hbm,
    step_hbm,
    rate_hbm,
    cw_hbm,
    cb_hbm,
    skip_hbm,
    gain_hbm,
    out_ref,
    sig_ref,
    gate_ref,
    bcf_ref,
    bcb_ref,
    step_ref,
    rate_ref,
    cw_ref,
    cb_ref,
    skip_ref,
    gain_ref,
    hl_sig,
    hr_sig,
    hl_bc,
    hr_bc,
    tot_buf,
    ext,
    ext_bc,
    xs,
    rt,
    roll_a,
    we,
    extra,
    dec_f,
    dec_b,
    sgate,
    acc,
    spread_ref,
    keep,
    snd,
    pin,
    csnd,
    crecv,
    esnd,
    ein,
    eown,
    yloc,
    outs,
    mid,
    landing,
    inv_snd,
    inv_buf,
    halo_ssem,
    halo_rsem,
    right_ssem,
    right_rsem,
    left_ssem,
    left_rsem,
    tot_ssem,
    tot_rsem,
    pin_ssem,
    pin_rsem,
    chip_ssem,
    chip_rsem,
    ein_ssem,
    ein_rsem,
    out_ssem,
    out_rsem,
    fwd_ssem,
    fwd_rsem,
    inv_ssem,
    inv_rsem,
    load_sem,
):
    T = tm_count
    M = T // 2
    CW = INNER // T
    HG = CW // HEADDIM
    N = INNER // GROUP
    lap = T // SPAN
    per = T // batch_count
    me = lax.axis_index("tm")
    rec = lax.axis_index("batch")
    core = lax.rem(me, 2)
    chip = me // 2
    forward = core == 1
    partner = me + 1 - 2 * core
    dest = me // per
    place = jnp.where(forward, chip, M - 1 - chip)

    def at(tm, batch=None):
        return {"tm": tm, "batch": rec if batch is None else batch}

    small = [(step_hbm, step_ref), (rate_hbm, rate_ref), (bcf_hbm, bcf_ref), (bcb_hbm, bcb_ref),
             (skip_hbm, skip_ref), (cb_hbm, cb_ref), (cw_hbm, cw_ref), (sig_hbm, sig_ref)]
    late = [(gate_hbm, gate_ref), (gain_hbm, gain_ref)]
    loads = [
        pltpu.make_async_copy(src, dst, load_sem.at[k]) for k, (src, dst) in enumerate(small + late)
    ]
    for load in loads:
        load.start()

    barrier = pltpu.get_barrier_semaphore()

    def greet(tm, batch):
        pl.semaphore_signal(
            barrier, inc=1, device_id={"tm": tm, "batch": batch},
            device_id_type=pl.DeviceIdType.MESH,
        )

    own_dest = dest == rec
    for j in range(T):

        @pl.when(j != me)
        def _():
            greet(j, rec)

        @pl.when(jnp.logical_or(j != me, jnp.logical_not(own_dest)))
        def _():
            greet(j, dest)

    for b in range(batch_count):
        for q in range(per):

            @pl.when(jnp.logical_or(b != rec, rec * per + q != me))
            def _():
                greet(rec * per + q, b)

    for b in range(batch_count):

        @pl.when(b != rec)
        def _():
            greet(me, b)


    def remote(src, dst, ssem, rsem, device):
        return pltpu.make_async_remote_copy(
            src_ref=src, dst_ref=dst, send_sem=ssem, recv_sem=rsem,
            device_id=device, device_id_type=pl.DeviceIdType.MESH,
        )

    spot = lax.broadcasted_iota(jnp.int32, (2 * HEADS, GROUP), 1)
    offset = (lax.broadcasted_iota(jnp.int32, (2 * HEADS, GROUP), 0) & (HEADS - 1)) - (
        (spot >> 7) * HG + ((spot >> 6) & 1)
    )

    def head_of(g):
        return lax.rem(g, lap) * SPAN * HG + 2 * (g // lap)

    def lay_out(g, _):
        spread_ref[g] = jnp.where(offset == head_of(g), 1.0, 0.0).astype(BF16)
        return 0

    lax.fori_loop(0, N, lay_out, 0)

    def wide(k):
        return pl.ds(pl.multiple_of(k * SPAN * CW, SPAN * CW), SPAN * CW)

    bc_right = remote(
        bcf_hbm.at[pl.ds(ROWS - RIM, RIM)], hl_bc, halo_ssem.at[0], halo_rsem.at[0], at(me + 1)
    )
    bc_left = remote(bcb_hbm.at[pl.ds(0, RIM)], hr_bc, halo_ssem.at[1], halo_rsem.at[1], at(me - 1))

    def sig_right(g):
        return remote(
            sig_hbm.at[pl.ds(ROWS - RIM, RIM), wide(g)], hl_sig.at[:, wide(g)],
            right_ssem.at[g], right_rsem.at[g], at(me + 1),
        )

    def sig_left(g):
        return remote(
            sig_hbm.at[pl.ds(0, RIM), wide(g)], hr_sig.at[:, wide(g)],
            left_ssem.at[g], left_rsem.at[g], at(me - 1),
        )

    pl.semaphore_wait(barrier, (T - 1) + 2 * (T - jnp.where(own_dest, 1, 0)) + batch_count - 1)

    @pl.when(me < T - 1)
    def _():
        bc_right.start()
        sig_right(0).start()

    @pl.when(me > 0)
    def _():
        bc_left.start()
        sig_left(0).start()

    for g in range(1, lap):

        @pl.when(me < T - 1)
        def _():
            sig_right(g).start()

        @pl.when(me > 0)
        def _():
            sig_left(g).start()

    for load in loads[: len(small)]:
        load.wait()
    raw = step_ref[...].astype(F32)
    step = jnp.maximum(raw, 0.0) + jnp.log1p(jnp.exp(-jnp.abs(raw)))
    rate = jnp.concatenate([rate_ref[0:1, :], rate_ref[1:2, :]], axis=1)
    log_decay = -step * rate
    row = lax.broadcasted_iota(jnp.int32, (ROWS, ROWS), 0)
    col = lax.broadcasted_iota(jnp.int32, (ROWS, ROWS), 1)
    lower = row >= col
    upper = row <= col
    fwd_lane = col < HEADS
    high = lax.Precision.HIGHEST
    cum = jnp.where(
        fwd_lane,
        dot(lower.astype(F32), log_decay, precision=high),
        dot(upper.astype(F32), log_decay, precision=high),
    )
    total = jnp.where(fwd_lane[0:1], cum[ROWS - 1 : ROWS], cum[0:1])
    tot_buf[me] = jnp.broadcast_to(total, (8, ROWS))

    def tot_copy(j):
        return remote(tot_buf.at[me], tot_buf.at[me], tot_ssem.at[j], tot_rsem.at[me], at(j))

    at_end, entered = jnp.exp(total - cum) * step, jnp.exp(cum)
    we[0:ROWS] = split_bf16(at_end[:, :HEADS])
    we[ROWS : 2 * ROWS] = split_bf16(entered[:, :HEADS])
    we[2 * ROWS : 3 * ROWS] = split_bf16(at_end[:, HEADS:])
    we[3 * ROWS : 4 * ROWS] = split_bf16(entered[:, HEADS:])
    rt[...] = (jnp.log(step) - cum).T
    roll_a[...] = cum
    acc[...] = jnp.zeros_like(acc)

    def own_heads(value):
        return jnp.where(forward, value[:, :HEADS], value[:, HEADS:])

    for j in range(T):

        @pl.when(j != me)
        def _():
            tot_copy(j).start()

    def place_of(g, piece):
        start = (lax.rem(g, lap) * SPAN + piece) * CW + (g // lap) * PIECE
        return (
            pl.ds(pl.multiple_of(start, PIECE), PIECE),
            pl.ds(pl.multiple_of(g * GROUP + piece * PIECE, PIECE), PIECE),
        )

    for load in loads[len(small) :]:
        load.wait()

    def gate_of(g, _):
        for piece in range(SPAN):
            cols, inside = place_of(g, piece)
            sgate[:, inside] = half_silu(0.5 * gate_ref[:, cols].astype(F32))
        return 0

    lax.fori_loop(0, N, gate_of, 0)

    @pl.when(me == 0)
    def _():
        hl_sig[...] = jnp.zeros_like(hl_sig)
        hl_bc[...] = jnp.zeros_like(hl_bc)

    @pl.when(me == T - 1)
    def _():
        hr_sig[...] = jnp.zeros_like(hr_sig)
        hr_bc[...] = jnp.zeros_like(hr_bc)

    @pl.when(me > 0)
    def _():
        bc_right.wait_recv()

    @pl.when(me < T - 1)
    def _():
        bc_left.wait_recv()

    def conv(buf, direction, cols):
        half = 0.5 * cb_ref[direction : direction + 1, cols]
        for k in range(4):
            start = 5 + k if direction == 0 else 11 - k
            tap = 0.5 * cw_ref[direction, k : k + 1, cols]
            half = half + tap * buf[start : start + ROWS, :]
        return half_silu(half).astype(BF16)

    bc_cols = slice(INNER, INNER + 2 * STATE)
    ext_bc[0:8] = hl_bc[...].astype(F32)[8:16]
    ext_bc[8 : 8 + ROWS] = bcf_ref[...].astype(F32)
    bc_f = conv(ext_bc, 0, bc_cols)
    ext_bc[8 : 8 + ROWS] = bcb_ref[...].astype(F32)
    ext_bc[8 + ROWS : 16 + ROWS] = hr_bc[...].astype(F32)[0:8]
    bc_b = conv(ext_bc, 1, bc_cols)
    bt_f = bc_f.astype(F32).T[:STATE].astype(BF16)
    bt_b = bc_b.astype(F32).T[:STATE].astype(BF16)
    c_f = bc_f[:, STATE:]
    c_b = bc_b[:, STATE:]
    scores_f = dot(c_f, bt_f)
    scores_b = dot(c_b, bt_b)
    bias_f = jnp.where(lower, 0.0, MASKED)
    bias_b = jnp.where(upper, 0.0, MASKED)

    for j in range(T):

        @pl.when(j != me)
        def _():
            remote(tot_buf.at[j], tot_buf.at[j], tot_ssem.at[j], tot_rsem.at[j], at(partner)).wait_recv()

    rows = [total, tot_buf[partner][0:1]]
    chips = [tot_buf[2 * q][0:1] + tot_buf[2 * q + 1][0:1] for q in range(M)]
    for source in range(M - 1):
        sum_f = jnp.zeros((1, 2 * HEADS), F32)
        sum_b = jnp.zeros((1, 2 * HEADS), F32)
        for q in range(source + 1, M):
            sum_f = sum_f + jnp.where(q < place, chips[q], 0.0)
            sum_b = sum_b + jnp.where(q < place, chips[M - 1 - q], 0.0)
        rows.append(jnp.where(forward, sum_f, sum_b))
    rows = jnp.exp(own_heads(jnp.concatenate(rows, axis=0)))
    rows = jnp.concatenate([skip_ref[...], rows], axis=0)
    padding = jnp.zeros((we.shape[0] - 4 * ROWS - rows.shape[0], HEADS), F32)
    we[4 * ROWS :] = split_bf16(jnp.concatenate([rows, padding], axis=0))

    def pin_copy(g):
        return remote(snd.at[g], pin.at[g], pin_ssem.at[g], pin_rsem.at[g], at(partner))

    def chip_copy(g, target):
        tm = jnp.where(forward, 2 * target + 1, 2 * (M - 1 - target))
        return remote(
            csnd.at[g], crecv.at[place, g], chip_ssem.at[target, g], chip_rsem.at[place, g], at(tm)
        )

    def recv_chip(g, source):
        return remote(
            csnd.at[g], crecv.at[source, g], chip_ssem.at[source, g], chip_rsem.at[source, g], at(partner)
        )

    def cols_of(g):
        return pl.ds(pl.multiple_of(g * GROUP, GROUP), GROUP)

    def first(g):
        @pl.when(jnp.logical_and(me > 0, g < lap))
        def _():
            sig_right(g).wait_recv()

        @pl.when(jnp.logical_and(me < T - 1, g < lap))
        def _():
            sig_left(g).wait_recv()

        for piece in range(SPAN):
            cols, inside = place_of(g, piece)
            buf = ext.at[piece]
            buf[0:8] = hl_sig[:, cols].astype(F32)[8:16]
            buf[8 : 8 + ROWS] = sig_ref[:, cols].astype(F32)
            buf[8 + ROWS : 16 + ROWS] = hr_sig[:, cols].astype(F32)[0:8]
            xs[0:ROWS, inside] = conv(buf, 0, cols)
            xs[ROWS : 2 * ROWS, inside] = conv(buf, 1, cols)
        cols = cols_of(g)
        by = dot(we[...], spread_ref[g])
        x_f, x_b = xs[0:ROWS, cols].astype(F32), xs[ROWS : 2 * ROWS, cols].astype(F32)
        state_f = dot(bt_f, (x_f * by[0:ROWS]).astype(BF16))
        state_b = dot(bt_b, (x_b * by[2 * ROWS : 3 * ROWS]).astype(BF16))
        snd[g] = jnp.where(forward, state_b, state_f).astype(BF16)
        pin_copy(g).start()
        keep[g] = jnp.where(forward, state_f, state_b)
        dec_f[:, cols] = by[ROWS : 2 * ROWS]
        dec_b[:, cols] = by[3 * ROWS : 4 * ROWS]
        extra[g] = by[4 * ROWS :]

    def combine(g):
        pin_copy(g).wait_recv()
        csnd[g] = (pin[g].astype(F32) * extra[g, 2:3] + keep[g]).astype(BF16)
        for target in range(1, M):

            @pl.when(place < target)
            def _():
                chip_copy(g, target).start()

    lane = lax.broadcasted_iota(jnp.int32, (ROWS, 2 * HEADDIM), 1)

    def local(g):
        rolled = pltpu.roll(roll_a[...], lax.rem(2 * HEADS - head_of(g), 2 * HEADS), 1)
        skips = extra[g, 0:2]

        def mixing(h):
            a_f = rolled[:, h : h + 1]
            a_b = rolled[:, HEADS + h : HEADS + h + 1]
            r_f = rt[pl.ds(head_of(g) + h, 1), :]
            r_b = rt[pl.ds(HEADS + head_of(g) + h, 1), :]
            mix_f = (scores_f * jnp.exp((a_f + r_f) + bias_f)).astype(BF16)
            mix_b = (scores_b * jnp.exp((a_b + r_b) + bias_b)).astype(BF16)
            return jnp.concatenate([mix_f, mix_b], axis=1)

        for piece in range(SPAN):
            _, inside = place_of(g, piece)
            x_pair = xs[:, inside]
            head = piece * HG
            stacked = jnp.concatenate([mixing(head), mixing(head + 1)], axis=0)
            both = dot(stacked, x_pair)
            out = jnp.where(lane < HEADDIM, both[:ROWS], both[ROWS:])
            part = slice(piece * PIECE, (piece + 1) * PIECE)
            out = out + skips[0:1, part] * x_pair[:ROWS].astype(F32)
            out = out + skips[1:2, part] * x_pair[ROWS:].astype(F32)
            yloc[:, inside] = out

    def ein_copy(g):
        return remote(esnd.at[g], ein.at[g], ein_ssem.at[g], ein_rsem.at[g], at(partner))

    def enter(g):
        factors = extra[g, 3 : 3 + M]
        entering = keep.at[g]
        entering[...] = jnp.zeros((STATE, GROUP), F32)
        for source in range(M - 1):

            @pl.when(source < place)
            def _():
                recv_chip(g, source).wait_recv()
                entering[...] += factors[source + 1 : source + 2] * crecv[source, g].astype(F32)

        value = entering[...]
        esnd[g] = value.astype(BF16)
        ein_copy(g).start()
        eown[g] = (value * factors[0:1] + pin[g].astype(F32)).astype(BF16)

    slot = lax.rem(me, per)

    def out_copy(step, j):
        return remote(
            outs.at[step * T + j], mid.at[step * T + me],
            out_ssem.at[step * T + j], out_rsem.at[step * T + me], at(j),
        )

    def forward_copy(step, i):
        n = step * T + rec * per + lax.rem(i, per)
        return remote(
            mid.at[step * T + i], landing.at[n], fwd_ssem.at[step * T + i], fwd_rsem.at[n],
            at(me, i // per),
        )

    def pass_on(g):
        for piece in range(SPAN):
            step, i = g // lap, lax.rem(g, lap) * SPAN + piece
            n = step * T + i

            @pl.when(i != me)
            def _():
                remote(outs.at[n], mid.at[n], out_ssem.at[n], out_rsem.at[n], at(partner)).wait_recv()

            @pl.when(i // per == rec)
            def _():
                landing[n] = mid[n]

            @pl.when(i // per != rec)
            def _():
                forward_copy(step, i).start()

    def last(g):
        cols = cols_of(g)
        ein_copy(g).wait_recv()
        own, other = eown[g], ein[g]
        enter_f = jnp.where(forward, own, other)
        enter_b = jnp.where(forward, other, own)
        y = yloc[:, cols] + dec_f[:, cols] * dot(c_f, enter_f) + dec_b[:, cols] * dot(c_b, enter_b)
        gated = y * sgate[:, cols]
        squares = acc[...]
        for piece in range(SPAN):
            step, j = g // lap, lax.rem(g, lap) * SPAN + piece
            part = gated[:, piece * PIECE : (piece + 1) * PIECE]
            squares = squares + part * part
            outs[step * T + j] = part.astype(BF16)

            @pl.when(j == me)
            def _():
                mid[step * T + j] = outs[step * T + j]

            @pl.when(j != me)
            def _():
                out_copy(step, j).start()

        acc[...] = squares

    def turn(t, _):
        for stage, lag in (
            (first, 0), (combine, LAG_COMBINE), (local, LAG_LOCAL), (enter, LAG_ENTER),
            (last, LAG_LAST), (pass_on, LAG_PASS),
        ):

            @pl.when(jnp.logical_and(t >= lag, t < N + lag))
            def _():
                stage(t - lag)

        return 0

    lax.fori_loop(0, N + LAG_LAST, turn, 0)
    mean = jnp.sum(acc[...].T, axis=0, keepdims=True) * (1.0 / INNER)
    inv_snd[...] = jnp.broadcast_to(lax.rsqrt(mean + EPSILON), (8, ROWS))

    def inv_copy(j):
        return remote(
            inv_snd, inv_buf.at[rec * per + slot], inv_ssem.at[j], inv_rsem.at[rec * per + slot],
            at(j, dest),
        )

    for j in range(T):
        mine = jnp.logical_and(own_dest, j == me)

        @pl.when(mine)
        def _():
            inv_buf[rec * per + slot] = inv_snd[...]

        @pl.when(jnp.logical_not(mine))
        def _():
            inv_copy(j).start()

    def rest(t, _):
        pass_on(t)
        return 0

    lax.fori_loop(N + LAG_LAST - LAG_PASS, N, rest, 0)

    gain = gain_ref[:, pl.ds(pl.multiple_of(me * CW, CW), CW)]

    for b in range(batch_count):
        for q in range(per):
            n = b * per + q
            mine = jnp.logical_and(b == rec, rec * per + q == me)

            @pl.when(jnp.logical_not(mine))
            def _():
                remote(inv_snd, inv_buf.at[n], inv_ssem.at[0], inv_rsem.at[n], at(partner)).wait_recv()

            scale = jnp.broadcast_to(inv_buf[n][0:1], (ROWS, ROWS)).T
            for step in range(CW // PIECE):
                k = step * T + n

                @pl.when(b != rec)
                def _():
                    remote(
                        mid.at[0], landing.at[k], fwd_ssem.at[0], fwd_rsem.at[k], at(partner)
                    ).wait_recv()

                inside = slice(step * PIECE, (step + 1) * PIECE)
                piece = landing[k].astype(F32) * scale * gain[:, inside]
                out_ref[b, q * ROWS : (q + 1) * ROWS, inside] = piece.astype(BF16)

    @pl.when(me < T - 1)
    def _():
        bc_right.wait_send()
        for g in range(lap):
            sig_right(g).wait_send()

    @pl.when(me > 0)
    def _():
        bc_left.wait_send()
        for g in range(lap):
            sig_left(g).wait_send()

    for j in range(T):

        @pl.when(j != me)
        def _():
            tot_copy(j).wait_send()

        @pl.when(jnp.logical_not(jnp.logical_and(own_dest, j == me)))
        def _():
            inv_copy(j).wait_send()

        for step in range(CW // PIECE):

            @pl.when(j != me)
            def _():
                out_copy(step, j).wait_send()

            @pl.when(j // per != rec)
            def _():
                forward_copy(step, j).wait_send()

    def sent(g, _):
        pin_copy(g).wait_send()
        ein_copy(g).wait_send()
        for target in range(1, M):

            @pl.when(place < target)
            def _():
                chip_copy(g, target).wait_send()

        return 0

    lax.fori_loop(0, N, sent, 0)


def shards(tm_count, batch_count, signal, gate_input, bc_forward, bc_backward, step_raw,
           decay_rate, conv_weight, conv_bias, skip_gain, norm_gain):
    T, M = tm_count, tm_count // 2
    CW = INNER // T
    per = T // batch_count
    N, lap, pieces = INNER // GROUP, T // SPAN, INNER // PIECE
    few = -(-(M + 3) // 16) * 16
    vmem = pltpu.VMEM
    dma = pltpu.SemaphoreType.DMA
    args = (signal[0], gate_input[0], bc_forward[0], bc_backward[0], step_raw[0],
            decay_rate, conv_weight, conv_bias, skip_gain, norm_gain.reshape(1, INNER))
    scratch = [vmem(a.shape, a.dtype) for a in args] + [
        vmem((RIM, INNER), BF16),
        vmem((RIM, INNER), BF16),
        vmem((RIM, 2 * STATE), BF16),
        vmem((RIM, 2 * STATE), BF16),
        vmem((T, 8, ROWS), F32),
        vmem((SPAN, ROWS + 16, PIECE), F32),
        vmem((ROWS + 16, 2 * STATE), F32),
        vmem((2 * ROWS, INNER), BF16),
        vmem((2 * HEADS, ROWS), F32),
        vmem((ROWS, 2 * HEADS), F32),
        vmem((4 * ROWS + few, 2 * HEADS), BF16),
        vmem((N, few, GROUP), F32),
        vmem((ROWS, INNER), F32),
        vmem((ROWS, INNER), F32),
        vmem((ROWS, INNER), F32),
        vmem((ROWS, PIECE), F32),
        vmem((N, 2 * HEADS, GROUP), BF16),
        vmem((N, STATE, GROUP), F32),
        vmem((N, STATE, GROUP), BF16),
        vmem((N, STATE, GROUP), BF16),
        vmem((N, STATE, GROUP), BF16),
        vmem((M, N, STATE, GROUP), BF16),
        vmem((N, STATE, GROUP), BF16),
        vmem((N, STATE, GROUP), BF16),
        vmem((N, STATE, GROUP), BF16),
        vmem((ROWS, INNER), F32),
        vmem((pieces, ROWS, PIECE), BF16),
        vmem((pieces, ROWS, PIECE), BF16),
        vmem((pieces, ROWS, PIECE), BF16),
        vmem((8, ROWS), F32),
        vmem((T, 8, ROWS), F32),
        dma((2,)),
        dma((2,)),
        dma((lap,)),
        dma((lap,)),
        dma((lap,)),
        dma((lap,)),
        dma((T,)),
        dma((T,)),
        dma((N,)),
        dma((N,)),
        dma((M, N)),
        dma((M, N)),
        dma((N,)),
        dma((N,)),
        dma((pieces,)),
        dma((pieces,)),
        dma((pieces,)),
        dma((pieces,)),
        dma((T,)),
        dma((T,)),
        dma((len(args),)),
    ]
    return pl.pallas_call(
        functools.partial(mixer_kernel, T, batch_count),
        out_shape=pltpu.VMEM((batch_count, per * ROWS, CW), BF16),
        in_specs=[pl.BlockSpec(memory_space=pltpu.HBM)] * len(args),
        out_specs=pl.BlockSpec(memory_space=pltpu.VMEM),
        scratch_shapes=scratch,
        compiler_params=pltpu.CompilerParams(
            collective_id=0, has_side_effects=True, vmem_limit_bytes=62 * 2**20
        ),
        cost_estimate=pl.CostEstimate(
            flops=10**9, bytes_accessed=8 * 2**20, transcendentals=4 * 10**6
        ),
    )(*args)


def solution(mesh):
    in_specs = (P("batch", "tm", None),) * 5 + (P(),) * 5
    return jax.shard_map(
        functools.partial(shards, mesh.shape["tm"], mesh.shape["batch"]),
        mesh=mesh, in_specs=in_specs, out_specs=P(None, "batch", "tm"), check_vma=False,
    )
```
